256 devices in a mesh: orb: 32 (over y, z), slab: 8 (over x, core).
Axes of the slice: x: 4, y: 4, z: 8, core: 2. Of those that a mesh axis runs over, the one named last changes fastest.
Arguments:
- orbitals: bfloat16 [256, 64, 4096], P('orb', 'slab'), may hold values from -6 to 6
- pair_first: int32 [512], P('orb'), may hold values from 0 to 7
- second_owner: int32 [512, 1], replicated, may hold values from 0 to 31; in each aligned block of 16 rows (0 to 15, 16 to 31, ...) at most 2 rows name the same one
- second_local: int32 [512], replicated, may hold values from 0 to 7
- pair_shift: int32 [512, 2], P('orb'), may hold values from -32 to 32
- pair_count: int32 [32], replicated, may hold values from 1 to 16, 256 in all
Outputs:
- exchange_applied: bfloat16 [256, 64, 4096], P('orb', 'slab')
The draws below stay inside these ranges and needn't reach their ends.
Inputs may be any that keep to these rules, and one draw needn't show every extreme that they name: `second_owner`: in each aligned block of 16 pair slots (those of one orb index) no owner is named by more than 2 slots; some owner is named by exactly 2. `pair_count`: the counts sum to 16 * 32 // 2 and the largest equals 16.
All inputs are finite; a program needn't handle non-finite values.
Results may differ from the reference program's by a relative error of at most 0.0033.
Values may be sent and summed in bfloat16 or wider, within the bound.
No kernel may reach another device: no remote copies, remote signals or barrier semaphores. Data moves between devices by JAX's collectives and lax.ppermute only.
A program may use at most 128 MiB of HBM per device.

```python
import math
import jax
import jax.numpy as jnp
import numpy as np
from jax import lax

BOX = 64
ORB_DEV = 8
PAIR_DEV = 16
CAP = 2
ORBITALS = 256
PAIRS = 512
N_ORB = 32


def set_ends(values, stream_key, low, top_value):
    longest = values.shape.index(max(values.shape))
    spots = []
    for shift in (0, 1):
        where = [jax.random.randint(jax.random.fold_in(stream_key, axis), (), 0, length) for axis, length in enumerate(values.shape)]
        where[longest] = (where[longest] + shift) % values.shape[longest]
        spots.append(tuple(where))
    return values.at[spots[0]].set(low).at[spots[1]].set(top_value)


def shard_levels(key, shape, split, smallest, high):
    loudness, own = 1.0, jax.random.fold_in(key, 6)
    for axis_at, blocks in split:
        heights = jnp.exp(jax.random.uniform(jax.random.fold_in(own, axis_at), (blocks,), jnp.float32, smallest / len(split), high / len(split)))
        loudness = loudness * jnp.repeat(heights, shape[axis_at] // blocks).reshape([-1 if axis == axis_at else 1 for axis in range(len(shape))])
    return loudness


def profile(amount, total, bound, skew):
    loads = [(1 << 20) // math.isqrt(standing ** skew) + 1 for standing in range(2, amount + 1)]
    rest, holding = total - bound - (amount - 1), [1] * (amount - 1)
    while rest > 0:
        free = [i for i in range(amount - 1) if holding[i] < bound]
        pool, left = sum([loads[i] for i in free]), rest
        for i in free:
            extra = min(bound - holding[i], max(1, left * loads[i] // pool), rest)
            holding[i] = holding[i] + extra
            rest = rest - extra
    return np.array([bound] + holding)


def ragged(key, count, total, most, skew):
    if count == 2:
        one = jax.random.randint(key, (), max(1, total - most), min(most, total - 1) + 1)
        return jnp.stack([one, total - one])
    tallies = jnp.asarray(profile(count, total, most, skew), jnp.int32)
    pairs = (count - 1) // 2
    source_of, taker = tallies[1:1 + 2 * pairs:2], tallies[2:2 + 2 * pairs:2]
    margin = jnp.minimum(source_of - 1, most - taker)
    shifted = jax.random.randint(jax.random.fold_in(key, 1), (pairs,), 0, 1 << 20) % (margin + 1)
    tallies = tallies.at[1:1 + 2 * pairs:2].set(source_of - shifted).at[2:2 + 2 * pairs:2].set(taker + shifted)
    return tallies[jax.random.permutation(jax.random.fold_in(key, 2), count)]


def assign_block(stream_key, own, number, rows, number_of, top, limit, lean):
    ranking = jax.random.permutation(stream_key, number_of)
    crowded, usual = load_shares(number_of, rows * top, limit, lean, True), load_shares(number_of, rows * top, limit, lean, False)
    places = jnp.arange(number_of)

    def named(sizes, offset_by):
        used = int((sizes > 0).sum())
        fixed = max(1, used // 4)
        shifted = fixed + (places - fixed + offset_by * (used - fixed)) % max(1, number_of - fixed)
        return jnp.zeros((number_of,), jnp.int32).at[ranking[jnp.where(places < fixed, places, shifted)]].set(jnp.asarray(sizes, jnp.int32))

    sizes = jnp.where(number % 4 == 0, named(crowded, number // 4), named(usual, number - number // 4 - 1))
    mixed = jax.random.permutation(jax.random.fold_in(own, 3), number_of)
    giver, receiver = mixed[0:number_of // 2 * 2:2], mixed[1:number_of // 2 * 2:2]
    room = jnp.minimum(sizes[giver] - 1, limit - sizes[receiver]) // 2
    room = jnp.where((giver == ranking[0]) | (receiver == ranking[0]) | (sizes[receiver] == 0), 0, jnp.maximum(room, 0))
    shifted = jax.random.randint(jax.random.fold_in(own, 4), (number_of // 2,), 0, 1 << 20) % (room + 1)
    sizes = sizes.at[giver].add(-shifted).at[receiver].add(shifted)
    labels = jnp.searchsorted(jnp.cumsum(sizes), jnp.arange(rows * top), side="right").astype(jnp.int32)
    listing = labels.reshape(top, rows).T
    listing = listing[jax.random.permutation(jax.random.fold_in(own, 1), rows)]
    offset_by = jax.random.randint(jax.random.fold_in(own, 2), (rows, 1), 0, top)
    return jnp.take_along_axis(listing, (jnp.arange(top)[None, :] + offset_by) % top, axis=1)


def load_shares(amount, total, limit, skew, full):
    portions = [(1 << 20) // math.isqrt(standing ** skew) + 1 for standing in range(1, amount + 1)]
    largest = limit if full else min(limit, max(-(-total // amount), total * portions[0] // sum(portions)))
    least = 1 if total - largest >= amount - 1 else 0
    holding, surplus = [largest] + [least] * (amount - 1), total - largest - least * (amount - 1)
    while surplus > 0:
        movable = [i for i in range(1, amount) if holding[i] < largest] or [i for i in range(1, amount) if holding[i] < limit]
        mass, budget = sum([portions[i] for i in movable]), surplus
        for i in movable:
            extra = min(limit - holding[i], max(1, budget * portions[i] // mass), surplus)
            holding[i] = holding[i] + extra
            surplus = surplus - extra
    return np.array(holding)


def gaussian(key, extent, spread, most, pieces=(), kind=jnp.bfloat16):
    drawn = spread * jax.random.normal(key, extent, jnp.float32)
    if pieces:
        drawn = drawn * shard_levels(key, extent, pieces, -0.22, 0.18)
    return jnp.clip(drawn, -most, most).astype(kind)


def setup_inputs(seed: int = 0) -> dict:
    key_of = jax.random.split(jax.random.key(seed), 7)
    orbitals = gaussian(key_of[0], (ORBITALS, BOX, BOX * BOX), 1.0, 6.0, ((0, 32), (1, 8)))
    pair_first = set_ends(jax.random.randint(key_of[1], (PAIRS,), 0, ORB_DEV), jax.random.fold_in(key_of[1], 1), 0, ORB_DEV - 1).astype(jnp.int32)
    second_owner_keys = jax.random.split(jax.random.fold_in(key_of[2], 1), PAIRS // PAIR_DEV)
    second_owner_turns = jax.random.permutation(jax.random.fold_in(key_of[2], 3), PAIRS // PAIR_DEV)
    second_owner = jax.vmap(lambda own, number: assign_block(jax.random.fold_in(key_of[2], 2), own, number, PAIR_DEV, N_ORB, 1, CAP, 2))(second_owner_keys, second_owner_turns).reshape((PAIRS, 1))
    second_local = set_ends(jax.random.randint(key_of[3], (PAIRS,), 0, ORB_DEV), jax.random.fold_in(key_of[3], 1), 0, ORB_DEV - 1).astype(jnp.int32)
    pair_shift = set_ends(jax.random.randint(key_of[4], (PAIRS, 2), 0 - BOX // 2, BOX // 2 + 1), jax.random.fold_in(key_of[4], 1), 0 - BOX // 2, (BOX // 2 + 1) - 1).astype(jnp.int32)
    pair_count = ragged(key_of[5], N_ORB, PAIR_DEV * N_ORB // 2, PAIR_DEV, 2).astype(jnp.int32)
    return dict(orbitals=orbitals, pair_first=pair_first, second_owner=second_owner, second_local=second_local, pair_shift=pair_shift, pair_count=pair_count)


screening = 0.02


def hartley(length):
    line = jnp.arange(length, dtype=jnp.int32)
    product = (line[:, None] * line[None, :]) % length
    angle = product.astype(jnp.float32) * (2.0 * math.pi / length)
    return jnp.cos(angle) + jnp.sin(angle)


def eigen(length, line):
    angle = (line % length).astype(jnp.float32) * (2.0 * math.pi / length)
    return 2.0 - 2.0 * jnp.cos(angle)


def move_box(field, shift_x, shift_y):
    length = field.shape[-1]
    rolled = jnp.roll(field, (shift_x, shift_y), axis=(1, 2))
    line = jnp.arange(length, dtype=jnp.int32)
    keep_x = (line - shift_x >= 0) & (line - shift_x < length)
    keep_y = (line - shift_y >= 0) & (line - shift_y < length)
    mask = (keep_x[:, None] & keep_y[None, :]).astype(field.dtype)
    return rolled * mask[None]


def solve_box(density):
    length = density.shape[-1]
    table = hartley(length)
    line = jnp.arange(length, dtype=jnp.int32)
    lam = eigen(length, line)
    kernel = 1.0 / (lam[:, None, None] + lam[None, :, None] + lam[None, None, :] + screening)
    high = lax.Precision.HIGHEST
    spectrum = jnp.einsum('zxy,xa->zay', density, table, precision=high)
    spectrum = jnp.einsum('zay,yb->zab', spectrum, table, precision=high)
    spectrum = jnp.einsum('zab,zc->cab', spectrum, table, precision=high)
    spectrum = spectrum * kernel
    field = jnp.einsum('cab,cz->zab', spectrum, table, precision=high) / length
    field = jnp.einsum('zab,ax->zxb', field, table, precision=high) / length
    field = jnp.einsum('zxb,by->zxy', field, table, precision=high) / length
    return field


def reference(orbitals, pair_first, second_owner, second_local, pair_shift, pair_count):
    boxes = orbitals.reshape(ORBITALS, BOX, BOX, BOX)
    total = jnp.zeros(boxes.shape, jnp.float32)

    def visit(index, result):
        owner_first = index // PAIR_DEV
        live = ((index % PAIR_DEV) < pair_count[owner_first]).astype(jnp.float32)
        first = (owner_first * ORB_DEV + pair_first[index]).astype(jnp.int32)
        second = (second_owner[index, 0] * ORB_DEV + second_local[index]).astype(jnp.int32)
        shift_x = pair_shift[index, 0]
        shift_y = pair_shift[index, 1]
        first_box = boxes[first]
        moved = move_box(boxes[second], shift_x, shift_y)
        density = first_box.astype(jnp.float32) * moved.astype(jnp.float32)
        potential = solve_box(density)
        own_term = live * potential * moved.astype(jnp.float32)
        carried = potential * first_box.astype(jnp.float32)
        other_term = (live * move_box(carried, -shift_x, -shift_y)).astype(jnp.bfloat16)
        result = result.at[first].add(own_term)
        result = result.at[second].add(other_term.astype(jnp.float32))
        return result

    total = lax.fori_loop(0, PAIRS, visit, total)
    return total.reshape(ORBITALS, BOX, BOX * BOX).astype(jnp.bfloat16)
```

```python
import math

import jax
import jax.numpy as jnp
import numpy as np
from jax import lax
from jax.experimental import pallas as pl
from jax.experimental.pallas import tpu as pltpu
from jax.sharding import PartitionSpec as P

BOX = 64
ORB_DEV = 8
PAIR_DEV = 16
N_ORB = 32
N_DEV = 256
TILES = 32
LANES = 128
SCREENING = 0.02
PARAMS = pltpu.CompilerParams(vmem_limit_bytes=48 * 1024 * 1024)
WHOLE_V = pl.BlockSpec(memory_space=pltpu.VMEM)
WHOLE_S = pl.BlockSpec(memory_space=pltpu.SMEM)


def hartley_table():
    line = np.arange(BOX)
    angle = (line[:, None] * line[None, :] % BOX) * (2.0 * math.pi / BOX)
    return np.cos(angle) + np.sin(angle)


def halves(table):
    high = table.astype(np.float32).astype(jnp.bfloat16)
    low = (table - high.astype(np.float64)).astype(np.float32).astype(jnp.bfloat16)
    return high, low


def tables():
    high, low = halves(hartley_table())
    zero = np.zeros((BOX, BOX), high.dtype)

    def twice(table):
        return np.block([[table, zero], [zero, table]])

    right = np.block([[twice(high), twice(low)], [twice(high), np.zeros((128, 128), high.dtype)]])
    left = np.concatenate([high, high, low], axis=1)
    lam = 2.0 - 2.0 * np.cos(np.arange(BOX) * (2.0 * math.pi / BOX))
    base = lam[:, None] + np.tile(lam, 2)[None, :] + SCREENING
    lam_a = np.repeat(lam.reshape(2, TILES).T, BOX, axis=1)
    return right, left, base.astype(np.float32), lam_a.astype(np.float32)


def split(field):
    high = field.astype(jnp.bfloat16)
    low = (field - high.astype(jnp.float32)).astype(jnp.bfloat16)
    return high, low


def fast_hartley(parts):
    n = len(parts)
    if n == 1:
        return parts
    if n == 2:
        return [parts[0] + parts[1], parts[0] - parts[1]]
    even, odd = fast_hartley(parts[0::2]), fast_hartley(parts[1::2])
    m = n // 2
    out = [None] * n
    for k in range(m):
        if k == 0 or 4 * k == n:
            turned = odd[k]
        else:
            angle = 2.0 * math.pi * k / n
            turned = odd[k] * math.cos(angle) + odd[m - k] * math.sin(angle)
        out[k] = even[k] + turned
        out[k + m] = even[k] - turned
    return out


def twist(parts, first):
    out = []
    for k in range(TILES):
        mirror = parts[(TILES - k) % TILES]
        angle = 2.0 * math.pi * k / BOX
        if k == 0 or 2 * k == TILES:
            out.append(parts[k])
        else:
            out.append(jnp.where(first, parts[k], parts[k] * math.cos(angle) + mirror * math.sin(angle)))
    return out


def untwist(parts, first):
    out = []
    for k in range(TILES):
        mirror = parts[(TILES - k) % TILES]
        angle = 2.0 * math.pi * k / BOX
        back = 2.0 * math.pi * ((TILES - k) % TILES) / BOX
        if k == 0 or 2 * k == TILES:
            out.append(parts[k])
        else:
            out.append(jnp.where(first, parts[k], parts[k] * math.cos(angle) + mirror * math.sin(back)))
    return out


def spread_kernel(orbitals, pieces):
    for pair in range(ORB_DEV // 2):
        one = orbitals[2 * pair].astype(jnp.float32)
        two = orbitals[2 * pair + 1].astype(jnp.float32)
        for tile in range(TILES):
            at = slice(tile * LANES, (tile + 1) * LANES)
            pieces[tile, 16 * pair : 16 * pair + 16, :] = jnp.concatenate(
                [one[:, at], two[:, at]], axis=0
            ).astype(jnp.bfloat16)


def pick_kernel(count, owner, local, about, pieces, picked, index, held):
    def widen(e, carry):
        block = pieces[e].astype(jnp.float32).reshape(ORB_DEV, 8, LANES)
        held[pl.ds(e * ORB_DEV, ORB_DEV)] = block
        return carry

    lax.fori_loop(0, N_ORB, widen, 0)

    def of_orb(e, base):
        live = count[e]

        def of_slot(k, carry):
            slot = e * PAIR_DEV + k
            first = e * ORB_DEV + about[e * 3 * PAIR_DEV + k]
            second = owner[slot] * ORB_DEV + local[slot]
            picked[base + k] = jnp.concatenate([held[first], held[second]], axis=0).astype(jnp.bfloat16)
            index[base + k] = first
            index[N_DEV + base + k] = second
            index[2 * N_DEV + base + k] = e * 3 * PAIR_DEV + PAIR_DEV + k
            return carry

        lax.fori_loop(0, live, of_slot, 0)
        return base + live

    lax.fori_loop(0, N_ORB, of_orb, 0)


def shifted(source, tile, flat, shift_x, shift_y, lane):
    whole, rest = flat // LANES, flat % LANES
    here = source[(tile - whole + 2 * TILES) % TILES]
    before = source[(tile - whole - 1 + 2 * TILES) % TILES]
    both = jnp.where(lane >= rest, pltpu.roll(here, rest, 1), pltpu.roll(before, rest, 1))
    x = 2 * tile + lane // BOX - shift_x
    y = lane % BOX - shift_y
    keep = (x >= 0) & (x < BOX) & (y >= 0) & (y < BOX)
    return jnp.where(keep, both, 0.0)


def solve_kernel(me, index, about, right, left, base, lam_a, boxes, terms, first_box, moved, field, other):
    at = index[2 * N_DEV + me[0]]
    shift_x, shift_y = about[at], about[at + PAIR_DEV]
    full = BOX * BOX
    ahead = (shift_x * BOX + shift_y + full) % full
    back = (full - ahead) % full
    lane = lax.broadcasted_iota(jnp.int32, (BOX, LANES), 1)
    lane_small = lax.broadcasted_iota(jnp.int32, (8, LANES), 1)
    early = lane_small < BOX
    sign = jnp.where(early, 1.0, -1.0)

    def unpack(tile, carry):
        block = boxes[pl.ds(tile * 8, 8)].astype(jnp.float32)
        first_box[tile] = block[:, :8].reshape(BOX, LANES)
        other[tile] = block[:, 8:].reshape(BOX, LANES)
        return carry

    lax.fori_loop(0, TILES, unpack, 0)

    def along_y(blocks):
        high, low = split(jnp.concatenate(blocks, axis=0))
        product = jnp.dot(
            jnp.concatenate([high, low], axis=1), right[...], preferred_element_type=jnp.float32
        )
        return product[:, :LANES] + product[:, LANES:]

    def forward_y(step, carry):
        blocks = []
        for k in range(4):
            tile = step * 4 + k
            box = shifted(other, tile, ahead, shift_x, shift_y, lane)
            moved[tile] = box
            blocks.append(first_box[tile] * box)
        field[pl.ds(step * 4, 4)] = along_y(blocks).reshape(4, BOX, LANES)
        return carry

    lax.fori_loop(0, TILES // 4, forward_y, 0)

    def forward_x(step, carry):
        rows = pl.ds(pl.multiple_of(step * 8, 8), 8)
        parts = twist(fast_hartley([field[k, rows, :] for k in range(TILES)]), early)
        for k in range(TILES):
            field[k, rows, :] = sign * parts[k] + pltpu.roll(parts[k], BOX, 1)
        return carry

    lax.fori_loop(0, 8, forward_x, 0)

    def along_z(block):
        high, low = split(block)
        return jnp.dot(
            left[...], jnp.concatenate([high, low, high], axis=0), preferred_element_type=jnp.float32
        )

    def screened_z(step, carry):
        block = jnp.concatenate([field[2 * step], field[2 * step + 1]], axis=1)
        under = jnp.concatenate(
            [base[...] + lam_a[pl.ds(2 * step + k, 1), :] for k in range(2)], axis=1
        )
        block = along_z(block) * ((1.0 / BOX**3) / under)
        block = along_z(block)
        field[2 * step] = block[:, :LANES]
        field[2 * step + 1] = block[:, LANES:]
        return carry

    lax.fori_loop(0, TILES // 2, screened_z, 0)

    def inverse_x(step, carry):
        rows = pl.ds(pl.multiple_of(step * 8, 8), 8)
        parts = [field[k, rows, :] for k in range(TILES)]
        parts = [sign * part + pltpu.roll(part, BOX, 1) for part in parts]
        parts = fast_hartley(untwist(parts, early))
        for k in range(TILES):
            field[k, rows, :] = parts[k]
        return carry

    lax.fori_loop(0, 8, inverse_x, 0)

    def inverse_y(step, carry):
        tiles = pl.ds(step * 4, 4)
        potential = along_y([field[step * 4 + k] for k in range(4)]).reshape(4, BOX, LANES)
        other[tiles] = potential * first_box[tiles]
        moved[tiles] = potential * moved[tiles]
        return carry

    lax.fori_loop(0, TILES // 4, inverse_y, 0)

    def pack(tile, carry):
        own = moved[tile].reshape(8, 8, LANES)
        carried = shifted(other, tile, back, -shift_x, -shift_y, lane).reshape(8, 8, LANES)
        terms[pl.ds(tile * 8, 8)] = jnp.concatenate([own, carried], axis=1).astype(jnp.bfloat16)
        return carry

    lax.fori_loop(0, TILES, pack, 0)


def sum_kernel(index, terms, pieces, own, carried):
    own[...] = jnp.zeros_like(own)
    carried[...] = jnp.zeros_like(carried)

    def of_pair(d, carry):
        both = terms[d].astype(jnp.float32)
        first, second = index[d], index[N_DEV + d]
        own[first] = own[first] + both[:8]
        carried[second] = carried[second] + both[8:]
        return carry

    lax.fori_loop(0, N_DEV, of_pair, 0)

    def narrow(e, carry):
        at = pl.ds(e * ORB_DEV, ORB_DEV)
        pieces[e] = (own[at] + carried[at]).reshape(ORB_DEV * 8, LANES).astype(jnp.bfloat16)
        return carry

    lax.fori_loop(0, N_ORB, narrow, 0)


def join_kernel(pieces, result):
    for pair in range(ORB_DEV // 2):
        tiles = [pieces[tile, 16 * pair : 16 * pair + 16, :].astype(jnp.float32) for tile in range(TILES)]
        for side in range(2):
            rows = [tile[8 * side : 8 * side + 8] for tile in tiles]
            result[2 * pair + side] = jnp.concatenate(rows, axis=1).astype(jnp.bfloat16)


def body(orbitals, pair_first, second_owner, second_local, pair_shift, pair_count):
    f32, bf16 = jnp.float32, jnp.bfloat16
    about = jnp.concatenate([pair_first, pair_shift[:, 0], pair_shift[:, 1]])
    about = lax.all_gather(about, "orb", axis=0, tiled=True)
    me = (lax.axis_index("orb") * 8 + lax.axis_index("slab")).reshape(1)
    piece_shape = jax.ShapeDtypeStruct((N_ORB, ORB_DEV * 8, LANES), bf16)
    pair_shape = jax.ShapeDtypeStruct((N_DEV, 16, LANES), bf16)
    pieces = pl.pallas_call(
        spread_kernel, out_shape=piece_shape, in_specs=[WHOLE_V], out_specs=WHOLE_V,
        compiler_params=PARAMS, name="spread",
    )(orbitals)
    pieces = lax.all_to_all(pieces, "orb", split_axis=0, concat_axis=0, tiled=True)
    picked, index = pl.pallas_call(
        pick_kernel,
        out_shape=(pair_shape, jax.ShapeDtypeStruct((3 * N_DEV,), jnp.int32)),
        in_specs=[WHOLE_S] * 4 + [WHOLE_V],
        out_specs=(WHOLE_V, WHOLE_S),
        scratch_shapes=[pltpu.VMEM((N_DEV, 8, LANES), f32)],
        compiler_params=PARAMS, name="pick",
    )(pair_count, second_owner[:, 0], second_local, about, pieces)
    boxes = lax.all_to_all(picked, ("orb", "slab"), split_axis=0, concat_axis=0, tiled=True)
    right, left, base, lam_a = (jnp.asarray(table) for table in tables())
    terms = pl.pallas_call(
        solve_kernel, out_shape=pair_shape,
        in_specs=[WHOLE_S] * 3 + [WHOLE_V] * 5,
        out_specs=WHOLE_V,
        scratch_shapes=[pltpu.VMEM((TILES, BOX, LANES), f32)] * 4,
        compiler_params=PARAMS, name="solve",
    )(me, index, about, right, left, base, lam_a, boxes)
    terms = lax.all_to_all(terms, ("orb", "slab"), split_axis=0, concat_axis=0, tiled=True)
    pieces = pl.pallas_call(
        sum_kernel, out_shape=piece_shape,
        in_specs=[WHOLE_S, WHOLE_V], out_specs=WHOLE_V,
        scratch_shapes=[pltpu.VMEM((N_DEV, 8, LANES), f32)] * 2,
        compiler_params=PARAMS, name="sum",
    )(index, terms)
    pieces = lax.all_to_all(pieces, "orb", split_axis=0, concat_axis=0, tiled=True)
    return pl.pallas_call(
        join_kernel, out_shape=jax.ShapeDtypeStruct((ORB_DEV, 8, BOX * BOX), bf16),
        in_specs=[WHOLE_V], out_specs=WHOLE_V,
        compiler_params=PARAMS, name="join",
    )(pieces)


def solution(mesh):
    in_specs = (P("orb", "slab", None), P("orb"), P(), P(), P("orb", None), P())
    out_specs = P("orb", "slab", None)
    return jax.shard_map(body, mesh=mesh, in_specs=in_specs, out_specs=out_specs, check_vma=False)
```

```python
import math

import jax
import jax.numpy as jnp
import numpy as np
from jax import lax
from jax.experimental import pallas as pl
from jax.experimental.pallas import tpu as pltpu
from jax.sharding import PartitionSpec as P

BOX = 64
ORB_DEV = 8
PAIR_DEV = 16
N_ORB = 32
N_DEV = 256
TILES = 32
LANES = 128
SCREENING = 0.02
PARAMS = pltpu.CompilerParams(vmem_limit_bytes=48 * 1024 * 1024)
WHOLE_V = pl.BlockSpec(memory_space=pltpu.VMEM)
WHOLE_S = pl.BlockSpec(memory_space=pltpu.SMEM)


def hartley_table():
    line = np.arange(BOX)
    angle = (line[:, None] * line[None, :] % BOX) * (2.0 * math.pi / BOX)
    return np.cos(angle) + np.sin(angle)


def halves(table):
    high = table.astype(np.float32).astype(jnp.bfloat16)
    low = (table - high.astype(np.float64)).astype(np.float32).astype(jnp.bfloat16)
    return high, low


def tables():
    high, low = halves(hartley_table())
    zero = np.zeros((BOX, BOX), high.dtype)

    def twice(table):
        return np.block([[table, zero], [zero, table]])

    right = np.block([[twice(high), twice(low)], [twice(high), np.zeros((128, 128), high.dtype)]])
    left = np.concatenate([high, high, low], axis=1)
    lam = 2.0 - 2.0 * np.cos(np.arange(BOX) * (2.0 * math.pi / BOX))
    lam_a = np.repeat(lam.reshape(2, TILES).T, BOX, axis=1)
    under = lam_a[:, None, :] + lam[None, :, None] + np.tile(lam, 2)[None, None, :] + SCREENING
    return right, left, (1.0 / BOX**3 / under).astype(np.float32)


def split(field):
    high = field.astype(jnp.bfloat16)
    low = (field - high.astype(jnp.float32)).astype(jnp.bfloat16)
    return high, low


def fast_hartley(parts):
    n = len(parts)
    if n == 1:
        return parts
    if n == 2:
        return [parts[0] + parts[1], parts[0] - parts[1]]
    even, odd = fast_hartley(parts[0::2]), fast_hartley(parts[1::2])
    m = n // 2
    out = [None] * n
    for k in range(m):
        if k == 0 or 4 * k == n:
            turned = odd[k]
        else:
            angle = 2.0 * math.pi * k / n
            turned = odd[k] * math.cos(angle) + odd[m - k] * math.sin(angle)
        out[k] = even[k] + turned
        out[k + m] = even[k] - turned
    return out


def twist(parts, first):
    out = []
    for k in range(TILES):
        mirror = parts[(TILES - k) % TILES]
        angle = 2.0 * math.pi * k / BOX
        if k == 0 or 2 * k == TILES:
            out.append(parts[k])
        else:
            out.append(jnp.where(first, parts[k], parts[k] * math.cos(angle) + mirror * math.sin(angle)))
    return out


def untwist(parts, first):
    out = []
    for k in range(TILES):
        mirror = parts[(TILES - k) % TILES]
        angle = 2.0 * math.pi * k / BOX
        back = 2.0 * math.pi * ((TILES - k) % TILES) / BOX
        if k == 0 or 2 * k == TILES:
            out.append(parts[k])
        else:
            out.append(jnp.where(first, parts[k], parts[k] * math.cos(angle) + mirror * math.sin(back)))
    return out


def spread_kernel(first, shift, orbitals, pieces):
    for pair in range(ORB_DEV // 2):
        one = orbitals[2 * pair].astype(jnp.float32)
        two = orbitals[2 * pair + 1].astype(jnp.float32)
        for tile in range(TILES):
            at = slice(tile * LANES, (tile + 1) * LANES)
            pieces[tile, 16 * pair : 16 * pair + 16, :] = jnp.concatenate(
                [one[:, at], two[:, at]], axis=0
            ).astype(jnp.bfloat16)
    lane = lax.broadcasted_iota(jnp.int32, (8, LANES), 1)
    about = jnp.zeros((8, LANES), jnp.int32)
    for k in range(PAIR_DEV):
        about = jnp.where(lane == k, first[k], about)
        about = jnp.where(lane == PAIR_DEV + k, shift[k, 0], about)
        about = jnp.where(lane == 2 * PAIR_DEV + k, shift[k, 1], about)
    about = about.astype(jnp.float32).astype(jnp.bfloat16)
    for tile in range(TILES):
        pieces[tile, ORB_DEV * 8 :, :] = about


def list_kernel(count, owner, local, listed):
    def of_orb(e, base):
        live = count[e]

        def of_slot(k, carry):
            slot = e * PAIR_DEV + k
            listed[base + k] = e * LANES + k
            listed[N_DEV + base + k] = owner[slot] * ORB_DEV + local[slot]
            return carry

        lax.fori_loop(0, live, of_slot, 0)
        return base + live

    lax.fori_loop(0, N_ORB, of_orb, 0)


def pick_kernel(me, listed, pieces, picked, firsts, mine, held, whole, about, done):
    whole[...] = pieces[:, ORB_DEV * 8, :].astype(jnp.float32).astype(jnp.int32)
    copy = pltpu.make_async_copy(whole, about, done)
    copy.start()
    for e in range(N_ORB):
        block = pieces[e, : ORB_DEV * 8, :].astype(jnp.float32)
        held[e * ORB_DEV : (e + 1) * ORB_DEV] = block.reshape(ORB_DEV, 8, LANES)
    copy.wait()

    def step(at, carry):
        for k in range(8):
            d = at * 8 + k
            e, lane = listed[d] // LANES, listed[d] % LANES
            first = e * ORB_DEV + about[e, lane]
            firsts[d] = first
            both = jnp.concatenate([held[first], held[listed[N_DEV + d]]], axis=0)
            picked[d] = both.astype(jnp.bfloat16)
        return carry

    lax.fori_loop(0, N_DEV // 8, step, 0)
    e, lane = listed[me[0]] // LANES, listed[me[0]] % LANES
    mine[0] = about[e, lane + PAIR_DEV]
    mine[1] = about[e, lane + 2 * PAIR_DEV]


def shifted(tiles, start, count, flat, shift_x, shift_y):
    lane = lax.broadcasted_iota(jnp.int32, (8, LANES), 1)
    whole, rest = flat // LANES, flat % LANES
    later = (lane >= rest)[None]
    y = lane % BOX - shift_y
    keep_y = (y >= 0) & (y < BOX)
    turned = [
        pltpu.roll(tiles((start + k - whole - 1 + 2 * TILES) % TILES), rest, 2) for k in range(count + 1)
    ]
    out = []
    for k in range(count):
        x = 2 * (start + k) + lane // BOX - shift_x
        keep = jnp.where(keep_y & (x >= 0) & (x < BOX), 1.0, 0.0)
        out.append(jnp.where(later, turned[k + 1], turned[k]) * keep[None])
    return out


def solve_kernel(shift, right, left, screen, boxes, terms, moved, field, other):
    shift_x, shift_y = shift[0], shift[1]
    full = BOX * BOX
    ahead = (shift_x * BOX + shift_y + full) % full
    back = (full - ahead) % full
    early = lax.broadcasted_iota(jnp.int32, (8, LANES), 1) < BOX
    sign = jnp.where(early, 1.0, -1.0)

    def first_tile(tile):
        return boxes[pl.ds(tile * 8, 8), :8, :].astype(jnp.float32)

    def second_tile(tile):
        return boxes[pl.ds(tile * 8, 8), 8:, :].astype(jnp.float32)

    def along_y(block):
        high, low = split(block)
        product = jnp.dot(
            jnp.concatenate([high, low], axis=1), right[...], preferred_element_type=jnp.float32
        )
        return product[:, :LANES] + product[:, LANES:]

    def forward_y(step, carry):
        for k, box in enumerate(shifted(second_tile, step * 4, 4, ahead, shift_x, shift_y)):
            tile = step * 4 + k
            moved[tile] = box
            other[tile] = first_tile(tile) * box
        tiles = pl.ds(step * 4, 4)
        field[tiles] = along_y(other[tiles].reshape(4 * BOX, LANES)).reshape(4, BOX, LANES)
        return carry

    lax.fori_loop(0, TILES // 4, forward_y, 0)

    def forward_x(step, carry):
        rows = pl.ds(pl.multiple_of(step * 8, 8), 8)
        parts = twist(fast_hartley([field[k, rows, :] for k in range(TILES)]), early)
        for k in range(TILES):
            field[k, rows, :] = sign * parts[k] + pltpu.roll(parts[k], BOX, 1)
        return carry

    lax.fori_loop(0, 8, forward_x, 0)

    def along_z(block):
        high, low = split(block)
        return jnp.dot(
            left[...], jnp.concatenate([high, low, high], axis=0), preferred_element_type=jnp.float32
        )

    def screened_z(step, carry):
        tiles = [step * 8 + k for k in range(8)]
        blocks = [jnp.concatenate([field[tiles[k]], field[tiles[k + 1]]], axis=1) for k in range(0, 8, 2)]
        blocks = [along_z(block) for block in blocks]
        for k in range(8):
            half = slice(k % 2 * LANES, (k % 2 + 1) * LANES)
            field[tiles[k]] = blocks[k // 2][:, half] * screen[tiles[k]]
        blocks = [jnp.concatenate([field[tiles[k]], field[tiles[k + 1]]], axis=1) for k in range(0, 8, 2)]
        blocks = [along_z(block) for block in blocks]
        for k in range(8):
            half = slice(k % 2 * LANES, (k % 2 + 1) * LANES)
            field[tiles[k]] = blocks[k // 2][:, half]
        return carry

    lax.fori_loop(0, TILES // 8, screened_z, 0)

    def inverse_x(step, carry):
        rows = pl.ds(pl.multiple_of(step * 8, 8), 8)
        parts = [field[k, rows, :] for k in range(TILES)]
        parts = [sign * part + pltpu.roll(part, BOX, 1) for part in parts]
        parts = fast_hartley(untwist(parts, early))
        for k in range(TILES):
            field[k, rows, :] = parts[k]
        return carry

    lax.fori_loop(0, 8, inverse_x, 0)

    def inverse_y(step, carry):
        tiles = pl.ds(step * 4, 4)
        potential = along_y(field[tiles].reshape(4 * BOX, LANES)).reshape(4, 8, 8, LANES)
        for k in range(4):
            other[step * 4 + k] = potential[k] * first_tile(step * 4 + k)
            moved[step * 4 + k] = potential[k] * moved[step * 4 + k]
        return carry

    lax.fori_loop(0, TILES // 4, inverse_y, 0)

    def pack(step, carry):
        carried = shifted(lambda tile: other[tile], step * 4, 4, back, -shift_x, -shift_y)
        for k in range(4):
            both = jnp.concatenate([moved[step * 4 + k], carried[k]], axis=1)
            terms[pl.ds((step * 4 + k) * 8, 8)] = both.astype(jnp.bfloat16)
        return carry

    lax.fori_loop(0, TILES // 4, pack, 0)


def sum_kernel(firsts, listed, terms, pieces, own, carried):
    own[...] = jnp.zeros_like(own)
    carried[...] = jnp.zeros_like(carried)

    def step(at, carry):
        for k in range(8):
            d = at * 8 + k
            both = terms[d].astype(jnp.float32)
            first, second = firsts[d], listed[N_DEV + d]
            own[first] = own[first] + both[:8]
            carried[second] = carried[second] + both[8:]
        return carry

    lax.fori_loop(0, N_DEV // 8, step, 0)
    for e in range(N_ORB):
        at = slice(e * ORB_DEV, (e + 1) * ORB_DEV)
        pieces[e] = (own[at] + carried[at]).reshape(ORB_DEV * 8, LANES).astype(jnp.bfloat16)


def join_kernel(pieces, result):
    for pair in range(ORB_DEV // 2):
        tiles = [pieces[tile, 16 * pair : 16 * pair + 16, :].astype(jnp.float32) for tile in range(TILES)]
        for side in range(2):
            rows = [tile[8 * side : 8 * side + 8] for tile in tiles]
            result[2 * pair + side] = jnp.concatenate(rows, axis=1).astype(jnp.bfloat16)


def body(orbitals, pair_first, second_owner, second_local, pair_shift, pair_count):
    f32, bf16, i32 = jnp.float32, jnp.bfloat16, jnp.int32
    shape = jax.ShapeDtypeStruct
    me = (lax.axis_index("orb") * 8 + lax.axis_index("slab")).reshape(1)
    rows = ORB_DEV * 8
    pair_shape = shape((N_DEV, 16, LANES), bf16)
    pieces = pl.pallas_call(
        spread_kernel, out_shape=shape((N_ORB, rows + 8, LANES), bf16),
        in_specs=[WHOLE_S, WHOLE_S, WHOLE_V], out_specs=WHOLE_V,
        compiler_params=PARAMS, name="spread",
    )(pair_first, pair_shift, orbitals)
    pieces = lax.all_to_all(pieces, "orb", split_axis=0, concat_axis=0, tiled=True)
    listed = pl.pallas_call(
        list_kernel, out_shape=shape((2 * N_DEV,), i32),
        in_specs=[WHOLE_S] * 3, out_specs=WHOLE_S,
        compiler_params=PARAMS, name="list",
    )(pair_count, second_owner[:, 0], second_local)
    picked, firsts, mine = pl.pallas_call(
        pick_kernel,
        out_shape=(pair_shape, shape((N_DEV,), i32), shape((2,), i32)),
        in_specs=[WHOLE_S, WHOLE_S, WHOLE_V],
        out_specs=(WHOLE_V, WHOLE_S, WHOLE_S),
        scratch_shapes=[
            pltpu.VMEM((N_DEV, 8, LANES), f32),
            pltpu.VMEM((N_ORB, LANES), i32),
            pltpu.SMEM((N_ORB, LANES), i32),
            pltpu.SemaphoreType.DMA,
        ],
        compiler_params=PARAMS, name="pick",
    )(me, listed, pieces)
    boxes = lax.all_to_all(picked, ("orb", "slab"), split_axis=0, concat_axis=0, tiled=True)
    right, left, screen = (jnp.asarray(table) for table in tables())
    terms = pl.pallas_call(
        solve_kernel, out_shape=pair_shape,
        in_specs=[WHOLE_S] + [WHOLE_V] * 4,
        out_specs=WHOLE_V,
        scratch_shapes=[
            pltpu.VMEM((TILES, 8, 8, LANES), f32),
            pltpu.VMEM((TILES, BOX, LANES), f32),
            pltpu.VMEM((TILES, 8, 8, LANES), f32),
        ],
        compiler_params=PARAMS, name="solve",
    )(mine, right, left, screen, boxes)
    terms = lax.all_to_all(terms, ("orb", "slab"), split_axis=0, concat_axis=0, tiled=True)
    pieces = pl.pallas_call(
        sum_kernel, out_shape=shape((N_ORB, rows, LANES), bf16),
        in_specs=[WHOLE_S, WHOLE_S, WHOLE_V], out_specs=WHOLE_V,
        scratch_shapes=[pltpu.VMEM((N_DEV, 8, LANES), f32)] * 2,
        compiler_params=PARAMS, name="sum",
    )(firsts, listed, terms)
    pieces = lax.all_to_all(pieces, "orb", split_axis=0, concat_axis=0, tiled=True)
    return pl.pallas_call(
        join_kernel, out_shape=shape((ORB_DEV, 8, BOX * BOX), bf16),
        in_specs=[WHOLE_V], out_specs=WHOLE_V,
        compiler_params=PARAMS, name="join",
    )(pieces)


def solution(mesh):
    in_specs = (P("orb", "slab", None), P("orb"), P(), P(), P("orb", None), P())
    out_specs = P("orb", "slab", None)
    return jax.shard_map(body, mesh=mesh, in_specs=in_specs, out_specs=out_specs, check_vma=False)
```

```python
import math

import jax
import jax.numpy as jnp
import numpy as np
from jax import lax
from jax.experimental import pallas as pl
from jax.experimental.pallas import tpu as pltpu
from jax.sharding import PartitionSpec as P

BOX = 64
ORB_DEV = 8
PAIR_DEV = 16
N_ORB = 32
N_DEV = 256
TILES = 32
LANES = 128
SCREENING = 0.02
PARAMS = pltpu.CompilerParams(vmem_limit_bytes=48 * 1024 * 1024)
WHOLE_V = pl.BlockSpec(memory_space=pltpu.VMEM)
WHOLE_S = pl.BlockSpec(memory_space=pltpu.SMEM)


def hartley_table():
    line = np.arange(BOX)
    angle = (line[:, None] * line[None, :] % BOX) * (2.0 * math.pi / BOX)
    return np.cos(angle) + np.sin(angle)


def halves(table):
    high = table.astype(np.float32).astype(jnp.bfloat16)
    low = (table - high.astype(np.float64)).astype(np.float32).astype(jnp.bfloat16)
    return high, low


def tables():
    high, low = halves(hartley_table())
    zero = np.zeros((BOX, BOX), high.dtype)

    def twice(table):
        return np.block([[table, zero], [zero, table]])

    right = np.block([[twice(high), twice(low)], [twice(high), np.zeros((128, 128), high.dtype)]])
    left = np.concatenate([high, high, low], axis=1)
    lam = 2.0 - 2.0 * np.cos(np.arange(BOX) * (2.0 * math.pi / BOX))
    lam_a = np.repeat(lam.reshape(2, TILES).T, BOX, axis=1)
    under = lam_a[:, None, :] + lam[None, :, None] + np.tile(lam, 2)[None, None, :] + SCREENING
    return right, left, (1.0 / BOX**3 / under).astype(np.float32)


def split(field):
    high = field.astype(jnp.bfloat16)
    low = (field - high.astype(jnp.float32)).astype(jnp.bfloat16)
    return high, low


def fast_hartley(parts):
    n = len(parts)
    if n == 1:
        return parts
    if n == 2:
        return [parts[0] + parts[1], parts[0] - parts[1]]
    even, odd = fast_hartley(parts[0::2]), fast_hartley(parts[1::2])
    m = n // 2
    out = [None] * n
    for k in range(m):
        if k == 0 or 4 * k == n:
            turned = odd[k]
        else:
            angle = 2.0 * math.pi * k / n
            turned = odd[k] * math.cos(angle) + odd[m - k] * math.sin(angle)
        out[k] = even[k] + turned
        out[k + m] = even[k] - turned
    return out


def twist(parts, first):
    out = []
    for k in range(TILES):
        mirror = parts[(TILES - k) % TILES]
        angle = 2.0 * math.pi * k / BOX
        if k == 0 or 2 * k == TILES:
            out.append(parts[k])
        else:
            out.append(jnp.where(first, parts[k], parts[k] * math.cos(angle) + mirror * math.sin(angle)))
    return out


def untwist(parts, first):
    out = []
    for k in range(TILES):
        mirror = parts[(TILES - k) % TILES]
        angle = 2.0 * math.pi * k / BOX
        back = 2.0 * math.pi * ((TILES - k) % TILES) / BOX
        if k == 0 or 2 * k == TILES:
            out.append(parts[k])
        else:
            out.append(jnp.where(first, parts[k], parts[k] * math.cos(angle) + mirror * math.sin(back)))
    return out


def spread_kernel(first, shift, orbitals, pieces, tall, about):
    for orbital in range(ORB_DEV):
        box = orbitals[orbital].astype(jnp.float32)
        for tile in range(TILES):
            row = tile * ORB_DEV * 8 + 8 * orbital
            tall[row : row + 8, :] = box[:, tile * LANES : (tile + 1) * LANES]
    about[...] = jnp.zeros_like(about)
    about[0:1, :PAIR_DEV] = first[...].astype(jnp.float32)
    about[1:3, :PAIR_DEV] = shift[...].astype(jnp.float32)
    placed = pltpu.roll(about[...], lax.axis_index("orb") % 8 * PAIR_DEV, 1).astype(jnp.bfloat16)
    for tile in range(TILES):
        for z in range(8):
            row = tile * ORB_DEV * 8 + z
            pieces[tile, z] = tall[pl.ds(row, ORB_DEV, stride=8), :].astype(jnp.bfloat16)
        pieces[tile, 8] = placed


def dot_rows(one, two):
    return lax.dot_general(one, two, (((1,), (1,)), ((), ())), preferred_element_type=jnp.float32)


def chosen(column):
    lane = lax.broadcasted_iota(jnp.int32, (N_DEV, LANES), 1).astype(jnp.float32)
    hits = [jnp.where(column == lane + half * LANES, 1.0, 0.0) for half in range(2)]
    return jnp.concatenate(hits, axis=1).astype(jnp.bfloat16)


def place_kernel(count, owner, local, place, second, choose):
    shape = (4, LANES)
    slot = lax.broadcasted_iota(jnp.int32, shape, 0) * LANES + lax.broadcasted_iota(jnp.int32, shape, 1)
    orb, rank = slot // PAIR_DEV, slot % PAIR_DEV
    before, live = jnp.zeros(shape, jnp.int32), jnp.zeros(shape, jnp.int32)
    for e in range(N_ORB):
        before = before + jnp.where(orb > e, count[e], 0)
        live = jnp.where(orb == e, count[e], live)
    rank = jnp.where(rank < live, before + rank, -1).astype(jnp.float32)
    pair = lax.broadcasted_iota(jnp.int32, (N_DEV, LANES), 0).astype(jnp.float32)
    second[...] = (owner[...] * ORB_DEV + local[...]).astype(jnp.float32)
    for k in range(4):
        at = slice(k * LANES, (k + 1) * LANES)
        place[:, at] = jnp.where(pair == rank[k : k + 1], 1.0, 0.0).astype(jnp.bfloat16)
    rows = jnp.concatenate([second[k : k + 1, :] for k in range(4)], axis=1)
    rows = jnp.broadcast_to(rows, (LANES, 4 * LANES)).astype(jnp.bfloat16)
    choose[...] = chosen(dot_rows(place[...], rows))


def pick_kernel(me, place, second, choose, pieces, picked, index, mine, tall):
    blocks = []
    for k in range(4):
        block = jnp.sum(pieces[8 * k : 8 * k + 8, 8].astype(jnp.float32), axis=0)
        row = lax.broadcasted_iota(jnp.int32, (8, LANES), 0)
        lane = lax.broadcasted_iota(jnp.int32, (8, LANES), 1)
        orbital = (8 * (8 * k + lane // PAIR_DEV)).astype(jnp.float32)
        block = jnp.where(row == 0, block + orbital, block)
        blocks.append(jnp.where(row == 3, jnp.broadcast_to(second[k : k + 1, :], (8, LANES)), block))
    facts = jnp.concatenate(blocks, axis=1)
    first = jnp.broadcast_to(facts[0:1], (LANES, 4 * LANES)).astype(jnp.bfloat16)
    choose_first = chosen(dot_rows(place[...], first))
    known = dot_rows(facts.astype(jnp.bfloat16), place[...])
    index[0:1, :] = known[0:1].astype(jnp.int32)
    index[1:2, :] = known[3:4].astype(jnp.int32)
    lane = lax.broadcasted_iota(jnp.int32, (8, N_DEV), 1)
    here = jnp.sum(jnp.where(lane == me[0], known, 0.0), axis=1, keepdims=True)
    lane = lax.broadcasted_iota(jnp.int32, (1, LANES), 1)
    mine[...] = jnp.where(lane == 0, here[1:2], here[2:3]).astype(jnp.int32)
    for z in range(0, 8, 2):
        field = [
            pieces[:, z + k].astype(jnp.float32).reshape(N_DEV, LANES).astype(jnp.bfloat16) for k in range(2)
        ]
        field = jnp.concatenate(field, axis=1)
        for side, picker in enumerate((choose_first, choose[...])):
            out = jnp.dot(picker, field, preferred_element_type=jnp.float32)
            tall[pl.ds(8 * side + z, N_DEV, stride=16), :] = out[:, :LANES]
            tall[pl.ds(8 * side + z + 1, N_DEV, stride=16), :] = out[:, LANES:]
    for k in range(0, N_DEV, 8):
        picked[k : k + 8] = tall[16 * k : 16 * k + 128, :].reshape(8, 16, LANES).astype(jnp.bfloat16)


def shifted(tiles, start, count, flat, shift_x, shift_y):
    lane = lax.broadcasted_iota(jnp.int32, (8, LANES), 1)
    whole, rest = flat // LANES, flat % LANES
    later = (lane >= rest)[None]
    y = lane % BOX - shift_y
    keep_y = (y >= 0) & (y < BOX)
    turned = [
        pltpu.roll(tiles((start + k - whole - 1 + 2 * TILES) % TILES), rest, 2) for k in range(count + 1)
    ]
    out = []
    for k in range(count):
        x = 2 * (start + k) + lane // BOX - shift_x
        keep = jnp.where(keep_y & (x >= 0) & (x < BOX), 1.0, 0.0)
        out.append(jnp.where(later, turned[k + 1], turned[k]) * keep[None])
    return out


def solve_kernel(shift, right, left, screen, boxes, terms, moved, field, other):
    shift_x, shift_y = shift[0, 0], shift[0, 1]
    full = BOX * BOX
    ahead = (shift_x * BOX + shift_y + full) % full
    back = (full - ahead) % full
    early = lax.broadcasted_iota(jnp.int32, (8, LANES), 1) < BOX
    sign = jnp.where(early, 1.0, -1.0)

    def first_tile(tile):
        return boxes[pl.ds(tile * 8, 8), :8, :].astype(jnp.float32)

    def second_tile(tile):
        return boxes[pl.ds(tile * 8, 8), 8:, :].astype(jnp.float32)

    def along_y(block):
        high, low = split(block)
        product = jnp.dot(
            jnp.concatenate([high, low], axis=1), right[...], preferred_element_type=jnp.float32
        )
        return product[:, :LANES] + product[:, LANES:]

    def forward_y(step, carry):
        for k, box in enumerate(shifted(second_tile, step * 4, 4, ahead, shift_x, shift_y)):
            tile = step * 4 + k
            moved[tile] = box
            other[tile] = first_tile(tile) * box
        tiles = pl.ds(step * 4, 4)
        field[tiles] = along_y(other[tiles].reshape(4 * BOX, LANES)).reshape(4, BOX, LANES)
        return carry

    lax.fori_loop(0, TILES // 4, forward_y, 0)

    def forward_x(step, carry):
        rows = pl.ds(pl.multiple_of(step * 8, 8), 8)
        parts = twist(fast_hartley([field[k, rows, :] for k in range(TILES)]), early)
        for k in range(TILES):
            field[k, rows, :] = sign * parts[k] + pltpu.roll(parts[k], BOX, 1)
        return carry

    lax.fori_loop(0, 8, forward_x, 0)

    def along_z(block):
        high, low = split(block)
        return jnp.dot(
            left[...], jnp.concatenate([high, low, high], axis=0), preferred_element_type=jnp.float32
        )

    def screened_z(step, carry):
        tiles = [step * 8 + k for k in range(8)]
        blocks = [jnp.concatenate([field[tiles[k]], field[tiles[k + 1]]], axis=1) for k in range(0, 8, 2)]
        blocks = [along_z(block) for block in blocks]
        for k in range(8):
            half = slice(k % 2 * LANES, (k % 2 + 1) * LANES)
            field[tiles[k]] = blocks[k // 2][:, half] * screen[tiles[k]]
        blocks = [jnp.concatenate([field[tiles[k]], field[tiles[k + 1]]], axis=1) for k in range(0, 8, 2)]
        blocks = [along_z(block) for block in blocks]
        for k in range(8):
            half = slice(k % 2 * LANES, (k % 2 + 1) * LANES)
            field[tiles[k]] = blocks[k // 2][:, half]
        return carry

    lax.fori_loop(0, TILES // 8, screened_z, 0)

    def inverse_x(step, carry):
        rows = pl.ds(pl.multiple_of(step * 8, 8), 8)
        parts = [field[k, rows, :] for k in range(TILES)]
        parts = [sign * part + pltpu.roll(part, BOX, 1) for part in parts]
        parts = fast_hartley(untwist(parts, early))
        for k in range(TILES):
            field[k, rows, :] = parts[k]
        return carry

    lax.fori_loop(0, 8, inverse_x, 0)

    def inverse_y(step, carry):
        tiles = pl.ds(step * 4, 4)
        potential = along_y(field[tiles].reshape(4 * BOX, LANES)).reshape(4, 8, 8, LANES)
        for k in range(4):
            other[step * 4 + k] = potential[k] * first_tile(step * 4 + k)
            moved[step * 4 + k] = potential[k] * moved[step * 4 + k]
        return carry

    lax.fori_loop(0, TILES // 4, inverse_y, 0)

    def pack(step, carry):
        carried = shifted(lambda tile: other[tile], step * 4, 4, back, -shift_x, -shift_y)
        for k in range(4):
            both = jnp.concatenate([moved[step * 4 + k], carried[k]], axis=1)
            terms[pl.ds((step * 4 + k) * 8, 8)] = both.astype(jnp.bfloat16)
        return carry

    lax.fori_loop(0, TILES // 4, pack, 0)


def sum_kernel(index, terms, pieces, own, carried):
    own[...] = jnp.zeros_like(own)
    carried[...] = jnp.zeros_like(carried)

    def step(at, carry):
        both = terms[pl.ds(at * 8, 8)].astype(jnp.float32)
        first = [index[0, at * 8 + k] for k in range(8)]
        second = [index[1, at * 8 + k] for k in range(8)]
        for k in range(8):
            own[first[k]] = own[first[k]] + both[k, :8]
            carried[second[k]] = carried[second[k]] + both[k, 8:]
        return carry

    lax.fori_loop(0, N_DEV // 8, step, 0)
    for e in range(N_ORB):
        at = slice(e * ORB_DEV, (e + 1) * ORB_DEV)
        pieces[e] = (own[at] + carried[at]).reshape(ORB_DEV * 8, LANES).astype(jnp.bfloat16)


def join_kernel(pieces, result):
    for pair in range(ORB_DEV // 2):
        tiles = [pieces[tile, 16 * pair : 16 * pair + 16, :].astype(jnp.float32) for tile in range(TILES)]
        for side in range(2):
            rows = [tile[8 * side : 8 * side + 8] for tile in tiles]
            result[2 * pair + side] = jnp.concatenate(rows, axis=1).astype(jnp.bfloat16)


def body(orbitals, pair_first, second_owner, second_local, pair_shift, pair_count):
    f32, bf16, i32 = jnp.float32, jnp.bfloat16, jnp.int32
    shape = jax.ShapeDtypeStruct
    me = (lax.axis_index("orb") * 8 + lax.axis_index("slab")).reshape(1)
    rows = ORB_DEV * 8
    pair_shape = shape((N_DEV, 16, LANES), bf16)
    pieces = pl.pallas_call(
        spread_kernel, out_shape=shape((N_ORB, 9, ORB_DEV, LANES), bf16),
        in_specs=[WHOLE_V] * 3, out_specs=WHOLE_V,
        scratch_shapes=[pltpu.VMEM((TILES * rows, LANES), f32), pltpu.VMEM((8, LANES), f32)],
        compiler_params=PARAMS, name="spread",
    )(pair_first.reshape(1, PAIR_DEV), pair_shift.T, orbitals)
    pieces = lax.all_to_all(pieces, "orb", split_axis=0, concat_axis=0, tiled=True)
    place, second, choose = pl.pallas_call(
        place_kernel,
        out_shape=(shape((N_DEV, 4 * LANES), bf16), shape((4, LANES), f32), shape((N_DEV, N_DEV), bf16)),
        in_specs=[WHOLE_S, WHOLE_V, WHOLE_V], out_specs=(WHOLE_V,) * 3,
        compiler_params=PARAMS, name="place",
    )(pair_count, second_owner.reshape(4, LANES), second_local.reshape(4, LANES))
    picked, index, mine = pl.pallas_call(
        pick_kernel,
        out_shape=(pair_shape, shape((2, N_DEV), i32), shape((1, LANES), i32)),
        in_specs=[WHOLE_S] + [WHOLE_V] * 4,
        out_specs=(WHOLE_V,) * 3,
        scratch_shapes=[pltpu.VMEM((N_DEV * 16, LANES), f32)],
        compiler_params=PARAMS, name="pick",
    )(me, place, second, choose, pieces)
    boxes = lax.all_to_all(picked, ("orb", "slab"), split_axis=0, concat_axis=0, tiled=True)
    right, left, screen = (jnp.asarray(table) for table in tables())
    terms = pl.pallas_call(
        solve_kernel, out_shape=pair_shape,
        in_specs=[WHOLE_S] + [WHOLE_V] * 4,
        out_specs=WHOLE_V,
        scratch_shapes=[
            pltpu.VMEM((TILES, 8, 8, LANES), f32),
            pltpu.VMEM((TILES, BOX, LANES), f32),
            pltpu.VMEM((TILES, 8, 8, LANES), f32),
        ],
        compiler_params=PARAMS, name="solve",
    )(mine, right, left, screen, boxes)
    terms = lax.all_to_all(terms, ("orb", "slab"), split_axis=0, concat_axis=0, tiled=True)
    pieces = pl.pallas_call(
        sum_kernel, out_shape=shape((N_ORB, rows, LANES), bf16),
        in_specs=[WHOLE_S, WHOLE_V], out_specs=WHOLE_V,
        scratch_shapes=[pltpu.VMEM((N_DEV, 8, LANES), f32)] * 2,
        compiler_params=PARAMS, name="sum",
    )(index, terms)
    pieces = lax.all_to_all(pieces, "orb", split_axis=0, concat_axis=0, tiled=True)
    return pl.pallas_call(
        join_kernel, out_shape=shape((ORB_DEV, 8, BOX * BOX), bf16),
        in_specs=[WHOLE_V], out_specs=WHOLE_V,
        compiler_params=PARAMS, name="join",
    )(pieces)


def solution(mesh):
    in_specs = (P("orb", "slab", None), P("orb"), P(), P(), P("orb", None), P())
    out_specs = P("orb", "slab", None)
    return jax.shard_map(body, mesh=mesh, in_specs=in_specs, out_specs=out_specs, check_vma=False)
```

```python
import math

import jax
import jax.numpy as jnp
import numpy as np
from jax import lax
from jax.experimental import pallas as pl
from jax.experimental.pallas import tpu as pltpu
from jax.sharding import PartitionSpec as P

BOX = 64
ORB_DEV = 8
PAIR_DEV = 16
N_ORB = 32
N_DEV = 256
TILES = 32
LANES = 128
SCREENING = 0.02
PARAMS = pltpu.CompilerParams(vmem_limit_bytes=48 * 1024 * 1024)
WHOLE_V = pl.BlockSpec(memory_space=pltpu.VMEM)
WHOLE_S = pl.BlockSpec(memory_space=pltpu.SMEM)


def hartley_table():
    line = np.arange(BOX)
    angle = (line[:, None] * line[None, :] % BOX) * (2.0 * math.pi / BOX)
    return np.cos(angle) + np.sin(angle)


def halves(table):
    high = table.astype(np.float32).astype(jnp.bfloat16)
    low = (table - high.astype(np.float64)).astype(np.float32).astype(jnp.bfloat16)
    return high, low


def tables():
    high, low = halves(hartley_table())
    zero = np.zeros((BOX, BOX), high.dtype)

    def twice(table):
        return np.block([[table, zero], [zero, table]])

    right = np.block([[twice(high), twice(low)], [twice(high), np.zeros((128, 128), high.dtype)]])
    left = np.concatenate([high, high, low], axis=1)
    lam = 2.0 - 2.0 * np.cos(np.arange(BOX) * (2.0 * math.pi / BOX))
    lam_a = np.repeat(lam.reshape(2, TILES).T, BOX, axis=1)
    under = lam_a[:, None, :] + lam[None, :, None] + np.tile(lam, 2)[None, None, :] + SCREENING
    return right, left, (1.0 / BOX**3 / under).astype(np.float32)


def split(field):
    high = field.astype(jnp.bfloat16)
    low = (field - high.astype(jnp.float32)).astype(jnp.bfloat16)
    return high, low


def fast_hartley(parts):
    n = len(parts)
    if n == 1:
        return parts
    if n == 2:
        return [parts[0] + parts[1], parts[0] - parts[1]]
    even, odd = fast_hartley(parts[0::2]), fast_hartley(parts[1::2])
    m = n // 2
    out = [None] * n
    for k in range(m):
        if k == 0 or 4 * k == n:
            turned = odd[k]
        else:
            angle = 2.0 * math.pi * k / n
            turned = odd[k] * math.cos(angle) + odd[m - k] * math.sin(angle)
        out[k] = even[k] + turned
        out[k + m] = even[k] - turned
    return out


def twist(parts, first):
    out = []
    for k in range(TILES):
        mirror = parts[(TILES - k) % TILES]
        angle = 2.0 * math.pi * k / BOX
        if k == 0 or 2 * k == TILES:
            out.append(parts[k])
        else:
            out.append(jnp.where(first, parts[k], parts[k] * math.cos(angle) + mirror * math.sin(angle)))
    return out


def untwist(parts, first):
    out = []
    for k in range(TILES):
        mirror = parts[(TILES - k) % TILES]
        angle = 2.0 * math.pi * k / BOX
        back = 2.0 * math.pi * ((TILES - k) % TILES) / BOX
        if k == 0 or 2 * k == TILES:
            out.append(parts[k])
        else:
            out.append(jnp.where(first, parts[k], parts[k] * math.cos(angle) + mirror * math.sin(back)))
    return out


def spread_kernel(first, shift, orbitals, pieces, tall, about):
    for orbital in range(ORB_DEV):
        box = orbitals[orbital].astype(jnp.float32)
        for tile in range(TILES):
            row = tile * ORB_DEV * 8 + 8 * orbital
            tall[row : row + 8, :] = box[:, tile * LANES : (tile + 1) * LANES]
    about[...] = jnp.zeros_like(about)
    about[0:1, :PAIR_DEV] = first[...].astype(jnp.float32)
    about[1:3, :PAIR_DEV] = shift[...].astype(jnp.float32)
    placed = pltpu.roll(about[...], lax.axis_index("orb") % 8 * PAIR_DEV, 1).astype(jnp.bfloat16)
    for tile in range(TILES):
        for z in range(8):
            row = tile * ORB_DEV * 8 + z
            pieces[tile, z] = tall[pl.ds(row, ORB_DEV, stride=8), :].astype(jnp.bfloat16)
        pieces[tile, 8] = placed


def dot_rows(one, two):
    return lax.dot_general(one, two, (((1,), (1,)), ((), ())), preferred_element_type=jnp.float32)


def chosen(column):
    lane = lax.broadcasted_iota(jnp.int32, (N_DEV, LANES), 1).astype(jnp.float32)
    hits = [jnp.where(column == lane + half * LANES, 1.0, 0.0) for half in range(2)]
    return jnp.concatenate(hits, axis=1).astype(jnp.bfloat16)


def place_kernel(count, owner, local, place, second, choose):
    shape = (4, LANES)
    slot = lax.broadcasted_iota(jnp.int32, shape, 0) * LANES + lax.broadcasted_iota(jnp.int32, shape, 1)
    orb, rank = slot // PAIR_DEV, slot % PAIR_DEV
    before, live = jnp.zeros(shape, jnp.int32), jnp.zeros(shape, jnp.int32)
    for e in range(N_ORB):
        before = before + jnp.where(orb > e, count[e], 0)
        live = jnp.where(orb == e, count[e], live)
    rank = jnp.where(rank < live, before + rank, -1).astype(jnp.float32)
    pair = lax.broadcasted_iota(jnp.int32, (N_DEV, LANES), 0).astype(jnp.float32)
    second[...] = (owner[...] * ORB_DEV + local[...]).astype(jnp.float32)
    for k in range(4):
        at = slice(k * LANES, (k + 1) * LANES)
        place[:, at] = jnp.where(pair == rank[k : k + 1], 1.0, 0.0).astype(jnp.bfloat16)
    rows = jnp.concatenate([second[k : k + 1, :] for k in range(4)], axis=1)
    rows = jnp.broadcast_to(rows, (LANES, 4 * LANES)).astype(jnp.bfloat16)
    choose[...] = chosen(dot_rows(place[...], rows))


def pick_kernel(me, place, second, choose, pieces, picked, index, mine, tall):
    blocks = []
    for k in range(4):
        block = jnp.sum(pieces[8 * k : 8 * k + 8, 8].astype(jnp.float32), axis=0)
        row = lax.broadcasted_iota(jnp.int32, (8, LANES), 0)
        lane = lax.broadcasted_iota(jnp.int32, (8, LANES), 1)
        orbital = (8 * (8 * k + lane // PAIR_DEV)).astype(jnp.float32)
        block = jnp.where(row == 0, block + orbital, block)
        blocks.append(jnp.where(row == 3, jnp.broadcast_to(second[k : k + 1, :], (8, LANES)), block))
    facts = jnp.concatenate(blocks, axis=1)
    first = jnp.broadcast_to(facts[0:1], (LANES, 4 * LANES)).astype(jnp.bfloat16)
    choose_first = chosen(dot_rows(place[...], first))
    known = dot_rows(facts.astype(jnp.bfloat16), place[...])
    index[0:1, :] = known[0:1].astype(jnp.int32)
    index[1:2, :] = known[3:4].astype(jnp.int32)
    lane = lax.broadcasted_iota(jnp.int32, (8, N_DEV), 1)
    here = jnp.sum(jnp.where(lane == me[0], known, 0.0), axis=1, keepdims=True)
    lane = lax.broadcasted_iota(jnp.int32, (1, LANES), 1)
    mine[...] = jnp.where(lane == 0, here[1:2], here[2:3]).astype(jnp.int32)
    for z in range(0, 8, 2):
        field = [
            pieces[:, z + k].astype(jnp.float32).reshape(N_DEV, LANES).astype(jnp.bfloat16) for k in range(2)
        ]
        field = jnp.concatenate(field, axis=1)
        for side, picker in enumerate((choose_first, choose[...])):
            out = jnp.dot(picker, field, preferred_element_type=jnp.float32)
            tall[pl.ds(8 * side + z, N_DEV, stride=16), :] = out[:, :LANES]
            tall[pl.ds(8 * side + z + 1, N_DEV, stride=16), :] = out[:, LANES:]
    for k in range(0, N_DEV, 8):
        picked[k : k + 8] = tall[16 * k : 16 * k + 128, :].reshape(8, 16, LANES).astype(jnp.bfloat16)


def shifted(tiles, start, count, flat, shift_x, shift_y):
    lane = lax.broadcasted_iota(jnp.int32, (8, LANES), 1)
    whole, rest = flat // LANES, flat % LANES
    later = (lane >= rest)[None]
    y = lane % BOX - shift_y
    keep_y = (y >= 0) & (y < BOX)
    turned = [
        pltpu.roll(tiles((start + k - whole - 1 + 2 * TILES) % TILES), rest, 2) for k in range(count + 1)
    ]
    out = []
    for k in range(count):
        x = 2 * (start + k) + lane // BOX - shift_x
        keep = jnp.where(keep_y & (x >= 0) & (x < BOX), 1.0, 0.0)
        out.append(jnp.where(later, turned[k + 1], turned[k]) * keep[None])
    return out


def solve_kernel(shift, right, left, screen, boxes, terms, moved, field, other):
    shift_x, shift_y = shift[0, 0], shift[0, 1]
    full = BOX * BOX
    ahead = (shift_x * BOX + shift_y + full) % full
    back = (full - ahead) % full
    early = lax.broadcasted_iota(jnp.int32, (8, LANES), 1) < BOX
    sign = jnp.where(early, 1.0, -1.0)

    def first_tile(tile):
        return boxes[pl.ds(tile * 8, 8), :8, :].astype(jnp.float32)

    def second_tile(tile):
        return boxes[pl.ds(tile * 8, 8), 8:, :].astype(jnp.float32)

    def along_y(block):
        high, low = split(block)
        product = jnp.dot(
            jnp.concatenate([high, low], axis=1), right[...], preferred_element_type=jnp.float32
        )
        return product[:, :LANES] + product[:, LANES:]

    for start in range(0, TILES, 4):
        products = []
        for k, box in enumerate(shifted(second_tile, start, 4, ahead, shift_x, shift_y)):
            moved[start + k] = box
            products.append(first_tile(start + k) * box)
        block = along_y(jnp.stack(products).reshape(4 * BOX, LANES)).reshape(4, BOX, LANES)
        for k in range(4):
            field[start + k] = block[k]

    for row in range(0, BOX, 8):
        parts = twist(fast_hartley([field[k, row : row + 8, :] for k in range(TILES)]), early)
        for k in range(TILES):
            field[k, row : row + 8, :] = sign * parts[k] + pltpu.roll(parts[k], BOX, 1)

    def along_z(block):
        high, low = split(block)
        return jnp.dot(
            left[...], jnp.concatenate([high, low, high], axis=0), preferred_element_type=jnp.float32
        )

    for tile in range(0, TILES, 2):
        block = along_z(jnp.concatenate([field[tile], field[tile + 1]], axis=1))
        block = block * jnp.concatenate([screen[tile], screen[tile + 1]], axis=1)
        block = along_z(block)
        field[tile] = block[:, :LANES]
        field[tile + 1] = block[:, LANES:]

    for row in range(0, BOX, 8):
        parts = [field[k, row : row + 8, :] for k in range(TILES)]
        parts = [sign * part + pltpu.roll(part, BOX, 1) for part in parts]
        parts = fast_hartley(untwist(parts, early))
        for k in range(TILES):
            field[k, row : row + 8, :] = parts[k]

    for start in range(0, TILES, 4):
        block = field[start : start + 4].reshape(4 * BOX, LANES)
        potential = along_y(block).reshape(4, 8, 8, LANES)
        for k in range(4):
            other[start + k] = potential[k] * first_tile(start + k)
            moved[start + k] = potential[k] * moved[start + k]

    for start in range(0, TILES, 4):
        carried = shifted(lambda tile: other[tile], start, 4, back, -shift_x, -shift_y)
        for k in range(4):
            both = jnp.concatenate([moved[start + k], carried[k]], axis=1)
            terms[(start + k) * 8 : (start + k + 1) * 8] = both.astype(jnp.bfloat16)


def sum_kernel(index, terms, pieces, own, carried):
    own[...] = jnp.zeros_like(own)
    carried[...] = jnp.zeros_like(carried)

    def step(at, carry):
        both = terms[pl.ds(at * 8, 8)].astype(jnp.float32)
        first = [index[0, at * 8 + k] for k in range(8)]
        second = [index[1, at * 8 + k] for k in range(8)]
        for k in range(8):
            own[first[k]] = own[first[k]] + both[k, :8]
            carried[second[k]] = carried[second[k]] + both[k, 8:]
        return carry

    lax.fori_loop(0, N_DEV // 8, step, 0)
    for e in range(N_ORB):
        at = slice(e * ORB_DEV, (e + 1) * ORB_DEV)
        pieces[e] = (own[at] + carried[at]).reshape(ORB_DEV * 8, LANES).astype(jnp.bfloat16)


def join_kernel(pieces, result):
    for pair in range(ORB_DEV // 2):
        tiles = [pieces[tile, 16 * pair : 16 * pair + 16, :].astype(jnp.float32) for tile in range(TILES)]
        for side in range(2):
            rows = [tile[8 * side : 8 * side + 8] for tile in tiles]
            result[2 * pair + side] = jnp.concatenate(rows, axis=1).astype(jnp.bfloat16)


def body(orbitals, pair_first, second_owner, second_local, pair_shift, pair_count):
    f32, bf16, i32 = jnp.float32, jnp.bfloat16, jnp.int32
    shape = jax.ShapeDtypeStruct
    me = (lax.axis_index("orb") * 8 + lax.axis_index("slab")).reshape(1)
    rows = ORB_DEV * 8
    pair_shape = shape((N_DEV, 16, LANES), bf16)
    pieces = pl.pallas_call(
        spread_kernel, out_shape=shape((N_ORB, 9, ORB_DEV, LANES), bf16),
        in_specs=[WHOLE_V] * 3, out_specs=WHOLE_V,
        scratch_shapes=[pltpu.VMEM((TILES * rows, LANES), f32), pltpu.VMEM((8, LANES), f32)],
        compiler_params=PARAMS, name="spread",
    )(pair_first.reshape(1, PAIR_DEV), pair_shift.T, orbitals)
    pieces = lax.all_to_all(pieces, "orb", split_axis=0, concat_axis=0, tiled=True)
    place, second, choose = pl.pallas_call(
        place_kernel,
        out_shape=(shape((N_DEV, 4 * LANES), bf16), shape((4, LANES), f32), shape((N_DEV, N_DEV), bf16)),
        in_specs=[WHOLE_S, WHOLE_V, WHOLE_V], out_specs=(WHOLE_V,) * 3,
        compiler_params=PARAMS, name="place",
    )(pair_count, second_owner.reshape(4, LANES), second_local.reshape(4, LANES))
    picked, index, mine = pl.pallas_call(
        pick_kernel,
        out_shape=(pair_shape, shape((2, N_DEV), i32), shape((1, LANES), i32)),
        in_specs=[WHOLE_S] + [WHOLE_V] * 4,
        out_specs=(WHOLE_V,) * 3,
        scratch_shapes=[pltpu.VMEM((N_DEV * 16, LANES), f32)],
        compiler_params=PARAMS, name="pick",
    )(me, place, second, choose, pieces)
    boxes = lax.all_to_all(picked, ("orb", "slab"), split_axis=0, concat_axis=0, tiled=True)
    right, left, screen = (jnp.asarray(table) for table in tables())
    terms = pl.pallas_call(
        solve_kernel, out_shape=pair_shape,
        in_specs=[WHOLE_S] + [WHOLE_V] * 4,
        out_specs=WHOLE_V,
        scratch_shapes=[
            pltpu.VMEM((TILES, 8, 8, LANES), f32),
            pltpu.VMEM((TILES, BOX, LANES), f32),
            pltpu.VMEM((TILES, 8, 8, LANES), f32),
        ],
        compiler_params=PARAMS, name="solve",
    )(mine, right, left, screen, boxes)
    terms = lax.all_to_all(terms, ("orb", "slab"), split_axis=0, concat_axis=0, tiled=True)
    pieces = pl.pallas_call(
        sum_kernel, out_shape=shape((N_ORB, rows, LANES), bf16),
        in_specs=[WHOLE_S, WHOLE_V], out_specs=WHOLE_V,
        scratch_shapes=[pltpu.VMEM((N_DEV, 8, LANES), f32)] * 2,
        compiler_params=PARAMS, name="sum",
    )(index, terms)
    pieces = lax.all_to_all(pieces, "orb", split_axis=0, concat_axis=0, tiled=True)
    return pl.pallas_call(
        join_kernel, out_shape=shape((ORB_DEV, 8, BOX * BOX), bf16),
        in_specs=[WHOLE_V], out_specs=WHOLE_V,
        compiler_params=PARAMS, name="join",
    )(pieces)


def solution(mesh):
    in_specs = (P("orb", "slab", None), P("orb"), P(), P(), P("orb", None), P())
    out_specs = P("orb", "slab", None)
    return jax.shard_map(body, mesh=mesh, in_specs=in_specs, out_specs=out_specs, check_vma=False)
```

```python
import math

import jax
import jax.numpy as jnp
import numpy as np
from jax import lax
from jax.experimental import pallas as pl
from jax.experimental.pallas import tpu as pltpu
from jax.sharding import PartitionSpec as P

BOX = 64
ORB_DEV = 8
PAIR_DEV = 16
N_ORB = 32
N_DEV = 256
TILES = 32
LANES = 128
SCREENING = 0.02
GROUPS = 4
PARAMS = pltpu.CompilerParams(vmem_limit_bytes=48 * 1024 * 1024)
WHOLE_V = pl.BlockSpec(memory_space=pltpu.VMEM)
WHOLE_H = pl.BlockSpec(memory_space=pltpu.HBM)
WHOLE_S = pl.BlockSpec(memory_space=pltpu.SMEM)


def hartley_table():
    line = np.arange(BOX)
    angle = (line[:, None] * line[None, :] % BOX) * (2.0 * math.pi / BOX)
    return np.cos(angle) + np.sin(angle)


def halves(table):
    high = table.astype(np.float32).astype(jnp.bfloat16)
    low = (table - high.astype(np.float64)).astype(np.float32).astype(jnp.bfloat16)
    return high, low


def tables():
    high, low = halves(hartley_table())
    zero = np.zeros((BOX, BOX), high.dtype)

    def twice(table):
        return np.block([[table, zero], [zero, table]])

    right = np.block([[twice(high), twice(low)], [twice(high), np.zeros((128, 128), high.dtype)]])
    left = np.concatenate([high, high, low], axis=1)
    lam = 2.0 - 2.0 * np.cos(np.arange(BOX) * (2.0 * math.pi / BOX))
    lam_a = np.repeat(lam.reshape(2, TILES).T, BOX, axis=1)
    under = lam_a[:, None, :] + lam[None, :, None] + np.tile(lam, 2)[None, None, :] + SCREENING
    return right, left, (1.0 / BOX**3 / under).astype(np.float32)


def split(field):
    high = field.astype(jnp.bfloat16)
    low = (field - high.astype(jnp.float32)).astype(jnp.bfloat16)
    return high, low


def fast_hartley(parts):
    n = len(parts)
    if n == 1:
        return parts
    if n == 2:
        return [parts[0] + parts[1], parts[0] - parts[1]]
    even, odd = fast_hartley(parts[0::2]), fast_hartley(parts[1::2])
    m = n // 2
    out = [None] * n
    for k in range(m):
        if k == 0 or 4 * k == n:
            turned = odd[k]
        else:
            angle = 2.0 * math.pi * k / n
            turned = odd[k] * math.cos(angle) + odd[m - k] * math.sin(angle)
        out[k] = even[k] + turned
        out[k + m] = even[k] - turned
    return out


def twist(parts, first):
    out = []
    for k in range(TILES):
        mirror = parts[(TILES - k) % TILES]
        angle = 2.0 * math.pi * k / BOX
        if k == 0 or 2 * k == TILES:
            out.append(parts[k])
        else:
            out.append(jnp.where(first, parts[k], parts[k] * math.cos(angle) + mirror * math.sin(angle)))
    return out


def untwist(parts, first):
    out = []
    for k in range(TILES):
        mirror = parts[(TILES - k) % TILES]
        angle = 2.0 * math.pi * k / BOX
        back = 2.0 * math.pi * ((TILES - k) % TILES) / BOX
        if k == 0 or 2 * k == TILES:
            out.append(parts[k])
        else:
            out.append(jnp.where(first, parts[k], parts[k] * math.cos(angle) + mirror * math.sin(back)))
    return out


def spread_kernel(first, shift, orbitals, pieces, taken, tall, small, about, packed, arrived, sent):
    few = [
        pltpu.make_async_copy(first, small.at[0:1], arrived.at[GROUPS]),
        pltpu.make_async_copy(shift, small.at[8:10], arrived.at[GROUPS + 1]),
    ]
    width = BOX * BOX // GROUPS
    many = [
        pltpu.make_async_copy(orbitals.at[:, :, pl.ds(k * width, width)], taken.at[k], arrived.at[k])
        for k in range(GROUPS)
    ]
    for copy in few + many:
        copy.start()
    about[...] = jnp.zeros_like(about)
    for copy in few:
        copy.wait()
    about[0:1, :PAIR_DEV] = small[0:1, :].astype(jnp.float32)
    about[1:3, :PAIR_DEV] = small[8:10, :].astype(jnp.float32)
    placed = pltpu.roll(about[...], lax.axis_index("orb") % 8 * PAIR_DEV, 1).astype(jnp.bfloat16)
    inside = TILES // GROUPS
    out = []
    for k in range(GROUPS):
        many[k].wait()
        for orbital in range(ORB_DEV):
            box = taken[k, orbital].astype(jnp.float32)
            for tile in range(inside):
                row = (k * inside + tile) * ORB_DEV * 8 + 8 * orbital
                tall[row : row + 8, :] = box[:, tile * LANES : (tile + 1) * LANES]
        for tile in range(k * inside, (k + 1) * inside):
            for z in range(8):
                row = tile * ORB_DEV * 8 + z
                packed[tile, z] = tall[pl.ds(row, ORB_DEV, stride=8), :].astype(jnp.bfloat16)
            packed[tile, 8] = placed
        at = pl.ds(k * inside, inside)
        out.append(pltpu.make_async_copy(packed.at[at], pieces.at[at], sent.at[k]))
        out[k].start()
    for copy in out:
        copy.wait()


def dot_rows(one, two):
    return lax.dot_general(one, two, (((1,), (1,)), ((), ())), preferred_element_type=jnp.float32)


def chosen(column):
    lane = lax.broadcasted_iota(jnp.int32, (N_DEV, LANES), 1).astype(jnp.float32)
    hits = [jnp.where(column == lane + half * LANES, 1.0, 0.0) for half in range(2)]
    return jnp.concatenate(hits, axis=1).astype(jnp.bfloat16)


def place_kernel(count, owner, local, place, second, choose):
    shape = (4, LANES)
    slot = lax.broadcasted_iota(jnp.int32, shape, 0) * LANES + lax.broadcasted_iota(jnp.int32, shape, 1)
    orb, rank = slot // PAIR_DEV, slot % PAIR_DEV
    before, live = jnp.zeros(shape, jnp.int32), jnp.zeros(shape, jnp.int32)
    for e in range(N_ORB):
        before = before + jnp.where(orb > e, count[e], 0)
        live = jnp.where(orb == e, count[e], live)
    rank = jnp.where(rank < live, before + rank, -1).astype(jnp.float32)
    pair = lax.broadcasted_iota(jnp.int32, (N_DEV, LANES), 0).astype(jnp.float32)
    second[...] = (owner[...] * ORB_DEV + local[...]).astype(jnp.float32)
    for k in range(4):
        at = slice(k * LANES, (k + 1) * LANES)
        place[:, at] = jnp.where(pair == rank[k : k + 1], 1.0, 0.0).astype(jnp.bfloat16)
    rows = jnp.concatenate([second[k : k + 1, :] for k in range(4)], axis=1)
    rows = jnp.broadcast_to(rows, (LANES, 4 * LANES)).astype(jnp.bfloat16)
    choose[...] = chosen(dot_rows(place[...], rows))


def pick_kernel(me, place, second, choose, pieces, picked, index, mine, tall):
    blocks = []
    for k in range(4):
        block = jnp.sum(pieces[8 * k : 8 * k + 8, 8].astype(jnp.float32), axis=0)
        row = lax.broadcasted_iota(jnp.int32, (8, LANES), 0)
        lane = lax.broadcasted_iota(jnp.int32, (8, LANES), 1)
        orbital = (8 * (8 * k + lane // PAIR_DEV)).astype(jnp.float32)
        block = jnp.where(row == 0, block + orbital, block)
        blocks.append(jnp.where(row == 3, jnp.broadcast_to(second[k : k + 1, :], (8, LANES)), block))
    facts = jnp.concatenate(blocks, axis=1)
    first = jnp.broadcast_to(facts[0:1], (LANES, 4 * LANES)).astype(jnp.bfloat16)
    choose_first = chosen(dot_rows(place[...], first))
    known = dot_rows(facts.astype(jnp.bfloat16), place[...])
    index[0:1, :] = known[0:1].astype(jnp.int32)
    index[1:2, :] = known[3:4].astype(jnp.int32)
    lane = lax.broadcasted_iota(jnp.int32, (8, N_DEV), 1)
    here = jnp.sum(jnp.where(lane == me[0], known, 0.0), axis=1, keepdims=True)
    lane = lax.broadcasted_iota(jnp.int32, (1, LANES), 1)
    mine[...] = jnp.where(lane == 0, here[1:2], here[2:3]).astype(jnp.int32)
    for z in range(0, 8, 2):
        field = [
            pieces[:, z + k].astype(jnp.float32).reshape(N_DEV, LANES).astype(jnp.bfloat16) for k in range(2)
        ]
        field = jnp.concatenate(field, axis=1)
        for side, picker in enumerate((choose_first, choose[...])):
            out = jnp.dot(picker, field, preferred_element_type=jnp.float32)
            tall[pl.ds(8 * side + z, N_DEV, stride=16), :] = out[:, :LANES]
            tall[pl.ds(8 * side + z + 1, N_DEV, stride=16), :] = out[:, LANES:]
    for k in range(0, N_DEV, 8):
        picked[k : k + 8] = tall[16 * k : 16 * k + 128, :].reshape(8, 16, LANES).astype(jnp.bfloat16)


def shifted(tiles, start, count, flat, shift_x, shift_y):
    lane = lax.broadcasted_iota(jnp.int32, (8, LANES), 1)
    whole, rest = flat // LANES, flat % LANES
    later = (lane >= rest)[None]
    y = lane % BOX - shift_y
    keep_y = (y >= 0) & (y < BOX)
    turned = [
        pltpu.roll(tiles((start + k - whole - 1 + 2 * TILES) % TILES), rest, 2) for k in range(count + 1)
    ]
    out = []
    for k in range(count):
        x = 2 * (start + k) + lane // BOX - shift_x
        keep = jnp.where(keep_y & (x >= 0) & (x < BOX), 1.0, 0.0)
        out.append(jnp.where(later, turned[k + 1], turned[k]) * keep[None])
    return out


def solve_kernel(shift, right, left, screen, boxes, terms, moved, field, other):
    shift_x, shift_y = shift[0, 0], shift[0, 1]
    full = BOX * BOX
    ahead = (shift_x * BOX + shift_y + full) % full
    back = (full - ahead) % full
    early = lax.broadcasted_iota(jnp.int32, (8, LANES), 1) < BOX
    sign = jnp.where(early, 1.0, -1.0)

    def first_tile(tile):
        return boxes[pl.ds(tile * 8, 8), :8, :].astype(jnp.float32)

    def second_tile(tile):
        return boxes[pl.ds(tile * 8, 8), 8:, :].astype(jnp.float32)

    def along_y(block):
        high, low = split(block)
        product = jnp.dot(
            jnp.concatenate([high, low], axis=1), right[...], preferred_element_type=jnp.float32
        )
        return product[:, :LANES] + product[:, LANES:]

    for start in range(0, TILES, 4):
        products = []
        for k, box in enumerate(shifted(second_tile, start, 4, ahead, shift_x, shift_y)):
            moved[start + k] = box
            products.append(first_tile(start + k) * box)
        block = along_y(jnp.stack(products).reshape(4 * BOX, LANES)).reshape(4, BOX, LANES)
        for k in range(4):
            field[start + k] = block[k]

    for row in range(0, BOX, 8):
        parts = twist(fast_hartley([field[k, row : row + 8, :] for k in range(TILES)]), early)
        for k in range(TILES):
            field[k, row : row + 8, :] = sign * parts[k] + pltpu.roll(parts[k], BOX, 1)

    def along_z(block):
        high, low = split(block)
        return jnp.dot(
            left[...], jnp.concatenate([high, low, high], axis=0), preferred_element_type=jnp.float32
        )

    for tile in range(0, TILES, 2):
        block = along_z(jnp.concatenate([field[tile], field[tile + 1]], axis=1))
        block = block * jnp.concatenate([screen[tile], screen[tile + 1]], axis=1)
        block = along_z(block)
        field[tile] = block[:, :LANES]
        field[tile + 1] = block[:, LANES:]

    for row in range(0, BOX, 8):
        parts = [field[k, row : row + 8, :] for k in range(TILES)]
        parts = [sign * part + pltpu.roll(part, BOX, 1) for part in parts]
        parts = fast_hartley(untwist(parts, early))
        for k in range(TILES):
            field[k, row : row + 8, :] = parts[k]

    for start in range(0, TILES, 4):
        block = field[start : start + 4].reshape(4 * BOX, LANES)
        potential = along_y(block).reshape(4, 8, 8, LANES)
        for k in range(4):
            other[start + k] = potential[k] * first_tile(start + k)
            moved[start + k] = potential[k] * moved[start + k]

    for start in range(0, TILES, 4):
        carried = shifted(lambda tile: other[tile], start, 4, back, -shift_x, -shift_y)
        for k in range(4):
            both = jnp.concatenate([moved[start + k], carried[k]], axis=1)
            terms[(start + k) * 8 : (start + k + 1) * 8] = both.astype(jnp.bfloat16)


def sum_kernel(index, terms, pieces, tall, summed):
    for k in range(0, N_DEV, 8):
        tall[16 * k : 16 * k + 128, :] = terms[k : k + 8].astype(jnp.float32).reshape(128, LANES)
    orbital = lax.broadcasted_iota(jnp.int32, (N_DEV, N_DEV), 0)
    hits = [jnp.where(orbital == index[side : side + 1, :], 1.0, 0.0) for side in range(2)]
    hits = jnp.concatenate(hits, axis=1).astype(jnp.bfloat16)
    for z in range(0, 8, 2):
        field = [
            jnp.concatenate(
                [tall[pl.ds(8 * side + z + k, N_DEV, stride=16), :] for side in range(2)], axis=0
            ).astype(jnp.bfloat16)
            for k in range(2)
        ]
        out = jnp.dot(hits, jnp.concatenate(field, axis=1), preferred_element_type=jnp.float32)
        summed[pl.ds(z, N_DEV, stride=8), :] = out[:, :LANES]
        summed[pl.ds(z + 1, N_DEV, stride=8), :] = out[:, LANES:]
    for e in range(N_ORB):
        pieces[e] = summed[e * ORB_DEV * 8 : (e + 1) * ORB_DEV * 8, :].astype(jnp.bfloat16)


def join_kernel(pieces, result):
    for pair in range(ORB_DEV // 2):
        tiles = [pieces[tile, 16 * pair : 16 * pair + 16, :].astype(jnp.float32) for tile in range(TILES)]
        for side in range(2):
            rows = [tile[8 * side : 8 * side + 8] for tile in tiles]
            result[2 * pair + side] = jnp.concatenate(rows, axis=1).astype(jnp.bfloat16)


def body(orbitals, pair_first, second_owner, second_local, pair_shift, pair_count):
    f32, bf16, i32 = jnp.float32, jnp.bfloat16, jnp.int32
    shape = jax.ShapeDtypeStruct
    me = (lax.axis_index("orb") * 8 + lax.axis_index("slab")).reshape(1)
    rows = ORB_DEV * 8
    pair_shape = shape((N_DEV, 16, LANES), bf16)
    pieces = pl.pallas_call(
        spread_kernel, out_shape=shape((N_ORB, 9, ORB_DEV, LANES), bf16),
        in_specs=[WHOLE_H] * 3, out_specs=WHOLE_H,
        scratch_shapes=[
            pltpu.VMEM((GROUPS, ORB_DEV, 8, BOX * BOX // GROUPS), bf16),
            pltpu.VMEM((TILES * rows, LANES), f32),
            pltpu.VMEM((16, PAIR_DEV), i32),
            pltpu.VMEM((8, LANES), f32),
            pltpu.VMEM((N_ORB, 9, ORB_DEV, LANES), bf16),
            pltpu.SemaphoreType.DMA((GROUPS + 2,)),
            pltpu.SemaphoreType.DMA((GROUPS,)),
        ],
        compiler_params=pltpu.CompilerParams(vmem_limit_bytes=60 * 1024 * 1024), name="spread",
    )(pair_first.reshape(1, PAIR_DEV), pair_shift.T, orbitals)
    pieces = lax.all_to_all(pieces, "orb", split_axis=0, concat_axis=0, tiled=True)
    place, second, choose = pl.pallas_call(
        place_kernel,
        out_shape=(shape((N_DEV, 4 * LANES), bf16), shape((4, LANES), f32), shape((N_DEV, N_DEV), bf16)),
        in_specs=[WHOLE_S, WHOLE_V, WHOLE_V], out_specs=(WHOLE_V,) * 3,
        compiler_params=PARAMS, name="place",
    )(pair_count, second_owner.reshape(4, LANES), second_local.reshape(4, LANES))
    picked, index, mine = pl.pallas_call(
        pick_kernel,
        out_shape=(pair_shape, shape((2, N_DEV), i32), shape((1, LANES), i32)),
        in_specs=[WHOLE_S] + [WHOLE_V] * 4,
        out_specs=(WHOLE_V,) * 3,
        scratch_shapes=[pltpu.VMEM((N_DEV * 16, LANES), f32)],
        compiler_params=PARAMS, name="pick",
    )(me, place, second, choose, pieces)
    boxes = lax.all_to_all(picked, ("orb", "slab"), split_axis=0, concat_axis=0, tiled=True)
    right, left, screen = (jnp.asarray(table) for table in tables())
    terms = pl.pallas_call(
        solve_kernel, out_shape=pair_shape,
        in_specs=[WHOLE_S] + [WHOLE_V] * 4,
        out_specs=WHOLE_V,
        scratch_shapes=[
            pltpu.VMEM((TILES, 8, 8, LANES), f32),
            pltpu.VMEM((TILES, BOX, LANES), f32),
            pltpu.VMEM((TILES, 8, 8, LANES), f32),
        ],
        compiler_params=PARAMS, name="solve",
    )(mine, right, left, screen, boxes)
    terms = lax.all_to_all(terms, ("orb", "slab"), split_axis=0, concat_axis=0, tiled=True)
    pieces = pl.pallas_call(
        sum_kernel, out_shape=shape((N_ORB, rows, LANES), bf16),
        in_specs=[WHOLE_V, WHOLE_V], out_specs=WHOLE_V,
        scratch_shapes=[pltpu.VMEM((N_DEV * 16, LANES), f32), pltpu.VMEM((N_DEV * 8, LANES), f32)],
        compiler_params=PARAMS, name="sum",
    )(index, terms)
    pieces = lax.all_to_all(pieces, "orb", split_axis=0, concat_axis=0, tiled=True)
    return pl.pallas_call(
        join_kernel, out_shape=shape((ORB_DEV, 8, BOX * BOX), bf16),
        in_specs=[WHOLE_V], out_specs=WHOLE_V,
        compiler_params=PARAMS, name="join",
    )(pieces)


def solution(mesh):
    in_specs = (P("orb", "slab", None), P("orb"), P(), P(), P("orb", None), P())
    out_specs = P("orb", "slab", None)
    return jax.shard_map(body, mesh=mesh, in_specs=in_specs, out_specs=out_specs, check_vma=False)
```

```python
import math

import jax
import jax.numpy as jnp
import numpy as np
from jax import lax
from jax.experimental import pallas as pl
from jax.experimental.pallas import tpu as pltpu
from jax.sharding import PartitionSpec as P

BOX = 64
ORB_DEV = 8
PAIR_DEV = 16
N_ORB = 32
N_DEV = 256
TILES = 32
LANES = 128
SCREENING = 0.02
GROUPS = 4
PARAMS = pltpu.CompilerParams(vmem_limit_bytes=48 * 1024 * 1024)
WHOLE_V = pl.BlockSpec(memory_space=pltpu.VMEM)
WHOLE_H = pl.BlockSpec(memory_space=pltpu.HBM)
WHOLE_S = pl.BlockSpec(memory_space=pltpu.SMEM)


def hartley_table():
    line = np.arange(BOX)
    angle = (line[:, None] * line[None, :] % BOX) * (2.0 * math.pi / BOX)
    return np.cos(angle) + np.sin(angle)


def halves(table):
    high = table.astype(np.float32).astype(jnp.bfloat16)
    low = (table - high.astype(np.float64)).astype(np.float32).astype(jnp.bfloat16)
    return high, low


def tables():
    high, low = halves(hartley_table())
    zero = np.zeros((BOX, BOX), high.dtype)

    def twice(table):
        return np.block([[table, zero], [zero, table]])

    right = np.block([[twice(high), twice(low)], [twice(high), np.zeros((128, 128), high.dtype)]])
    left = np.concatenate([high, high, low], axis=1)
    lam = 2.0 - 2.0 * np.cos(np.arange(BOX) * (2.0 * math.pi / BOX))
    lam_a = np.repeat(lam.reshape(2, TILES).T, BOX, axis=1)
    under = lam_a[:, None, :] + lam[None, :, None] + np.tile(lam, 2)[None, None, :] + SCREENING
    return right, left, (1.0 / BOX**3 / under).astype(np.float32)


def split(field):
    high = field.astype(jnp.bfloat16)
    low = (field - high.astype(jnp.float32)).astype(jnp.bfloat16)
    return high, low


def fast_hartley(parts):
    n = len(parts)
    if n == 1:
        return parts
    if n == 2:
        return [parts[0] + parts[1], parts[0] - parts[1]]
    even, odd = fast_hartley(parts[0::2]), fast_hartley(parts[1::2])
    m = n // 2
    out = [None] * n
    for k in range(m):
        if k == 0 or 4 * k == n:
            turned = odd[k]
        else:
            angle = 2.0 * math.pi * k / n
            turned = odd[k] * math.cos(angle) + odd[m - k] * math.sin(angle)
        out[k] = even[k] + turned
        out[k + m] = even[k] - turned
    return out


def twist(parts, first):
    out = []
    for k in range(TILES):
        mirror = parts[(TILES - k) % TILES]
        angle = 2.0 * math.pi * k / BOX
        if k == 0 or 2 * k == TILES:
            out.append(parts[k])
        else:
            out.append(jnp.where(first, parts[k], parts[k] * math.cos(angle) + mirror * math.sin(angle)))
    return out


def untwist(parts, first):
    out = []
    for k in range(TILES):
        mirror = parts[(TILES - k) % TILES]
        angle = 2.0 * math.pi * k / BOX
        back = 2.0 * math.pi * ((TILES - k) % TILES) / BOX
        if k == 0 or 2 * k == TILES:
            out.append(parts[k])
        else:
            out.append(jnp.where(first, parts[k], parts[k] * math.cos(angle) + mirror * math.sin(back)))
    return out


def spread_kernel(first, shift, orbitals, pieces, taken, tall, small, about, packed, arrived, sent):
    few = [
        pltpu.make_async_copy(first, small.at[0:1], arrived.at[GROUPS]),
        pltpu.make_async_copy(shift, small.at[8:10], arrived.at[GROUPS + 1]),
    ]
    width = BOX * BOX // GROUPS
    many = [
        pltpu.make_async_copy(orbitals.at[:, :, pl.ds(k * width, width)], taken.at[k], arrived.at[k])
        for k in range(GROUPS)
    ]
    for copy in few + many:
        copy.start()
    about[...] = jnp.zeros_like(about)
    for copy in few:
        copy.wait()
    about[0:1, :PAIR_DEV] = small[0:1, :].astype(jnp.float32)
    about[1:3, :PAIR_DEV] = small[8:10, :].astype(jnp.float32)
    placed = pltpu.roll(about[...], lax.axis_index("orb") % 8 * PAIR_DEV, 1).astype(jnp.bfloat16)
    inside = TILES // GROUPS
    out = []
    for k in range(GROUPS):
        many[k].wait()
        for orbital in range(ORB_DEV):
            box = taken[k, orbital].astype(jnp.float32)
            for tile in range(inside):
                row = (k * inside + tile) * ORB_DEV * 8 + 8 * orbital
                tall[row : row + 8, :] = box[:, tile * LANES : (tile + 1) * LANES]
        for tile in range(k * inside, (k + 1) * inside):
            for z in range(8):
                row = tile * ORB_DEV * 8 + z
                packed[tile, z] = tall[pl.ds(row, ORB_DEV, stride=8), :].astype(jnp.bfloat16)
            packed[tile, 8] = placed
        at = pl.ds(k * inside, inside)
        out.append(pltpu.make_async_copy(packed.at[at], pieces.at[at], sent.at[k]))
        out[k].start()
    for copy in out:
        copy.wait()


def dot_rows(one, two):
    return lax.dot_general(one, two, (((1,), (1,)), ((), ())), preferred_element_type=jnp.float32)


def chosen(column):
    lane = lax.broadcasted_iota(jnp.int32, (N_DEV, LANES), 1).astype(jnp.float32)
    hits = [jnp.where(column == lane + half * LANES, 1.0, 0.0) for half in range(2)]
    return jnp.concatenate(hits, axis=1).astype(jnp.bfloat16)


def place_kernel(count, owner, local, place, second, choose):
    shape = (4, LANES)
    slot = lax.broadcasted_iota(jnp.int32, shape, 0) * LANES + lax.broadcasted_iota(jnp.int32, shape, 1)
    orb, rank = slot // PAIR_DEV, slot % PAIR_DEV
    before, live = jnp.zeros(shape, jnp.int32), jnp.zeros(shape, jnp.int32)
    for e in range(N_ORB):
        before = before + jnp.where(orb > e, count[e], 0)
        live = jnp.where(orb == e, count[e], live)
    rank = jnp.where(rank < live, before + rank, -1).astype(jnp.float32)
    pair = lax.broadcasted_iota(jnp.int32, (N_DEV, LANES), 0).astype(jnp.float32)
    second[...] = (owner[...] * ORB_DEV + local[...]).astype(jnp.float32)
    for k in range(4):
        at = slice(k * LANES, (k + 1) * LANES)
        place[:, at] = jnp.where(pair == rank[k : k + 1], 1.0, 0.0).astype(jnp.bfloat16)
    rows = jnp.concatenate([second[k : k + 1, :] for k in range(4)], axis=1)
    rows = jnp.broadcast_to(rows, (LANES, 4 * LANES)).astype(jnp.bfloat16)
    choose[...] = chosen(dot_rows(place[...], rows))


def pick_kernel(me, place, second, choose, pieces, picked, index, mine, tall):
    blocks = []
    for k in range(4):
        block = jnp.sum(pieces[8 * k : 8 * k + 8, 8].astype(jnp.float32), axis=0)
        row = lax.broadcasted_iota(jnp.int32, (8, LANES), 0)
        lane = lax.broadcasted_iota(jnp.int32, (8, LANES), 1)
        orbital = (8 * (8 * k + lane // PAIR_DEV)).astype(jnp.float32)
        block = jnp.where(row == 0, block + orbital, block)
        blocks.append(jnp.where(row == 3, jnp.broadcast_to(second[k : k + 1, :], (8, LANES)), block))
    facts = jnp.concatenate(blocks, axis=1)
    first = jnp.broadcast_to(facts[0:1], (LANES, 4 * LANES)).astype(jnp.bfloat16)
    choose_first = chosen(dot_rows(place[...], first))
    known = dot_rows(facts.astype(jnp.bfloat16), place[...])
    index[0:1, :] = known[0:1].astype(jnp.int32)
    index[1:2, :] = known[3:4].astype(jnp.int32)
    lane = lax.broadcasted_iota(jnp.int32, (8, N_DEV), 1)
    here = jnp.sum(jnp.where(lane == me[0], known, 0.0), axis=1, keepdims=True)
    lane = lax.broadcasted_iota(jnp.int32, (1, LANES), 1)
    mine[...] = jnp.where(lane == 0, here[1:2], here[2:3]).astype(jnp.int32)
    for z in range(0, 8, 2):
        field = [
            pieces[:, z + k].astype(jnp.float32).reshape(N_DEV, LANES).astype(jnp.bfloat16) for k in range(2)
        ]
        field = jnp.concatenate(field, axis=1)
        for side, picker in enumerate((choose_first, choose[...])):
            out = jnp.dot(picker, field, preferred_element_type=jnp.float32)
            tall[pl.ds(8 * side + z, N_DEV, stride=16), :] = out[:, :LANES]
            tall[pl.ds(8 * side + z + 1, N_DEV, stride=16), :] = out[:, LANES:]
    for k in range(0, N_DEV, 8):
        picked[k : k + 8] = tall[16 * k : 16 * k + 128, :].reshape(8, 16, LANES).astype(jnp.bfloat16)


def shifted(tiles, start, count, flat, shift_x, shift_y):
    lane = lax.broadcasted_iota(jnp.int32, (8, LANES), 1)
    whole, rest = flat // LANES, flat % LANES
    later = (lane >= rest)[None]
    y = lane % BOX - shift_y
    keep_y = (y >= 0) & (y < BOX)
    turned = [
        pltpu.roll(tiles((start + k - whole - 1 + 2 * TILES) % TILES), rest, 2) for k in range(count + 1)
    ]
    out = []
    for k in range(count):
        x = 2 * (start + k) + lane // BOX - shift_x
        keep = jnp.where(keep_y & (x >= 0) & (x < BOX), 1.0, 0.0)
        out.append(jnp.where(later, turned[k + 1], turned[k]) * keep[None])
    return out


def solve_kernel(shift, right, left, screen, boxes, terms, moved, field, other):
    shift_x, shift_y = shift[0, 0], shift[0, 1]
    full = BOX * BOX
    ahead = (shift_x * BOX + shift_y + full) % full
    back = (full - ahead) % full
    early = lax.broadcasted_iota(jnp.int32, (8, LANES), 1) < BOX
    sign = jnp.where(early, 1.0, -1.0)

    def first_tile(tile):
        return boxes[:, tile, :8, :].astype(jnp.float32)

    def second_tile(tile):
        return boxes[:, tile, 8:, :].astype(jnp.float32)

    def along_y(block):
        high, low = split(block)
        product = jnp.dot(
            jnp.concatenate([high, low], axis=1), right[...], preferred_element_type=jnp.float32
        )
        return product[:, :LANES] + product[:, LANES:]

    for start in range(0, TILES, 4):
        products = []
        for k, box in enumerate(shifted(second_tile, start, 4, ahead, shift_x, shift_y)):
            moved[start + k] = box
            products.append(first_tile(start + k) * box)
        block = along_y(jnp.stack(products).reshape(4 * BOX, LANES)).reshape(4, BOX, LANES)
        for k in range(4):
            field[start + k] = block[k]

    for row in range(0, BOX, 8):
        parts = twist(fast_hartley([field[k, row : row + 8, :] for k in range(TILES)]), early)
        for k in range(TILES):
            field[k, row : row + 8, :] = sign * parts[k] + pltpu.roll(parts[k], BOX, 1)

    def along_z(block):
        high, low = split(block)
        return jnp.dot(
            left[...], jnp.concatenate([high, low, high], axis=0), preferred_element_type=jnp.float32
        )

    for tile in range(0, TILES, 2):
        block = along_z(jnp.concatenate([field[tile], field[tile + 1]], axis=1))
        block = block * jnp.concatenate([screen[tile], screen[tile + 1]], axis=1)
        block = along_z(block)
        field[tile] = block[:, :LANES]
        field[tile + 1] = block[:, LANES:]

    for row in range(0, BOX, 8):
        parts = [field[k, row : row + 8, :] for k in range(TILES)]
        parts = [sign * part + pltpu.roll(part, BOX, 1) for part in parts]
        parts = fast_hartley(untwist(parts, early))
        for k in range(TILES):
            field[k, row : row + 8, :] = parts[k]

    for start in range(0, TILES, 4):
        block = field[start : start + 4].reshape(4 * BOX, LANES)
        potential = along_y(block).reshape(4, 8, 8, LANES)
        for k in range(4):
            other[start + k] = potential[k] * first_tile(start + k)
            moved[start + k] = potential[k] * moved[start + k]

    for start in range(0, TILES, 4):
        carried = shifted(lambda tile: other[tile], start, 4, back, -shift_x, -shift_y)
        for k in range(4):
            both = jnp.concatenate([moved[start + k], carried[k]], axis=1)
            terms[:, start + k] = both.astype(jnp.bfloat16)


def sum_kernel(index, terms, pieces, tall, summed):
    for k in range(0, N_DEV, 8):
        tall[16 * k : 16 * k + 128, :] = terms[k : k + 8].astype(jnp.float32).reshape(128, LANES)
    orbital = lax.broadcasted_iota(jnp.int32, (N_DEV, N_DEV), 0)
    hits = [jnp.where(orbital == index[side : side + 1, :], 1.0, 0.0) for side in range(2)]
    hits = jnp.concatenate(hits, axis=1).astype(jnp.bfloat16)
    for z in range(0, 8, 2):
        field = [
            jnp.concatenate(
                [tall[pl.ds(8 * side + z + k, N_DEV, stride=16), :] for side in range(2)], axis=0
            ).astype(jnp.bfloat16)
            for k in range(2)
        ]
        out = jnp.dot(hits, jnp.concatenate(field, axis=1), preferred_element_type=jnp.float32)
        summed[pl.ds(z, N_DEV, stride=8), :] = out[:, :LANES]
        summed[pl.ds(z + 1, N_DEV, stride=8), :] = out[:, LANES:]
    for e in range(N_ORB):
        pieces[e] = summed[e * ORB_DEV * 8 : (e + 1) * ORB_DEV * 8, :].astype(jnp.bfloat16)


def join_kernel(pieces, result):
    for pair in range(ORB_DEV // 2):
        tiles = [pieces[tile, 16 * pair : 16 * pair + 16, :].astype(jnp.float32) for tile in range(TILES)]
        for side in range(2):
            rows = [tile[8 * side : 8 * side + 8] for tile in tiles]
            result[2 * pair + side] = jnp.concatenate(rows, axis=1).astype(jnp.bfloat16)


def body(orbitals, pair_first, second_owner, second_local, pair_shift, pair_count):
    f32, bf16, i32 = jnp.float32, jnp.bfloat16, jnp.int32
    shape = jax.ShapeDtypeStruct
    me = (lax.axis_index("slab") * N_ORB + lax.axis_index("orb")).reshape(1)
    rows = ORB_DEV * 8
    pair_shape = shape((N_DEV, 16, LANES), bf16)
    pieces = pl.pallas_call(
        spread_kernel, out_shape=shape((N_ORB, 9, ORB_DEV, LANES), bf16),
        in_specs=[WHOLE_H] * 3, out_specs=WHOLE_H,
        scratch_shapes=[
            pltpu.VMEM((GROUPS, ORB_DEV, 8, BOX * BOX // GROUPS), bf16),
            pltpu.VMEM((TILES * rows, LANES), f32),
            pltpu.VMEM((16, PAIR_DEV), i32),
            pltpu.VMEM((8, LANES), f32),
            pltpu.VMEM((N_ORB, 9, ORB_DEV, LANES), bf16),
            pltpu.SemaphoreType.DMA((GROUPS + 2,)),
            pltpu.SemaphoreType.DMA((GROUPS,)),
        ],
        compiler_params=pltpu.CompilerParams(vmem_limit_bytes=60 * 1024 * 1024), name="spread",
    )(pair_first.reshape(1, PAIR_DEV), pair_shift.T, orbitals)
    pieces = lax.all_to_all(pieces, "orb", split_axis=0, concat_axis=0, tiled=True)
    place, second, choose = pl.pallas_call(
        place_kernel,
        out_shape=(shape((N_DEV, 4 * LANES), bf16), shape((4, LANES), f32), shape((N_DEV, N_DEV), bf16)),
        in_specs=[WHOLE_S, WHOLE_V, WHOLE_V], out_specs=(WHOLE_V,) * 3,
        compiler_params=PARAMS, name="place",
    )(pair_count, second_owner.reshape(4, LANES), second_local.reshape(4, LANES))
    picked, index, mine = pl.pallas_call(
        pick_kernel,
        out_shape=(pair_shape, shape((2, N_DEV), i32), shape((1, LANES), i32)),
        in_specs=[WHOLE_S] + [WHOLE_V] * 4,
        out_specs=(WHOLE_V,) * 3,
        scratch_shapes=[pltpu.VMEM((N_DEV * 16, LANES), f32)],
        compiler_params=PARAMS, name="pick",
    )(me, place, second, choose, pieces)
    boxes = lax.all_to_all(picked, ("slab", "orb"), split_axis=0, concat_axis=0, tiled=True)
    right, left, screen = (jnp.asarray(table) for table in tables())
    terms = pl.pallas_call(
        solve_kernel, out_shape=shape((8, TILES, 16, LANES), bf16),
        in_specs=[WHOLE_S] + [WHOLE_V] * 4,
        out_specs=WHOLE_V,
        scratch_shapes=[
            pltpu.VMEM((TILES, 8, 8, LANES), f32),
            pltpu.VMEM((TILES, BOX, LANES), f32),
            pltpu.VMEM((TILES, 8, 8, LANES), f32),
        ],
        compiler_params=PARAMS, name="solve",
    )(mine, right, left, screen, boxes.reshape(8, TILES, 16, LANES))
    terms = terms.reshape(N_DEV, 16, LANES)
    terms = lax.all_to_all(terms, ("slab", "orb"), split_axis=0, concat_axis=0, tiled=True)
    pieces = pl.pallas_call(
        sum_kernel, out_shape=shape((N_ORB, rows, LANES), bf16),
        in_specs=[WHOLE_V, WHOLE_V], out_specs=WHOLE_V,
        scratch_shapes=[pltpu.VMEM((N_DEV * 16, LANES), f32), pltpu.VMEM((N_DEV * 8, LANES), f32)],
        compiler_params=PARAMS, name="sum",
    )(index, terms)
    pieces = lax.all_to_all(pieces, "orb", split_axis=0, concat_axis=0, tiled=True)
    return pl.pallas_call(
        join_kernel, out_shape=shape((ORB_DEV, 8, BOX * BOX), bf16),
        in_specs=[WHOLE_V], out_specs=WHOLE_V,
        compiler_params=PARAMS, name="join",
    )(pieces)


def solution(mesh):
    in_specs = (P("orb", "slab", None), P("orb"), P(), P(), P("orb", None), P())
    out_specs = P("orb", "slab", None)
    return jax.shard_map(body, mesh=mesh, in_specs=in_specs, out_specs=out_specs, check_vma=False)
```

```python
import math

import jax
import jax.numpy as jnp
import numpy as np
from jax import lax
from jax.experimental import pallas as pl
from jax.experimental.pallas import tpu as pltpu
from jax.sharding import PartitionSpec as P

BOX = 64
ORB_DEV = 8
PAIR_DEV = 16
N_ORB = 32
N_DEV = 256
TILES = 32
LANES = 128
SCREENING = 0.02
GROUPS = 8
PARAMS = pltpu.CompilerParams(vmem_limit_bytes=48 * 1024 * 1024)
WHOLE_V = pl.BlockSpec(memory_space=pltpu.VMEM)
WHOLE_H = pl.BlockSpec(memory_space=pltpu.HBM)
WHOLE_S = pl.BlockSpec(memory_space=pltpu.SMEM)


def hartley_table():
    line = np.arange(BOX)
    angle = (line[:, None] * line[None, :] % BOX) * (2.0 * math.pi / BOX)
    return np.cos(angle) + np.sin(angle)


def halves(table):
    high = table.astype(np.float32).astype(jnp.bfloat16)
    low = (table - high.astype(np.float64)).astype(np.float32).astype(jnp.bfloat16)
    return high, low


def tables():
    high, low = halves(hartley_table())
    zero = np.zeros((BOX, BOX), high.dtype)

    def twice(table):
        return np.block([[table, zero], [zero, table]])

    right = np.block([[twice(high), twice(low)], [twice(high), np.zeros((128, 128), high.dtype)]])
    left = np.concatenate([high, high, low], axis=1)
    lam = 2.0 - 2.0 * np.cos(np.arange(BOX) * (2.0 * math.pi / BOX))
    lam_a = np.repeat(lam.reshape(2, TILES).T, BOX, axis=1)
    under = lam_a[:, None, :] + lam[None, :, None] + np.tile(lam, 2)[None, None, :] + SCREENING
    return right, left, (1.0 / BOX**3 / under).astype(np.float32)


def split(field):
    high = field.astype(jnp.bfloat16)
    low = (field - high.astype(jnp.float32)).astype(jnp.bfloat16)
    return high, low


def fast_hartley(parts):
    n = len(parts)
    if n == 1:
        return parts
    if n == 2:
        return [parts[0] + parts[1], parts[0] - parts[1]]
    even, odd = fast_hartley(parts[0::2]), fast_hartley(parts[1::2])
    m = n // 2
    out = [None] * n
    for k in range(m):
        if k == 0 or 4 * k == n:
            turned = odd[k]
        else:
            angle = 2.0 * math.pi * k / n
            turned = odd[k] * math.cos(angle) + odd[m - k] * math.sin(angle)
        out[k] = even[k] + turned
        out[k + m] = even[k] - turned
    return out


def twist(parts, first):
    out = []
    for k in range(TILES):
        mirror = parts[(TILES - k) % TILES]
        angle = 2.0 * math.pi * k / BOX
        if k == 0 or 2 * k == TILES:
            out.append(parts[k])
        else:
            out.append(jnp.where(first, parts[k], parts[k] * math.cos(angle) + mirror * math.sin(angle)))
    return out


def untwist(parts, first):
    out = []
    for k in range(TILES):
        mirror = parts[(TILES - k) % TILES]
        angle = 2.0 * math.pi * k / BOX
        back = 2.0 * math.pi * ((TILES - k) % TILES) / BOX
        if k == 0 or 2 * k == TILES:
            out.append(parts[k])
        else:
            out.append(jnp.where(first, parts[k], parts[k] * math.cos(angle) + mirror * math.sin(back)))
    return out


def spread_kernel(first, shift, orbitals, pieces, taken, tall, small, about, packed, arrived, sent):
    few = [
        pltpu.make_async_copy(first, small.at[0:1], arrived.at[GROUPS]),
        pltpu.make_async_copy(shift, small.at[8:10], arrived.at[GROUPS + 1]),
    ]
    width = BOX * BOX // GROUPS
    many = [
        pltpu.make_async_copy(orbitals.at[:, :, pl.ds(k * width, width)], taken.at[k], arrived.at[k])
        for k in range(GROUPS)
    ]
    for copy in few + many:
        copy.start()
    about[...] = jnp.zeros_like(about)
    for copy in few:
        copy.wait()
    about[0:1, :PAIR_DEV] = small[0:1, :].astype(jnp.float32)
    about[1:3, :PAIR_DEV] = small[8:10, :].astype(jnp.float32)
    placed = pltpu.roll(about[...], lax.axis_index("orb") % 8 * PAIR_DEV, 1).astype(jnp.bfloat16)
    inside = TILES // GROUPS
    out = []
    for k in range(GROUPS):
        many[k].wait()
        for orbital in range(ORB_DEV):
            box = taken[k, orbital].astype(jnp.float32)
            for tile in range(inside):
                row = (k * inside + tile) * ORB_DEV * 8 + 8 * orbital
                tall[row : row + 8, :] = box[:, tile * LANES : (tile + 1) * LANES]
        for tile in range(k * inside, (k + 1) * inside):
            for z in range(8):
                row = tile * ORB_DEV * 8 + z
                packed[tile, z] = tall[pl.ds(row, ORB_DEV, stride=8), :].astype(jnp.bfloat16)
            packed[tile, 8] = placed
        at = pl.ds(k * inside, inside)
        out.append(pltpu.make_async_copy(packed.at[at], pieces.at[at], sent.at[k]))
        out[k].start()
    for copy in out:
        copy.wait()


def dot_rows(one, two):
    return lax.dot_general(one, two, (((1,), (1,)), ((), ())), preferred_element_type=jnp.float32)


def chosen(column):
    lane = lax.broadcasted_iota(jnp.int32, (N_DEV, LANES), 1).astype(jnp.float32)
    hits = [jnp.where(column == lane + half * LANES, 1.0, 0.0) for half in range(2)]
    return jnp.concatenate(hits, axis=1).astype(jnp.bfloat16)


def place_kernel(count, owner, local, place, second, choose):
    shape = (4, LANES)
    slot = lax.broadcasted_iota(jnp.int32, shape, 0) * LANES + lax.broadcasted_iota(jnp.int32, shape, 1)
    orb, rank = slot // PAIR_DEV, slot % PAIR_DEV
    before, live = jnp.zeros(shape, jnp.int32), jnp.zeros(shape, jnp.int32)
    for e in range(N_ORB):
        before = before + jnp.where(orb > e, count[e], 0)
        live = jnp.where(orb == e, count[e], live)
    rank = jnp.where(rank < live, before + rank, -1).astype(jnp.float32)
    pair = lax.broadcasted_iota(jnp.int32, (N_DEV, LANES), 0).astype(jnp.float32)
    second[...] = (owner[...] * ORB_DEV + local[...]).astype(jnp.float32)
    for k in range(4):
        at = slice(k * LANES, (k + 1) * LANES)
        place[:, at] = jnp.where(pair == rank[k : k + 1], 1.0, 0.0).astype(jnp.bfloat16)
    rows = jnp.concatenate([second[k : k + 1, :] for k in range(4)], axis=1)
    rows = jnp.broadcast_to(rows, (LANES, 4 * LANES)).astype(jnp.bfloat16)
    choose[...] = chosen(dot_rows(place[...], rows))


def pick_kernel(me, place, second, choose, pieces, picked, index, mine, tall):
    blocks = []
    for k in range(4):
        block = jnp.sum(pieces[8 * k : 8 * k + 8, 8].astype(jnp.float32), axis=0)
        row = lax.broadcasted_iota(jnp.int32, (8, LANES), 0)
        lane = lax.broadcasted_iota(jnp.int32, (8, LANES), 1)
        orbital = (8 * (8 * k + lane // PAIR_DEV)).astype(jnp.float32)
        block = jnp.where(row == 0, block + orbital, block)
        blocks.append(jnp.where(row == 3, jnp.broadcast_to(second[k : k + 1, :], (8, LANES)), block))
    facts = jnp.concatenate(blocks, axis=1)
    first = jnp.broadcast_to(facts[0:1], (LANES, 4 * LANES)).astype(jnp.bfloat16)
    choose_first = chosen(dot_rows(place[...], first))
    known = dot_rows(facts.astype(jnp.bfloat16), place[...])
    index[0:1, :] = known[0:1].astype(jnp.int32)
    index[1:2, :] = known[3:4].astype(jnp.int32)
    lane = lax.broadcasted_iota(jnp.int32, (8, N_DEV), 1)
    here = jnp.sum(jnp.where(lane == me[0], known, 0.0), axis=1, keepdims=True)
    lane = lax.broadcasted_iota(jnp.int32, (1, LANES), 1)
    mine[...] = jnp.where(lane == 0, here[1:2], here[2:3]).astype(jnp.int32)
    for z in range(0, 8, 2):
        field = [
            pieces[:, z + k].astype(jnp.float32).reshape(N_DEV, LANES).astype(jnp.bfloat16) for k in range(2)
        ]
        field = jnp.concatenate(field, axis=1)
        for side, picker in enumerate((choose_first, choose[...])):
            out = jnp.dot(picker, field, preferred_element_type=jnp.float32)
            tall[pl.ds(8 * side + z, N_DEV, stride=16), :] = out[:, :LANES]
            tall[pl.ds(8 * side + z + 1, N_DEV, stride=16), :] = out[:, LANES:]
    for k in range(0, N_DEV, 8):
        picked[k : k + 8] = tall[16 * k : 16 * k + 128, :].reshape(8, 16, LANES).astype(jnp.bfloat16)


def shifted(tiles, start, count, flat, shift_x, shift_y, held):
    lane = lax.broadcasted_iota(jnp.int32, (8, LANES), 1)
    whole, rest = flat // LANES, flat % LANES
    later = (lane >= rest)[None]
    y = lane % BOX - shift_y
    keep_y = (y >= 0) & (y < BOX)
    turned = [
        pltpu.roll(tiles((start + k - whole - 1 + 2 * TILES) % TILES), rest, 2)
        for k in range(0 if held is None else 1, count + 1)
    ]
    turned = turned if held is None else [held] + turned
    out = []
    for k in range(count):
        x = 2 * (start + k) + lane // BOX - shift_x
        keep = jnp.where(keep_y & (x >= 0) & (x < BOX), 1.0, 0.0)
        out.append(jnp.where(later, turned[k + 1], turned[k]) * keep[None])
    return out, turned[count]


def solve_kernel(shift, right, left, screen, boxes, terms, moved, field, other):
    shift_x, shift_y = shift[0, 0], shift[0, 1]
    full = BOX * BOX
    ahead = (shift_x * BOX + shift_y + full) % full
    back = (full - ahead) % full
    early = lax.broadcasted_iota(jnp.int32, (8, LANES), 1) < BOX
    sign = jnp.where(early, 1.0, -1.0)

    def first_tile(tile):
        return boxes[pl.ds(tile * 8, 8), :8, :].astype(jnp.float32)

    def second_tile(tile):
        return boxes[pl.ds(tile * 8, 8), 8:, :].astype(jnp.float32)

    def along_y(block):
        high, low = split(block)
        product = jnp.dot(
            jnp.concatenate([high, low], axis=1), right[...], preferred_element_type=jnp.float32
        )
        return product[:, :LANES] + product[:, LANES:]

    held = None
    for start in range(0, TILES, 4):
        products = []
        found, held = shifted(second_tile, start, 4, ahead, shift_x, shift_y, held)
        for k, box in enumerate(found):
            moved[start + k] = box
            products.append(first_tile(start + k) * box)
        block = along_y(jnp.stack(products).reshape(4 * BOX, LANES)).reshape(4, BOX, LANES)
        for k in range(4):
            field[start + k] = block[k]

    for row in range(0, BOX, 8):
        parts = twist(fast_hartley([field[k, row : row + 8, :] for k in range(TILES)]), early)
        for k in range(TILES):
            field[k, row : row + 8, :] = sign * parts[k] + pltpu.roll(parts[k], BOX, 1)

    def along_z(block):
        high, low = split(block)
        return jnp.dot(
            left[...], jnp.concatenate([high, low, high], axis=0), preferred_element_type=jnp.float32
        )

    for tile in range(0, TILES, 2):
        block = along_z(jnp.concatenate([field[tile], field[tile + 1]], axis=1))
        block = block * jnp.concatenate([screen[tile], screen[tile + 1]], axis=1)
        block = along_z(block)
        field[tile] = block[:, :LANES]
        field[tile + 1] = block[:, LANES:]

    for row in range(0, BOX, 8):
        parts = [field[k, row : row + 8, :] for k in range(TILES)]
        parts = [sign * part + pltpu.roll(part, BOX, 1) for part in parts]
        parts = fast_hartley(untwist(parts, early))
        for k in range(TILES):
            field[k, row : row + 8, :] = parts[k]

    for start in range(0, TILES, 4):
        block = field[start : start + 4].reshape(4 * BOX, LANES)
        potential = along_y(block).reshape(4, 8, 8, LANES)
        for k in range(4):
            other[start + k] = potential[k] * first_tile(start + k)
            moved[start + k] = potential[k] * moved[start + k]

    held = None
    for start in range(0, TILES, 4):
        carried, held = shifted(lambda tile: other[tile], start, 4, back, -shift_x, -shift_y, held)
        for k in range(4):
            both = jnp.concatenate([moved[start + k], carried[k]], axis=1)
            terms[(start + k) * 8 : (start + k + 1) * 8] = both.astype(jnp.bfloat16)


def sum_kernel(index, terms, pieces, tall, summed):
    for k in range(0, N_DEV, 8):
        tall[16 * k : 16 * k + 128, :] = terms[k : k + 8].astype(jnp.float32).reshape(128, LANES)
    orbital = lax.broadcasted_iota(jnp.int32, (N_DEV, N_DEV), 0)
    hits = [jnp.where(orbital == index[side : side + 1, :], 1.0, 0.0) for side in range(2)]
    hits = jnp.concatenate(hits, axis=1).astype(jnp.bfloat16)
    for z in range(0, 8, 2):
        field = [
            jnp.concatenate(
                [tall[pl.ds(8 * side + z + k, N_DEV, stride=16), :] for side in range(2)], axis=0
            ).astype(jnp.bfloat16)
            for k in range(2)
        ]
        out = jnp.dot(hits, jnp.concatenate(field, axis=1), preferred_element_type=jnp.float32)
        summed[pl.ds(z, N_DEV, stride=8), :] = out[:, :LANES]
        summed[pl.ds(z + 1, N_DEV, stride=8), :] = out[:, LANES:]
    for e in range(N_ORB):
        pieces[e] = summed[e * ORB_DEV * 8 : (e + 1) * ORB_DEV * 8, :].astype(jnp.bfloat16)


def join_kernel(pieces, result):
    rows = pl.ds(pl.multiple_of(pl.program_id(0) * 16, 16), 16)
    tiles = [pieces[tile, rows, :].astype(jnp.float32) for tile in range(TILES)]
    for side in range(2):
        box = [tile[8 * side : 8 * side + 8] for tile in tiles]
        result[side] = jnp.concatenate(box, axis=1).astype(jnp.bfloat16)


def body(orbitals, pair_first, second_owner, second_local, pair_shift, pair_count):
    f32, bf16, i32 = jnp.float32, jnp.bfloat16, jnp.int32
    shape = jax.ShapeDtypeStruct
    me = (lax.axis_index("orb") * 8 + lax.axis_index("slab")).reshape(1)
    rows = ORB_DEV * 8
    pair_shape = shape((N_DEV, 16, LANES), bf16)
    pieces = pl.pallas_call(
        spread_kernel, out_shape=shape((N_ORB, 9, ORB_DEV, LANES), bf16),
        in_specs=[WHOLE_H] * 3, out_specs=WHOLE_H,
        scratch_shapes=[
            pltpu.VMEM((GROUPS, ORB_DEV, 8, BOX * BOX // GROUPS), bf16),
            pltpu.VMEM((TILES * rows, LANES), f32),
            pltpu.VMEM((16, PAIR_DEV), i32),
            pltpu.VMEM((8, LANES), f32),
            pltpu.VMEM((N_ORB, 9, ORB_DEV, LANES), bf16),
            pltpu.SemaphoreType.DMA((GROUPS + 2,)),
            pltpu.SemaphoreType.DMA((GROUPS,)),
        ],
        compiler_params=pltpu.CompilerParams(vmem_limit_bytes=60 * 1024 * 1024), name="spread",
    )(pair_first.reshape(1, PAIR_DEV), pair_shift.T, orbitals)
    pieces = lax.all_to_all(pieces, "orb", split_axis=0, concat_axis=0, tiled=True)
    place, second, choose = pl.pallas_call(
        place_kernel,
        out_shape=(shape((N_DEV, 4 * LANES), bf16), shape((4, LANES), f32), shape((N_DEV, N_DEV), bf16)),
        in_specs=[WHOLE_S, WHOLE_V, WHOLE_V], out_specs=(WHOLE_V,) * 3,
        compiler_params=PARAMS, name="place",
    )(pair_count, second_owner.reshape(4, LANES), second_local.reshape(4, LANES))
    picked, index, mine = pl.pallas_call(
        pick_kernel,
        out_shape=(pair_shape, shape((2, N_DEV), i32), shape((1, LANES), i32)),
        in_specs=[WHOLE_S] + [WHOLE_V] * 4,
        out_specs=(WHOLE_V,) * 3,
        scratch_shapes=[pltpu.VMEM((N_DEV * 16, LANES), f32)],
        compiler_params=PARAMS, name="pick",
    )(me, place, second, choose, pieces)
    boxes = lax.all_to_all(picked, ("orb", "slab"), split_axis=0, concat_axis=0, tiled=True)
    right, left, screen = (jnp.asarray(table) for table in tables())
    terms = pl.pallas_call(
        solve_kernel, out_shape=pair_shape,
        in_specs=[WHOLE_S] + [WHOLE_V] * 4,
        out_specs=WHOLE_V,
        scratch_shapes=[
            pltpu.VMEM((TILES, 8, 8, LANES), f32),
            pltpu.VMEM((TILES, BOX, LANES), f32),
            pltpu.VMEM((TILES, 8, 8, LANES), f32),
        ],
        compiler_params=PARAMS, name="solve",
    )(mine, right, left, screen, boxes)
    terms = lax.all_to_all(terms, ("orb", "slab"), split_axis=0, concat_axis=0, tiled=True)
    pieces = pl.pallas_call(
        sum_kernel, out_shape=shape((N_ORB, rows, LANES), bf16),
        in_specs=[WHOLE_V, WHOLE_V], out_specs=WHOLE_V,
        scratch_shapes=[pltpu.VMEM((N_DEV * 16, LANES), f32), pltpu.VMEM((N_DEV * 8, LANES), f32)],
        compiler_params=PARAMS, name="sum",
    )(index, terms)
    pieces = lax.all_to_all(pieces, "orb", split_axis=0, concat_axis=0, tiled=True)
    return pl.pallas_call(
        join_kernel, out_shape=shape((ORB_DEV, 8, BOX * BOX), bf16), grid=(ORB_DEV // 2,),
        in_specs=[pl.BlockSpec((N_ORB, rows, LANES), lambda pair: (0, 0, 0))],
        out_specs=pl.BlockSpec((2, 8, BOX * BOX), lambda pair: (pair, 0, 0)),
        compiler_params=PARAMS, name="join",
    )(pieces)


def solution(mesh):
    in_specs = (P("orb", "slab", None), P("orb"), P(), P(), P("orb", None), P())
    out_specs = P("orb", "slab", None)
    return jax.shard_map(body, mesh=mesh, in_specs=in_specs, out_specs=out_specs, check_vma=False)
```

```python
import math

import jax
import jax.numpy as jnp
import numpy as np
from jax import lax
from jax.experimental import pallas as pl
from jax.experimental.pallas import tpu as pltpu
from jax.sharding import PartitionSpec as P

BOX = 64
ORB_DEV = 8
PAIR_DEV = 16
N_ORB = 32
N_DEV = 256
TILES = 32
LANES = 128
SCREENING = 0.02
GROUPS = 4
PARAMS = pltpu.CompilerParams(vmem_limit_bytes=48 * 1024 * 1024)
WHOLE_V = pl.BlockSpec(memory_space=pltpu.VMEM)
WHOLE_H = pl.BlockSpec(memory_space=pltpu.HBM)
WHOLE_S = pl.BlockSpec(memory_space=pltpu.SMEM)


def hartley_table():
    line = np.arange(BOX)
    angle = (line[:, None] * line[None, :] % BOX) * (2.0 * math.pi / BOX)
    return np.cos(angle) + np.sin(angle)


def halves(table):
    high = table.astype(np.float32).astype(jnp.bfloat16)
    low = (table - high.astype(np.float64)).astype(np.float32).astype(jnp.bfloat16)
    return high, low


def tables():
    high, low = halves(hartley_table())
    zero = np.zeros((BOX, BOX), high.dtype)

    def twice(table):
        return np.block([[table, zero], [zero, table]])

    right = np.block([[twice(high), twice(low)], [twice(high), np.zeros((128, 128), high.dtype)]])
    left = np.concatenate([high, high, low], axis=1)
    lam = 2.0 - 2.0 * np.cos(np.arange(BOX) * (2.0 * math.pi / BOX))
    lam_a = np.repeat(lam.reshape(2, TILES).T, BOX, axis=1)
    under = lam_a[:, None, :] + lam[None, :, None] + np.tile(lam, 2)[None, None, :] + SCREENING
    return right, left, (1.0 / BOX**3 / under).astype(np.float32)


def split(field):
    high = field.astype(jnp.bfloat16)
    low = (field - high.astype(jnp.float32)).astype(jnp.bfloat16)
    return high, low


def fast_hartley(parts):
    n = len(parts)
    if n == 1:
        return parts
    if n == 2:
        return [parts[0] + parts[1], parts[0] - parts[1]]
    even, odd = fast_hartley(parts[0::2]), fast_hartley(parts[1::2])
    m = n // 2
    out = [None] * n
    for k in range(m):
        if k == 0 or 4 * k == n:
            turned = odd[k]
        else:
            angle = 2.0 * math.pi * k / n
            turned = odd[k] * math.cos(angle) + odd[m - k] * math.sin(angle)
        out[k] = even[k] + turned
        out[k + m] = even[k] - turned
    return out


def twist(parts, first):
    out = []
    for k in range(TILES):
        mirror = parts[(TILES - k) % TILES]
        angle = 2.0 * math.pi * k / BOX
        if k == 0 or 2 * k == TILES:
            out.append(parts[k])
        else:
            out.append(jnp.where(first, parts[k], parts[k] * math.cos(angle) + mirror * math.sin(angle)))
    return out


def untwist(parts, first):
    out = []
    for k in range(TILES):
        mirror = parts[(TILES - k) % TILES]
        angle = 2.0 * math.pi * k / BOX
        back = 2.0 * math.pi * ((TILES - k) % TILES) / BOX
        if k == 0 or 2 * k == TILES:
            out.append(parts[k])
        else:
            out.append(jnp.where(first, parts[k], parts[k] * math.cos(angle) + mirror * math.sin(back)))
    return out


def spread_kernel(first, shift, orbitals, pieces, taken, tall, small, about, packed, arrived, sent):
    few = [
        pltpu.make_async_copy(first, small.at[0:1], arrived.at[GROUPS]),
        pltpu.make_async_copy(shift, small.at[8:10], arrived.at[GROUPS + 1]),
    ]
    width = BOX * BOX // GROUPS
    many = [
        pltpu.make_async_copy(orbitals.at[:, :, pl.ds(k * width, width)], taken.at[k], arrived.at[k])
        for k in range(GROUPS)
    ]
    for copy in few + many:
        copy.start()
    about[...] = jnp.zeros_like(about)
    for copy in few:
        copy.wait()
    about[0:1, :PAIR_DEV] = small[0:1, :].astype(jnp.float32)
    about[1:3, :PAIR_DEV] = small[8:10, :].astype(jnp.float32)
    placed = pltpu.roll(about[...], lax.axis_index("orb") % 8 * PAIR_DEV, 1).astype(jnp.bfloat16)
    inside = TILES // GROUPS
    out = []
    for k in range(GROUPS):
        many[k].wait()
        for orbital in range(ORB_DEV):
            box = taken[k, orbital].astype(jnp.float32)
            for tile in range(inside):
                row = (k * inside + tile) * ORB_DEV * 8 + 8 * orbital
                tall[row : row + 8, :] = box[:, tile * LANES : (tile + 1) * LANES]
        for tile in range(k * inside, (k + 1) * inside):
            for z in range(8):
                row = tile * ORB_DEV * 8 + z
                packed[tile, z] = tall[pl.ds(row, ORB_DEV, stride=8), :].astype(jnp.bfloat16)
            packed[tile, 8] = placed
        at = pl.ds(k * inside, inside)
        out.append(pltpu.make_async_copy(packed.at[at], pieces.at[at], sent.at[k]))
        out[k].start()
    for copy in out:
        copy.wait()


def dot_rows(one, two):
    return lax.dot_general(one, two, (((1,), (1,)), ((), ())), preferred_element_type=jnp.float32)


def chosen(column):
    lane = lax.broadcasted_iota(jnp.int32, (N_DEV, LANES), 1).astype(jnp.float32)
    hits = [jnp.where(column == lane + half * LANES, 1.0, 0.0) for half in range(2)]
    return jnp.concatenate(hits, axis=1).astype(jnp.bfloat16)


def place_kernel(count, owner, local, place, second, choose):
    shape = (4, LANES)
    slot = lax.broadcasted_iota(jnp.int32, shape, 0) * LANES + lax.broadcasted_iota(jnp.int32, shape, 1)
    orb, rank = slot // PAIR_DEV, slot % PAIR_DEV
    before, live = jnp.zeros(shape, jnp.int32), jnp.zeros(shape, jnp.int32)
    for e in range(N_ORB):
        before = before + jnp.where(orb > e, count[e], 0)
        live = jnp.where(orb == e, count[e], live)
    rank = jnp.where(rank < live, before + rank, -1).astype(jnp.float32)
    pair = lax.broadcasted_iota(jnp.int32, (N_DEV, LANES), 0).astype(jnp.float32)
    second[...] = (owner[...] * ORB_DEV + local[...]).astype(jnp.float32)
    for k in range(4):
        at = slice(k * LANES, (k + 1) * LANES)
        place[:, at] = jnp.where(pair == rank[k : k + 1], 1.0, 0.0).astype(jnp.bfloat16)
    rows = jnp.concatenate([second[k : k + 1, :] for k in range(4)], axis=1)
    rows = jnp.broadcast_to(rows, (LANES, 4 * LANES)).astype(jnp.bfloat16)
    choose[...] = chosen(dot_rows(place[...], rows))


def pick_kernel(me, place, second, choose, pieces, picked, index, mine, tall):
    blocks = []
    for k in range(4):
        block = jnp.sum(pieces[8 * k : 8 * k + 8, 8].astype(jnp.float32), axis=0)
        row = lax.broadcasted_iota(jnp.int32, (8, LANES), 0)
        lane = lax.broadcasted_iota(jnp.int32, (8, LANES), 1)
        orbital = (8 * (8 * k + lane // PAIR_DEV)).astype(jnp.float32)
        block = jnp.where(row == 0, block + orbital, block)
        blocks.append(jnp.where(row == 3, jnp.broadcast_to(second[k : k + 1, :], (8, LANES)), block))
    facts = jnp.concatenate(blocks, axis=1)
    first = jnp.broadcast_to(facts[0:1], (LANES, 4 * LANES)).astype(jnp.bfloat16)
    choose_first = chosen(dot_rows(place[...], first))
    known = dot_rows(facts.astype(jnp.bfloat16), place[...])
    index[0:1, :] = known[0:1].astype(jnp.int32)
    index[1:2, :] = known[3:4].astype(jnp.int32)
    lane = lax.broadcasted_iota(jnp.int32, (8, N_DEV), 1)
    here = jnp.sum(jnp.where(lane == me[0], known, 0.0), axis=1, keepdims=True)
    lane = lax.broadcasted_iota(jnp.int32, (1, LANES), 1)
    mine[...] = jnp.where(lane == 0, here[1:2], here[2:3]).astype(jnp.int32)
    for z in range(0, 8, 2):
        field = [
            pieces[:, z + k].astype(jnp.float32).reshape(N_DEV, LANES).astype(jnp.bfloat16) for k in range(2)
        ]
        field = jnp.concatenate(field, axis=1)
        for side, picker in enumerate((choose_first, choose[...])):
            out = jnp.dot(picker, field, preferred_element_type=jnp.float32)
            tall[pl.ds(8 * side + z, N_DEV, stride=16), :] = out[:, :LANES]
            tall[pl.ds(8 * side + z + 1, N_DEV, stride=16), :] = out[:, LANES:]
    for k in range(0, N_DEV, 8):
        picked[k : k + 8] = tall[16 * k : 16 * k + 128, :].reshape(8, 16, LANES).astype(jnp.bfloat16)


def shifted(tiles, start, count, flat, shift_x, shift_y):
    lane = lax.broadcasted_iota(jnp.int32, (8, LANES), 1)
    whole, rest = flat // LANES, flat % LANES
    later = (lane >= rest)[None]
    y = lane % BOX - shift_y
    keep_y = (y >= 0) & (y < BOX)
    turned = [
        pltpu.roll(tiles((start + k - whole - 1 + 2 * TILES) % TILES), rest, 2) for k in range(count + 1)
    ]
    out = []
    for k in range(count):
        x = 2 * (start + k) + lane // BOX - shift_x
        keep = jnp.where(keep_y & (x >= 0) & (x < BOX), 1.0, 0.0)
        out.append(jnp.where(later, turned[k + 1], turned[k]) * keep[None])
    return out


def solve_kernel(shift, right, left, screen, boxes, terms, moved, field, other):
    shift_x, shift_y = shift[0, 0], shift[0, 1]
    full = BOX * BOX
    ahead = (shift_x * BOX + shift_y + full) % full
    back = (full - ahead) % full
    early = lax.broadcasted_iota(jnp.int32, (8, LANES), 1) < BOX
    sign = jnp.where(early, 1.0, -1.0)

    def first_tile(tile):
        return boxes[pl.ds(tile * 8, 8), :8, :].astype(jnp.float32)

    def second_tile(tile):
        return boxes[pl.ds(tile * 8, 8), 8:, :].astype(jnp.float32)

    def along_y(block):
        high, low = split(block)
        product = jnp.dot(
            jnp.concatenate([high, low], axis=1), right[...], preferred_element_type=jnp.float32
        )
        return product[:, :LANES] + product[:, LANES:]

    for start in range(0, TILES, 4):
        products = []
        for k, box in enumerate(shifted(second_tile, start, 4, ahead, shift_x, shift_y)):
            moved[start + k] = box
            products.append(first_tile(start + k) * box)
        block = along_y(jnp.stack(products).reshape(4 * BOX, LANES)).reshape(4, BOX, LANES)
        for k in range(4):
            field[start + k] = block[k]

    for row in range(0, BOX, 8):
        parts = twist(fast_hartley([field[k, row : row + 8, :] for k in range(TILES)]), early)
        for k in range(TILES):
            field[k, row : row + 8, :] = sign * parts[k] + pltpu.roll(parts[k], BOX, 1)

    def along_z(block):
        high, low = split(block)
        return jnp.dot(
            left[...], jnp.concatenate([high, low, high], axis=0), preferred_element_type=jnp.float32
        )

    for tile in range(0, TILES, 2):
        block = along_z(jnp.concatenate([field[tile], field[tile + 1]], axis=1))
        block = block * jnp.concatenate([screen[tile], screen[tile + 1]], axis=1)
        block = along_z(block)
        field[tile] = block[:, :LANES]
        field[tile + 1] = block[:, LANES:]

    for row in range(0, BOX, 8):
        parts = [field[k, row : row + 8, :] for k in range(TILES)]
        parts = [sign * part + pltpu.roll(part, BOX, 1) for part in parts]
        parts = fast_hartley(untwist(parts, early))
        for k in range(TILES):
            field[k, row : row + 8, :] = parts[k]

    for start in range(0, TILES, 4):
        block = field[start : start + 4].reshape(4 * BOX, LANES)
        potential = along_y(block).reshape(4, 8, 8, LANES)
        for k in range(4):
            other[start + k] = potential[k] * first_tile(start + k)
            moved[start + k] = potential[k] * moved[start + k]

    for start in range(0, TILES, 4):
        carried = shifted(lambda tile: other[tile], start, 4, back, -shift_x, -shift_y)
        for k in range(4):
            both = jnp.concatenate([moved[start + k], carried[k]], axis=1)
            terms[(start + k) * 8 : (start + k + 1) * 8] = both.astype(jnp.bfloat16)


def sum_kernel(index, terms, pieces, tall, summed):
    for k in range(0, N_DEV, 8):
        tall[16 * k : 16 * k + 128, :] = terms[k : k + 8].astype(jnp.float32).reshape(128, LANES)
    orbital = lax.broadcasted_iota(jnp.int32, (N_DEV, N_DEV), 0)
    hits = [jnp.where(orbital == index[side : side + 1, :], 1.0, 0.0) for side in range(2)]
    hits = jnp.concatenate(hits, axis=1).astype(jnp.bfloat16)
    for z in range(0, 8, 2):
        field = [
            jnp.concatenate(
                [tall[pl.ds(8 * side + z + k, N_DEV, stride=16), :] for side in range(2)], axis=0
            ).astype(jnp.bfloat16)
            for k in range(2)
        ]
        out = jnp.dot(hits, jnp.concatenate(field, axis=1), preferred_element_type=jnp.float32)
        summed[pl.ds(z, N_DEV, stride=8), :] = out[:, :LANES]
        summed[pl.ds(z + 1, N_DEV, stride=8), :] = out[:, LANES:]
    for e in range(N_ORB):
        pieces[e] = summed[e * ORB_DEV * 8 : (e + 1) * ORB_DEV * 8, :].astype(jnp.bfloat16)


def join_kernel(pieces, result):
    for pair in range(ORB_DEV // 2):
        tiles = [pieces[tile, 16 * pair : 16 * pair + 16, :].astype(jnp.float32) for tile in range(TILES)]
        for side in range(2):
            rows = [tile[8 * side : 8 * side + 8] for tile in tiles]
            result[2 * pair + side] = jnp.concatenate(rows, axis=1).astype(jnp.bfloat16)


def body(orbitals, pair_first, second_owner, second_local, pair_shift, pair_count):
    f32, bf16, i32 = jnp.float32, jnp.bfloat16, jnp.int32
    shape = jax.ShapeDtypeStruct
    me = (lax.axis_index("orb") * 8 + lax.axis_index("slab")).reshape(1)
    rows = ORB_DEV * 8
    pair_shape = shape((N_DEV, 16, LANES), bf16)
    pieces = pl.pallas_call(
        spread_kernel, out_shape=shape((N_ORB, 9, ORB_DEV, LANES), bf16),
        in_specs=[WHOLE_H] * 3, out_specs=WHOLE_H,
        scratch_shapes=[
            pltpu.VMEM((GROUPS, ORB_DEV, 8, BOX * BOX // GROUPS), bf16),
            pltpu.VMEM((TILES * rows + 64, LANES), f32),
            pltpu.VMEM((16, PAIR_DEV), i32),
            pltpu.VMEM((8, LANES), f32),
            pltpu.VMEM((N_ORB, 9, ORB_DEV, LANES), bf16),
            pltpu.SemaphoreType.DMA((GROUPS + 2,)),
            pltpu.SemaphoreType.DMA((GROUPS,)),
        ],
        compiler_params=pltpu.CompilerParams(vmem_limit_bytes=60 * 1024 * 1024), name="spread",
    )(pair_first.reshape(1, PAIR_DEV), pair_shift.T, orbitals)
    pieces = lax.all_to_all(pieces, "orb", split_axis=0, concat_axis=0, tiled=True)
    place, second, choose = pl.pallas_call(
        place_kernel,
        out_shape=(shape((N_DEV, 4 * LANES), bf16), shape((4, LANES), f32), shape((N_DEV, N_DEV), bf16)),
        in_specs=[WHOLE_S, WHOLE_V, WHOLE_V], out_specs=(WHOLE_V,) * 3,
        compiler_params=PARAMS, name="place",
    )(pair_count, second_owner.reshape(4, LANES), second_local.reshape(4, LANES))
    picked, index, mine = pl.pallas_call(
        pick_kernel,
        out_shape=(pair_shape, shape((2, N_DEV), i32), shape((1, LANES), i32)),
        in_specs=[WHOLE_S] + [WHOLE_V] * 4,
        out_specs=(WHOLE_V,) * 3,
        scratch_shapes=[pltpu.VMEM((N_DEV * 16 + 16, LANES), f32)],
        compiler_params=PARAMS, name="pick",
    )(me, place, second, choose, pieces)
    boxes = lax.all_to_all(picked, ("orb", "slab"), split_axis=0, concat_axis=0, tiled=True)
    right, left, screen = (jnp.asarray(table) for table in tables())
    terms = pl.pallas_call(
        solve_kernel, out_shape=pair_shape,
        in_specs=[WHOLE_S] + [WHOLE_V] * 4,
        out_specs=WHOLE_V,
        scratch_shapes=[
            pltpu.VMEM((TILES, 8, 8, LANES), f32),
            pltpu.VMEM((TILES, BOX, LANES), f32),
            pltpu.VMEM((TILES, 8, 8, LANES), f32),
        ],
        compiler_params=PARAMS, name="solve",
    )(mine, right, left, screen, boxes)
    terms = lax.all_to_all(terms, ("orb", "slab"), split_axis=0, concat_axis=0, tiled=True)
    pieces = pl.pallas_call(
        sum_kernel, out_shape=shape((N_ORB, rows, LANES), bf16),
        in_specs=[WHOLE_V, WHOLE_V], out_specs=WHOLE_V,
        scratch_shapes=[pltpu.VMEM((N_DEV * 16 + 16, LANES), f32), pltpu.VMEM((N_DEV * 8 + 8, LANES), f32)],
        compiler_params=PARAMS, name="sum",
    )(index, terms)
    pieces = lax.all_to_all(pieces, "orb", split_axis=0, concat_axis=0, tiled=True)
    return pl.pallas_call(
        join_kernel, out_shape=shape((ORB_DEV, 8, BOX * BOX), bf16),
        in_specs=[WHOLE_V], out_specs=WHOLE_V,
        compiler_params=PARAMS, name="join",
    )(pieces)


def solution(mesh):
    in_specs = (P("orb", "slab", None), P("orb"), P(), P(), P("orb", None), P())
    out_specs = P("orb", "slab", None)
    return jax.shard_map(body, mesh=mesh, in_specs=in_specs, out_specs=out_specs, check_vma=False)
```

```python
import math

import jax
import jax.numpy as jnp
import numpy as np
from jax import lax
from jax.experimental import pallas as pl
from jax.experimental.pallas import tpu as pltpu
from jax.sharding import PartitionSpec as P

BOX = 64
ORB_DEV = 8
PAIR_DEV = 16
N_ORB = 32
N_DEV = 256
TILES = 32
LANES = 128
SCREENING = 0.02
STEPS = [(dy, dz) for dz in (4, 3, 5, 2, 6, 1, 7, 0) for dy in (2, 1, 3, 0)]
GROUPS = 4
PARAMS = pltpu.CompilerParams(vmem_limit_bytes=48 * 1024 * 1024)
WHOLE_V = pl.BlockSpec(memory_space=pltpu.VMEM)
WHOLE_H = pl.BlockSpec(memory_space=pltpu.HBM)
WHOLE_S = pl.BlockSpec(memory_space=pltpu.SMEM)


def hartley_table():
    line = np.arange(BOX)
    angle = (line[:, None] * line[None, :] % BOX) * (2.0 * math.pi / BOX)
    return np.cos(angle) + np.sin(angle)


def halves(table):
    high = table.astype(np.float32).astype(jnp.bfloat16)
    low = (table - high.astype(np.float64)).astype(np.float32).astype(jnp.bfloat16)
    return high, low


def tables():
    high, low = halves(hartley_table())
    zero = np.zeros((BOX, BOX), high.dtype)

    def twice(table):
        return np.block([[table, zero], [zero, table]])

    right = np.block([[twice(high), twice(low)], [twice(high), np.zeros((128, 128), high.dtype)]])
    left = np.concatenate([high, high, low], axis=1)
    lam = 2.0 - 2.0 * np.cos(np.arange(BOX) * (2.0 * math.pi / BOX))
    lam_a = np.repeat(lam.reshape(2, TILES).T, BOX, axis=1)
    under = lam_a[:, None, :] + lam[None, :, None] + np.tile(lam, 2)[None, None, :] + SCREENING
    return right, left, (1.0 / BOX**3 / under).astype(np.float32)


def split(field):
    high = field.astype(jnp.bfloat16)
    low = (field - high.astype(jnp.float32)).astype(jnp.bfloat16)
    return high, low


def fast_hartley(parts):
    n = len(parts)
    if n == 1:
        return parts
    if n == 2:
        return [parts[0] + parts[1], parts[0] - parts[1]]
    even, odd = fast_hartley(parts[0::2]), fast_hartley(parts[1::2])
    m = n // 2
    out = [None] * n
    for k in range(m):
        if k == 0 or 4 * k == n:
            turned = odd[k]
        else:
            angle = 2.0 * math.pi * k / n
            turned = odd[k] * math.cos(angle) + odd[m - k] * math.sin(angle)
        out[k] = even[k] + turned
        out[k + m] = even[k] - turned
    return out


def twist(parts, first):
    out = []
    for k in range(TILES):
        mirror = parts[(TILES - k) % TILES]
        angle = 2.0 * math.pi * k / BOX
        if k == 0 or 2 * k == TILES:
            out.append(parts[k])
        else:
            out.append(jnp.where(first, parts[k], parts[k] * math.cos(angle) + mirror * math.sin(angle)))
    return out


def untwist(parts, first):
    out = []
    for k in range(TILES):
        mirror = parts[(TILES - k) % TILES]
        angle = 2.0 * math.pi * k / BOX
        back = 2.0 * math.pi * ((TILES - k) % TILES) / BOX
        if k == 0 or 2 * k == TILES:
            out.append(parts[k])
        else:
            out.append(jnp.where(first, parts[k], parts[k] * math.cos(angle) + mirror * math.sin(back)))
    return out


def spread_kernel(first, shift, orbitals, pieces, taken, tall, small, about, packed, arrived, sent):
    few = [
        pltpu.make_async_copy(first, small.at[0:1], arrived.at[GROUPS]),
        pltpu.make_async_copy(shift, small.at[8:10], arrived.at[GROUPS + 1]),
    ]
    width = BOX * BOX // GROUPS
    many = [
        pltpu.make_async_copy(orbitals.at[:, :, pl.ds(k * width, width)], taken.at[k], arrived.at[k])
        for k in range(GROUPS)
    ]
    for copy in few + many:
        copy.start()
    about[...] = jnp.zeros_like(about)
    for copy in few:
        copy.wait()
    about[0:1, :PAIR_DEV] = small[0:1, :].astype(jnp.float32)
    about[1:3, :PAIR_DEV] = small[8:10, :].astype(jnp.float32)
    placed = pltpu.roll(about[...], lax.axis_index("orb") % 8 * PAIR_DEV, 1).astype(jnp.bfloat16)
    inside = TILES // GROUPS
    out = []
    for k in range(GROUPS):
        many[k].wait()
        for orbital in range(ORB_DEV):
            box = taken[k, orbital].astype(jnp.float32)
            for tile in range(inside):
                row = (k * inside + tile) * ORB_DEV * 8 + 8 * orbital
                tall[row : row + 8, :] = box[:, tile * LANES : (tile + 1) * LANES]
        for tile in range(k * inside, (k + 1) * inside):
            for z in range(8):
                row = tile * ORB_DEV * 8 + z
                packed[tile, z] = tall[pl.ds(row, ORB_DEV, stride=8), :].astype(jnp.bfloat16)
            packed[tile, 8] = placed
        at = pl.ds(k * inside, inside)
        out.append(pltpu.make_async_copy(packed.at[at], pieces.at[at], sent.at[k]))
        out[k].start()
    for copy in out:
        copy.wait()


def dot_rows(one, two):
    return lax.dot_general(one, two, (((1,), (1,)), ((), ())), preferred_element_type=jnp.float32)


def chosen(column):
    lane = lax.broadcasted_iota(jnp.int32, (N_DEV, LANES), 1).astype(jnp.float32)
    hits = [jnp.where(column == lane + half * LANES, 1.0, 0.0) for half in range(2)]
    return jnp.concatenate(hits, axis=1).astype(jnp.bfloat16)


def place_kernel(count, owner, local, place, second, choose):
    shape = (4, LANES)
    slot = lax.broadcasted_iota(jnp.int32, shape, 0) * LANES + lax.broadcasted_iota(jnp.int32, shape, 1)
    orb, rank = slot // PAIR_DEV, slot % PAIR_DEV
    before, live = jnp.zeros(shape, jnp.int32), jnp.zeros(shape, jnp.int32)
    for e in range(N_ORB):
        before = before + jnp.where(orb > e, count[e], 0)
        live = jnp.where(orb == e, count[e], live)
    rank = jnp.where(rank < live, before + rank, -1).astype(jnp.float32)
    pair = lax.broadcasted_iota(jnp.int32, (N_DEV, LANES), 0).astype(jnp.float32)
    second[...] = (owner[...] * ORB_DEV + local[...]).astype(jnp.float32)
    for k in range(4):
        at = slice(k * LANES, (k + 1) * LANES)
        place[:, at] = jnp.where(pair == rank[k : k + 1], 1.0, 0.0).astype(jnp.bfloat16)
    rows = jnp.concatenate([second[k : k + 1, :] for k in range(4)], axis=1)
    rows = jnp.broadcast_to(rows, (LANES, 4 * LANES)).astype(jnp.bfloat16)
    choose[...] = chosen(dot_rows(place[...], rows))


def pick_kernel(me, place, second, choose, pieces, picked, index, mine, tall):
    blocks = []
    for k in range(4):
        block = jnp.sum(pieces[8 * k : 8 * k + 8, 8].astype(jnp.float32), axis=0)
        row = lax.broadcasted_iota(jnp.int32, (8, LANES), 0)
        lane = lax.broadcasted_iota(jnp.int32, (8, LANES), 1)
        orbital = (8 * (8 * k + lane // PAIR_DEV)).astype(jnp.float32)
        block = jnp.where(row == 0, block + orbital, block)
        blocks.append(jnp.where(row == 3, jnp.broadcast_to(second[k : k + 1, :], (8, LANES)), block))
    facts = jnp.concatenate(blocks, axis=1)
    first = jnp.broadcast_to(facts[0:1], (LANES, 4 * LANES)).astype(jnp.bfloat16)
    choose_first = chosen(dot_rows(place[...], first))
    known = dot_rows(facts.astype(jnp.bfloat16), place[...])
    index[0:1, :] = known[0:1].astype(jnp.int32)
    index[1:2, :] = known[3:4].astype(jnp.int32)
    lane = lax.broadcasted_iota(jnp.int32, (8, N_DEV), 1)
    here = jnp.sum(jnp.where(lane == me[0], known, 0.0), axis=1, keepdims=True)
    lane = lax.broadcasted_iota(jnp.int32, (1, LANES), 1)
    mine[...] = jnp.where(lane == 0, here[1:2], here[2:3]).astype(jnp.int32)
    for z in range(0, 8, 2):
        field = [
            pieces[:, z + k].astype(jnp.float32).reshape(N_DEV, LANES).astype(jnp.bfloat16) for k in range(2)
        ]
        field = jnp.concatenate(field, axis=1)
        for side, picker in enumerate((choose_first, choose[...])):
            out = jnp.dot(picker, field, preferred_element_type=jnp.float32)
            tall[pl.ds(8 * side + z, N_DEV, stride=16), :] = out[:, :LANES]
            tall[pl.ds(8 * side + z + 1, N_DEV, stride=16), :] = out[:, LANES:]
    for k in range(0, N_DEV, 8):
        picked[k : k + 8] = tall[16 * k : 16 * k + 128, :].reshape(8, 16, LANES).astype(jnp.bfloat16)


def shifted(tiles, start, count, flat, shift_x, shift_y):
    lane = lax.broadcasted_iota(jnp.int32, (8, LANES), 1)
    whole, rest = flat // LANES, flat % LANES
    later = (lane >= rest)[None]
    y = lane % BOX - shift_y
    keep_y = (y >= 0) & (y < BOX)
    turned = [
        pltpu.roll(tiles((start + k - whole - 1 + 2 * TILES) % TILES), rest, 2) for k in range(count + 1)
    ]
    out = []
    for k in range(count):
        x = 2 * (start + k) + lane // BOX - shift_x
        keep = jnp.where(keep_y & (x >= 0) & (x < BOX), 1.0, 0.0)
        out.append(jnp.where(later, turned[k + 1], turned[k]) * keep[None])
    return out


def solve_kernel(shift, right, left, screen, boxes, terms, moved, field, other):
    shift_x, shift_y = shift[0, 0], shift[0, 1]
    full = BOX * BOX
    ahead = (shift_x * BOX + shift_y + full) % full
    back = (full - ahead) % full
    early = lax.broadcasted_iota(jnp.int32, (8, LANES), 1) < BOX
    sign = jnp.where(early, 1.0, -1.0)

    def first_tile(tile):
        return boxes[pl.ds(tile * 8, 8), :8, :].astype(jnp.float32)

    def second_tile(tile):
        return boxes[pl.ds(tile * 8, 8), 8:, :].astype(jnp.float32)

    def along_y(block):
        high, low = split(block)
        product = jnp.dot(
            jnp.concatenate([high, low], axis=1), right[...], preferred_element_type=jnp.float32
        )
        return product[:, :LANES] + product[:, LANES:]

    for start in range(0, TILES, 4):
        products = []
        for k, box in enumerate(shifted(second_tile, start, 4, ahead, shift_x, shift_y)):
            moved[start + k] = box
            products.append(first_tile(start + k) * box)
        block = along_y(jnp.stack(products).reshape(4 * BOX, LANES)).reshape(4, BOX, LANES)
        for k in range(4):
            field[start + k] = block[k]

    for row in range(0, BOX, 8):
        parts = twist(fast_hartley([field[k, row : row + 8, :] for k in range(TILES)]), early)
        for k in range(TILES):
            field[k, row : row + 8, :] = sign * parts[k] + pltpu.roll(parts[k], BOX, 1)

    def along_z(block):
        high, low = split(block)
        return jnp.dot(
            left[...], jnp.concatenate([high, low, high], axis=0), preferred_element_type=jnp.float32
        )

    for tile in range(0, TILES, 2):
        block = along_z(jnp.concatenate([field[tile], field[tile + 1]], axis=1))
        block = block * jnp.concatenate([screen[tile], screen[tile + 1]], axis=1)
        block = along_z(block)
        field[tile] = block[:, :LANES]
        field[tile + 1] = block[:, LANES:]

    for row in range(0, BOX, 8):
        parts = [field[k, row : row + 8, :] for k in range(TILES)]
        parts = [sign * part + pltpu.roll(part, BOX, 1) for part in parts]
        parts = fast_hartley(untwist(parts, early))
        for k in range(TILES):
            field[k, row : row + 8, :] = parts[k]

    for start in range(0, TILES, 4):
        block = field[start : start + 4].reshape(4 * BOX, LANES)
        potential = along_y(block).reshape(4, 8, 8, LANES)
        for k in range(4):
            other[start + k] = potential[k] * first_tile(start + k)
            moved[start + k] = potential[k] * moved[start + k]

    for start in range(0, TILES, 4):
        carried = shifted(lambda tile: other[tile], start, 4, back, -shift_x, -shift_y)
        for k in range(4):
            both = jnp.concatenate([moved[start + k], carried[k]], axis=1)
            terms[(start + k) * 8 : (start + k + 1) * 8] = both.astype(jnp.bfloat16)


def partner(step, sign):
    orb = lax.axis_index("orb")
    y, z = orb // 8 + sign * step[0] + 4, orb % 8 + sign * step[1] + 8
    return y % 4 * 8 + z % 8


def sum_kernel(index, terms, *rest):
    pieces, (tall, summed) = rest[:N_ORB], rest[N_ORB:]
    for k in range(0, N_DEV, 8):
        tall[16 * k : 16 * k + 128, :] = terms[k : k + 8].astype(jnp.float32).reshape(128, LANES)
    orbital = lax.broadcasted_iota(jnp.int32, (N_DEV, N_DEV), 0)
    hits = [jnp.where(orbital == index[side : side + 1, :], 1.0, 0.0) for side in range(2)]
    hits = jnp.concatenate(hits, axis=1).astype(jnp.bfloat16)
    for z in range(0, 8, 2):
        field = [
            jnp.concatenate(
                [tall[pl.ds(8 * side + z + k, N_DEV, stride=16), :] for side in range(2)], axis=0
            ).astype(jnp.bfloat16)
            for k in range(2)
        ]
        out = jnp.dot(hits, jnp.concatenate(field, axis=1), preferred_element_type=jnp.float32)
        summed[pl.ds(z, N_DEV, stride=8), :] = out[:, :LANES]
        summed[pl.ds(z + 1, N_DEV, stride=8), :] = out[:, LANES:]
    for k, away in enumerate(STEPS):
        rows = pl.ds(pl.multiple_of(partner(away, 1) * ORB_DEV * 8, ORB_DEV * 8), ORB_DEV * 8)
        pieces[k][...] = summed[rows, :].astype(jnp.bfloat16)


def join_kernel(*rest):
    pieces, result = rest[:N_ORB], rest[N_ORB]
    for k, away in enumerate(STEPS):
        lanes = pl.ds(pl.multiple_of(partner(away, -1) * LANES, LANES), LANES)
        rows = pieces[k][...].astype(jnp.float32)
        for orbital in range(ORB_DEV):
            result[orbital, :, lanes] = rows[8 * orbital : 8 * orbital + 8].astype(jnp.bfloat16)


def permuted(pieces, away):
    if away == (0, 0):
        return pieces
    pairs = []
    for orb in range(N_ORB):
        y, z = (orb // 8 + away[0]) % 4, (orb % 8 + away[1]) % 8
        pairs.append((orb, y * 8 + z))
    return lax.ppermute(pieces, "orb", pairs)


def body(orbitals, pair_first, second_owner, second_local, pair_shift, pair_count):
    f32, bf16, i32 = jnp.float32, jnp.bfloat16, jnp.int32
    shape = jax.ShapeDtypeStruct
    me = (lax.axis_index("orb") * 8 + lax.axis_index("slab")).reshape(1)
    rows = ORB_DEV * 8
    pair_shape = shape((N_DEV, 16, LANES), bf16)
    pieces = pl.pallas_call(
        spread_kernel, out_shape=shape((N_ORB, 9, ORB_DEV, LANES), bf16),
        in_specs=[WHOLE_H] * 3, out_specs=WHOLE_H,
        scratch_shapes=[
            pltpu.VMEM((GROUPS, ORB_DEV, 8, BOX * BOX // GROUPS), bf16),
            pltpu.VMEM((TILES * rows + 64, LANES), f32),
            pltpu.VMEM((16, PAIR_DEV), i32),
            pltpu.VMEM((8, LANES), f32),
            pltpu.VMEM((N_ORB, 9, ORB_DEV, LANES), bf16),
            pltpu.SemaphoreType.DMA((GROUPS + 2,)),
            pltpu.SemaphoreType.DMA((GROUPS,)),
        ],
        compiler_params=pltpu.CompilerParams(vmem_limit_bytes=60 * 1024 * 1024), name="spread",
    )(pair_first.reshape(1, PAIR_DEV), pair_shift.T, orbitals)
    pieces = lax.all_to_all(pieces, "orb", split_axis=0, concat_axis=0, tiled=True)
    place, second, choose = pl.pallas_call(
        place_kernel,
        out_shape=(shape((N_DEV, 4 * LANES), bf16), shape((4, LANES), f32), shape((N_DEV, N_DEV), bf16)),
        in_specs=[WHOLE_S, WHOLE_V, WHOLE_V], out_specs=(WHOLE_V,) * 3,
        compiler_params=PARAMS, name="place",
    )(pair_count, second_owner.reshape(4, LANES), second_local.reshape(4, LANES))
    picked, index, mine = pl.pallas_call(
        pick_kernel,
        out_shape=(pair_shape, shape((2, N_DEV), i32), shape((1, LANES), i32)),
        in_specs=[WHOLE_S] + [WHOLE_V] * 4,
        out_specs=(WHOLE_V,) * 3,
        scratch_shapes=[pltpu.VMEM((N_DEV * 16 + 16, LANES), f32)],
        compiler_params=PARAMS, name="pick",
    )(me, place, second, choose, pieces)
    boxes = lax.all_to_all(picked, ("orb", "slab"), split_axis=0, concat_axis=0, tiled=True)
    right, left, screen = (jnp.asarray(table) for table in tables())
    terms = pl.pallas_call(
        solve_kernel, out_shape=pair_shape,
        in_specs=[WHOLE_S] + [WHOLE_V] * 4,
        out_specs=WHOLE_V,
        scratch_shapes=[
            pltpu.VMEM((TILES, 8, 8, LANES), f32),
            pltpu.VMEM((TILES, BOX, LANES), f32),
            pltpu.VMEM((TILES, 8, 8, LANES), f32),
        ],
        compiler_params=PARAMS, name="solve",
    )(mine, right, left, screen, boxes)
    terms = lax.all_to_all(terms, ("orb", "slab"), split_axis=0, concat_axis=0, tiled=True)
    pieces = pl.pallas_call(
        sum_kernel, out_shape=(shape((rows, LANES), bf16),) * N_ORB,
        in_specs=[WHOLE_V, WHOLE_V], out_specs=(WHOLE_V,) * N_ORB,
        scratch_shapes=[pltpu.VMEM((N_DEV * 16 + 16, LANES), f32), pltpu.VMEM((N_DEV * 8 + 8, LANES), f32)],
        compiler_params=PARAMS, name="sum",
    )(index, terms)
    pieces = [permuted(piece, away) for piece, away in zip(pieces, STEPS)]
    return pl.pallas_call(
        join_kernel, out_shape=shape((ORB_DEV, 8, BOX * BOX), bf16),
        in_specs=[WHOLE_V] * N_ORB, out_specs=WHOLE_V,
        compiler_params=PARAMS, name="join",
    )(*pieces)


def solution(mesh):
    in_specs = (P("orb", "slab", None), P("orb"), P(), P(), P("orb", None), P())
    out_specs = P("orb", "slab", None)
    return jax.shard_map(body, mesh=mesh, in_specs=in_specs, out_specs=out_specs, check_vma=False)
```

```python
import math

import jax
import jax.numpy as jnp
import numpy as np
from jax import lax
from jax.experimental import pallas as pl
from jax.experimental.pallas import tpu as pltpu
from jax.sharding import PartitionSpec as P

BOX = 64
ORB_DEV = 8
PAIR_DEV = 16
N_ORB = 32
N_DEV = 256
TILES = 32
LANES = 128
SCREENING = 0.02
GROUPS = 4
PARAMS = pltpu.CompilerParams(vmem_limit_bytes=48 * 1024 * 1024)
WHOLE_V = pl.BlockSpec(memory_space=pltpu.VMEM)
WHOLE_H = pl.BlockSpec(memory_space=pltpu.HBM)
WHOLE_S = pl.BlockSpec(memory_space=pltpu.SMEM)


def hartley_table():
    line = np.arange(BOX)
    angle = (line[:, None] * line[None, :] % BOX) * (2.0 * math.pi / BOX)
    return np.cos(angle) + np.sin(angle)


def halves(table):
    high = table.astype(np.float32).astype(jnp.bfloat16)
    low = (table - high.astype(np.float64)).astype(np.float32).astype(jnp.bfloat16)
    return high, low


def tables():
    high, low = halves(hartley_table())
    zero = np.zeros((BOX, BOX), high.dtype)

    def twice(table):
        return np.block([[table, zero], [zero, table]])

    right = np.block([[twice(high), twice(low)], [twice(high), np.zeros((128, 128), high.dtype)]])
    left = np.block([[high, high], [low, np.zeros((BOX, BOX), high.dtype)]])
    lam = 2.0 - 2.0 * np.cos(np.arange(BOX) * (2.0 * math.pi / BOX))
    lam_a = np.repeat(lam.reshape(2, TILES).T, BOX, axis=1)
    under = lam_a[:, None, :] + lam[None, :, None] + np.tile(lam, 2)[None, None, :] + SCREENING
    return right, left, (1.0 / BOX**3 / under).astype(np.float32)


def split(field):
    high = field.astype(jnp.bfloat16)
    low = (field - high.astype(jnp.float32)).astype(jnp.bfloat16)
    return high, low


def fast_hartley(parts):
    n = len(parts)
    if n == 1:
        return parts
    if n == 2:
        return [parts[0] + parts[1], parts[0] - parts[1]]
    even, odd = fast_hartley(parts[0::2]), fast_hartley(parts[1::2])
    m = n // 2
    out = [None] * n
    for k in range(m):
        if k == 0 or 4 * k == n:
            turned = odd[k]
        else:
            angle = 2.0 * math.pi * k / n
            turned = odd[k] * math.cos(angle) + odd[m - k] * math.sin(angle)
        out[k] = even[k] + turned
        out[k + m] = even[k] - turned
    return out


def twist(parts, first):
    out = []
    for k in range(TILES):
        mirror = parts[(TILES - k) % TILES]
        angle = 2.0 * math.pi * k / BOX
        if k == 0 or 2 * k == TILES:
            out.append(parts[k])
        else:
            out.append(jnp.where(first, parts[k], parts[k] * math.cos(angle) + mirror * math.sin(angle)))
    return out


def untwist(parts, first):
    out = []
    for k in range(TILES):
        mirror = parts[(TILES - k) % TILES]
        angle = 2.0 * math.pi * k / BOX
        back = 2.0 * math.pi * ((TILES - k) % TILES) / BOX
        if k == 0 or 2 * k == TILES:
            out.append(parts[k])
        else:
            out.append(jnp.where(first, parts[k], parts[k] * math.cos(angle) + mirror * math.sin(back)))
    return out


def spread_kernel(first, shift, orbitals, pieces, taken, tall, small, about, packed, arrived, sent):
    few = [
        pltpu.make_async_copy(first, small.at[0:1], arrived.at[GROUPS]),
        pltpu.make_async_copy(shift, small.at[8:10], arrived.at[GROUPS + 1]),
    ]
    width = BOX * BOX // GROUPS
    many = [
        pltpu.make_async_copy(orbitals.at[:, :, pl.ds(k * width, width)], taken.at[k], arrived.at[k])
        for k in range(GROUPS)
    ]
    for copy in few + many:
        copy.start()
    about[...] = jnp.zeros_like(about)
    for copy in few:
        copy.wait()
    about[0:1, :PAIR_DEV] = small[0:1, :].astype(jnp.float32)
    about[1:3, :PAIR_DEV] = small[8:10, :].astype(jnp.float32)
    placed = pltpu.roll(about[...], lax.axis_index("orb") % 8 * PAIR_DEV, 1).astype(jnp.bfloat16)
    inside = TILES // GROUPS
    out = []
    for k in range(GROUPS):
        many[k].wait()
        for orbital in range(ORB_DEV):
            box = taken[k, orbital].astype(jnp.float32)
            for tile in range(inside):
                row = (k * inside + tile) * ORB_DEV * 8 + 8 * orbital
                tall[row : row + 8, :] = box[:, tile * LANES : (tile + 1) * LANES]
        for tile in range(k * inside, (k + 1) * inside):
            for z in range(8):
                row = tile * ORB_DEV * 8 + z
                packed[tile, z] = tall[pl.ds(row, ORB_DEV, stride=8), :].astype(jnp.bfloat16)
            packed[tile, 8] = placed
        at = pl.ds(k * inside, inside)
        out.append(pltpu.make_async_copy(packed.at[at], pieces.at[at], sent.at[k]))
        out[k].start()
    for copy in out:
        copy.wait()


def dot_rows(one, two):
    return lax.dot_general(one, two, (((1,), (1,)), ((), ())), preferred_element_type=jnp.float32)


def chosen(column):
    lane = lax.broadcasted_iota(jnp.int32, (N_DEV, LANES), 1).astype(jnp.float32)
    hits = [jnp.where(column == lane + half * LANES, 1.0, 0.0) for half in range(2)]
    return jnp.concatenate(hits, axis=1).astype(jnp.bfloat16)


def place_kernel(count, owner, local, place, second, choose):
    shape = (4, LANES)
    slot = lax.broadcasted_iota(jnp.int32, shape, 0) * LANES + lax.broadcasted_iota(jnp.int32, shape, 1)
    orb, rank = slot // PAIR_DEV, slot % PAIR_DEV
    before, live = jnp.zeros(shape, jnp.int32), jnp.zeros(shape, jnp.int32)
    for e in range(N_ORB):
        before = before + jnp.where(orb > e, count[e], 0)
        live = jnp.where(orb == e, count[e], live)
    rank = jnp.where(rank < live, before + rank, -1).astype(jnp.float32)
    pair = lax.broadcasted_iota(jnp.int32, (N_DEV, LANES), 0).astype(jnp.float32)
    second[...] = (owner[...] * ORB_DEV + local[...]).astype(jnp.float32)
    for k in range(4):
        at = slice(k * LANES, (k + 1) * LANES)
        place[:, at] = jnp.where(pair == rank[k : k + 1], 1.0, 0.0).astype(jnp.bfloat16)
    rows = jnp.concatenate([second[k : k + 1, :] for k in range(4)], axis=1)
    rows = jnp.broadcast_to(rows, (LANES, 4 * LANES)).astype(jnp.bfloat16)
    choose[...] = chosen(dot_rows(place[...], rows))


def pick_kernel(me, place, second, choose, pieces, picked, index, mine, tall):
    blocks = []
    for k in range(4):
        block = jnp.sum(pieces[8 * k : 8 * k + 8, 8].astype(jnp.float32), axis=0)
        row = lax.broadcasted_iota(jnp.int32, (8, LANES), 0)
        lane = lax.broadcasted_iota(jnp.int32, (8, LANES), 1)
        orbital = (8 * (8 * k + lane // PAIR_DEV)).astype(jnp.float32)
        block = jnp.where(row == 0, block + orbital, block)
        blocks.append(jnp.where(row == 3, jnp.broadcast_to(second[k : k + 1, :], (8, LANES)), block))
    facts = jnp.concatenate(blocks, axis=1)
    first = jnp.broadcast_to(facts[0:1], (LANES, 4 * LANES)).astype(jnp.bfloat16)
    choose_first = chosen(dot_rows(place[...], first))
    known = dot_rows(facts.astype(jnp.bfloat16), place[...])
    index[0:1, :] = known[0:1].astype(jnp.int32)
    index[1:2, :] = known[3:4].astype(jnp.int32)
    lane = lax.broadcasted_iota(jnp.int32, (8, N_DEV), 1)
    here = jnp.sum(jnp.where(lane == me[0], known, 0.0), axis=1, keepdims=True)
    lane = lax.broadcasted_iota(jnp.int32, (1, LANES), 1)
    mine[...] = jnp.where(lane == 0, here[1:2], here[2:3]).astype(jnp.int32)
    for z in range(0, 8, 2):
        field = [
            pieces[:, z + k].astype(jnp.float32).reshape(N_DEV, LANES).astype(jnp.bfloat16) for k in range(2)
        ]
        field = jnp.concatenate(field, axis=1)
        for side, picker in enumerate((choose_first, choose[...])):
            out = jnp.dot(picker, field, preferred_element_type=jnp.float32)
            tall[pl.ds(8 * side + z, N_DEV, stride=16), :] = out[:, :LANES]
            tall[pl.ds(8 * side + z + 1, N_DEV, stride=16), :] = out[:, LANES:]
    for k in range(0, N_DEV, 8):
        picked[k : k + 8] = tall[16 * k : 16 * k + 128, :].reshape(8, 16, LANES).astype(jnp.bfloat16)


def shifted(tiles, start, count, flat, shift_x, shift_y):
    lane = lax.broadcasted_iota(jnp.int32, (8, LANES), 1)
    whole, rest = flat // LANES, flat % LANES
    later = (lane >= rest)[None]
    y = lane % BOX - shift_y
    keep_y = (y >= 0) & (y < BOX)
    turned = [
        pltpu.roll(tiles((start + k - whole - 1 + 2 * TILES) % TILES), rest, 2) for k in range(count + 1)
    ]
    out = []
    for k in range(count):
        x = 2 * (start + k) + lane // BOX - shift_x
        keep = jnp.where(keep_y & (x >= 0) & (x < BOX), 1.0, 0.0)
        out.append(jnp.where(later, turned[k + 1], turned[k]) * keep[None])
    return out


def solve_kernel(shift, right, left, screen, boxes, terms, moved, field, other):
    shift_x, shift_y = shift[0, 0], shift[0, 1]
    full = BOX * BOX
    ahead = (shift_x * BOX + shift_y + full) % full
    back = (full - ahead) % full
    early = lax.broadcasted_iota(jnp.int32, (8, LANES), 1) < BOX
    sign = jnp.where(early, 1.0, -1.0)

    def first_tile(tile):
        return boxes[pl.ds(tile * 8, 8), :8, :].astype(jnp.float32)

    def second_tile(tile):
        return boxes[pl.ds(tile * 8, 8), 8:, :].astype(jnp.float32)

    def along_y(block):
        high, low = split(block)
        product = jnp.dot(
            jnp.concatenate([high, low], axis=1), right[...], preferred_element_type=jnp.float32
        )
        return product[:, :LANES] + product[:, LANES:]

    for start in range(0, TILES, 4):
        products = []
        for k, box in enumerate(shifted(second_tile, start, 4, ahead, shift_x, shift_y)):
            moved[start + k] = box
            products.append(first_tile(start + k) * box)
        block = along_y(jnp.stack(products).reshape(4 * BOX, LANES)).reshape(4, BOX, LANES)
        for k in range(4):
            field[start + k] = block[k]

    for row in range(0, BOX, 8):
        parts = twist(fast_hartley([field[k, row : row + 8, :] for k in range(TILES)]), early)
        for k in range(TILES):
            field[k, row : row + 8, :] = sign * parts[k] + pltpu.roll(parts[k], BOX, 1)

    def along_z(block):
        high, low = split(block)
        product = jnp.dot(
            left[...], jnp.concatenate([high, low], axis=0), preferred_element_type=jnp.float32
        )
        return product[:BOX] + product[BOX:]

    for tile in range(0, TILES, 2):
        block = along_z(jnp.concatenate([field[tile], field[tile + 1]], axis=1))
        block = block * jnp.concatenate([screen[tile], screen[tile + 1]], axis=1)
        block = along_z(block)
        field[tile] = block[:, :LANES]
        field[tile + 1] = block[:, LANES:]

    for row in range(0, BOX, 8):
        parts = [field[k, row : row + 8, :] for k in range(TILES)]
        parts = [sign * part + pltpu.roll(part, BOX, 1) for part in parts]
        parts = fast_hartley(untwist(parts, early))
        for k in range(TILES):
            field[k, row : row + 8, :] = parts[k]

    for start in range(0, TILES, 4):
        block = field[start : start + 4].reshape(4 * BOX, LANES)
        potential = along_y(block).reshape(4, 8, 8, LANES)
        for k in range(4):
            other[start + k] = potential[k] * first_tile(start + k)
            moved[start + k] = potential[k] * moved[start + k]

    for start in range(0, TILES, 4):
        carried = shifted(lambda tile: other[tile], start, 4, back, -shift_x, -shift_y)
        for k in range(4):
            both = jnp.concatenate([moved[start + k], carried[k]], axis=1)
            terms[(start + k) * 8 : (start + k + 1) * 8] = both.astype(jnp.bfloat16)


def sum_kernel(index, terms, pieces, tall, summed):
    for k in range(0, N_DEV, 8):
        tall[16 * k : 16 * k + 128, :] = terms[k : k + 8].astype(jnp.float32).reshape(128, LANES)
    orbital = lax.broadcasted_iota(jnp.int32, (N_DEV, N_DEV), 0)
    hits = [jnp.where(orbital == index[side : side + 1, :], 1.0, 0.0) for side in range(2)]
    hits = jnp.concatenate(hits, axis=1).astype(jnp.bfloat16)
    for z in range(0, 8, 2):
        field = [
            jnp.concatenate(
                [tall[pl.ds(8 * side + z + k, N_DEV, stride=16), :] for side in range(2)], axis=0
            ).astype(jnp.bfloat16)
            for k in range(2)
        ]
        out = jnp.dot(hits, jnp.concatenate(field, axis=1), preferred_element_type=jnp.float32)
        summed[pl.ds(z, N_DEV, stride=8), :] = out[:, :LANES]
        summed[pl.ds(z + 1, N_DEV, stride=8), :] = out[:, LANES:]
    for e in range(N_ORB):
        pieces[e] = summed[e * ORB_DEV * 8 : (e + 1) * ORB_DEV * 8, :].astype(jnp.bfloat16)


def join_kernel(pieces, result):
    for pair in range(ORB_DEV // 2):
        tiles = [pieces[tile, 16 * pair : 16 * pair + 16, :].astype(jnp.float32) for tile in range(TILES)]
        for side in range(2):
            rows = [tile[8 * side : 8 * side + 8] for tile in tiles]
            result[2 * pair + side] = jnp.concatenate(rows, axis=1).astype(jnp.bfloat16)


def body(orbitals, pair_first, second_owner, second_local, pair_shift, pair_count):
    f32, bf16, i32 = jnp.float32, jnp.bfloat16, jnp.int32
    shape = jax.ShapeDtypeStruct
    me = (lax.axis_index("orb") * 8 + lax.axis_index("slab")).reshape(1)
    rows = ORB_DEV * 8
    pair_shape = shape((N_DEV, 16, LANES), bf16)
    pieces = pl.pallas_call(
        spread_kernel, out_shape=shape((N_ORB, 9, ORB_DEV, LANES), bf16),
        in_specs=[WHOLE_H] * 3, out_specs=WHOLE_H,
        scratch_shapes=[
            pltpu.VMEM((GROUPS, ORB_DEV, 8, BOX * BOX // GROUPS), bf16),
            pltpu.VMEM((TILES * rows + 64, LANES), f32),
            pltpu.VMEM((16, PAIR_DEV), i32),
            pltpu.VMEM((8, LANES), f32),
            pltpu.VMEM((N_ORB, 9, ORB_DEV, LANES), bf16),
            pltpu.SemaphoreType.DMA((GROUPS + 2,)),
            pltpu.SemaphoreType.DMA((GROUPS,)),
        ],
        compiler_params=pltpu.CompilerParams(vmem_limit_bytes=60 * 1024 * 1024), name="spread",
    )(pair_first.reshape(1, PAIR_DEV), pair_shift.T, orbitals)
    pieces = lax.all_to_all(pieces, "orb", split_axis=0, concat_axis=0, tiled=True)
    place, second, choose = pl.pallas_call(
        place_kernel,
        out_shape=(shape((N_DEV, 4 * LANES), bf16), shape((4, LANES), f32), shape((N_DEV, N_DEV), bf16)),
        in_specs=[WHOLE_S, WHOLE_V, WHOLE_V], out_specs=(WHOLE_V,) * 3,
        compiler_params=PARAMS, name="place",
    )(pair_count, second_owner.reshape(4, LANES), second_local.reshape(4, LANES))
    picked, index, mine = pl.pallas_call(
        pick_kernel,
        out_shape=(pair_shape, shape((2, N_DEV), i32), shape((1, LANES), i32)),
        in_specs=[WHOLE_S] + [WHOLE_V] * 4,
        out_specs=(WHOLE_V,) * 3,
        scratch_shapes=[pltpu.VMEM((N_DEV * 16 + 16, LANES), f32)],
        compiler_params=PARAMS, name="pick",
    )(me, place, second, choose, pieces)
    boxes = lax.all_to_all(picked, ("orb", "slab"), split_axis=0, concat_axis=0, tiled=True)
    right, left, screen = (jnp.asarray(table) for table in tables())
    terms = pl.pallas_call(
        solve_kernel, out_shape=pair_shape,
        in_specs=[WHOLE_S] + [WHOLE_V] * 4,
        out_specs=WHOLE_V,
        scratch_shapes=[
            pltpu.VMEM((TILES, 8, 8, LANES), f32),
            pltpu.VMEM((TILES, BOX, LANES), f32),
            pltpu.VMEM((TILES, 8, 8, LANES), f32),
        ],
        compiler_params=PARAMS, name="solve",
    )(mine, right, left, screen, boxes)
    terms = lax.all_to_all(terms, ("orb", "slab"), split_axis=0, concat_axis=0, tiled=True)
    pieces = pl.pallas_call(
        sum_kernel, out_shape=shape((N_ORB, rows, LANES), bf16),
        in_specs=[WHOLE_V, WHOLE_V], out_specs=WHOLE_V,
        scratch_shapes=[pltpu.VMEM((N_DEV * 16 + 16, LANES), f32), pltpu.VMEM((N_DEV * 8 + 8, LANES), f32)],
        compiler_params=PARAMS, name="sum",
    )(index, terms)
    pieces = lax.all_to_all(pieces, "orb", split_axis=0, concat_axis=0, tiled=True)
    return pl.pallas_call(
        join_kernel, out_shape=shape((ORB_DEV, 8, BOX * BOX), bf16),
        in_specs=[WHOLE_V], out_specs=WHOLE_V,
        compiler_params=PARAMS, name="join",
    )(pieces)


def solution(mesh):
    in_specs = (P("orb", "slab", None), P("orb"), P(), P(), P("orb", None), P())
    out_specs = P("orb", "slab", None)
    return jax.shard_map(body, mesh=mesh, in_specs=in_specs, out_specs=out_specs, check_vma=False)
```

```python
import math

import jax
import jax.numpy as jnp
import numpy as np
from jax import lax
from jax.experimental import pallas as pl
from jax.experimental.pallas import tpu as pltpu
from jax.sharding import PartitionSpec as P

BOX = 64
ORB_DEV = 8
PAIR_DEV = 16
N_ORB = 32
N_DEV = 256
TILES = 32
LANES = 128
SCREENING = 0.02
GROUPS = 4
PARAMS = pltpu.CompilerParams(vmem_limit_bytes=48 * 1024 * 1024)
WHOLE_V = pl.BlockSpec(memory_space=pltpu.VMEM)
WHOLE_H = pl.BlockSpec(memory_space=pltpu.HBM)
WHOLE_S = pl.BlockSpec(memory_space=pltpu.SMEM)


def hartley_table():
    line = np.arange(BOX)
    angle = (line[:, None] * line[None, :] % BOX) * (2.0 * math.pi / BOX)
    return np.cos(angle) + np.sin(angle)


def halves(table):
    high = table.astype(np.float32).astype(jnp.bfloat16)
    low = (table - high.astype(np.float64)).astype(np.float32).astype(jnp.bfloat16)
    return high, low


def tables():
    high, low = halves(hartley_table())
    zero = np.zeros((BOX, BOX), high.dtype)

    def twice(table):
        return np.block([[table, zero], [zero, table]])

    right = np.block([[twice(high), twice(low)], [twice(high), np.zeros((128, 128), high.dtype)]])
    left = np.block([[high, high], [low, np.zeros((BOX, BOX), high.dtype)]])
    lam = 2.0 - 2.0 * np.cos(np.arange(BOX) * (2.0 * math.pi / BOX))
    lam_a = np.repeat(lam.reshape(2, TILES).T, BOX, axis=1)
    under = lam_a[:, None, :] + lam[None, :, None] + np.tile(lam, 2)[None, None, :] + SCREENING
    return right, left, (1.0 / BOX**3 / under).astype(np.float32)


def split(field):
    high = field.astype(jnp.bfloat16)
    low = (field - high.astype(jnp.float32)).astype(jnp.bfloat16)
    return high, low


def fast_hartley(parts):
    n = len(parts)
    if n == 1:
        return parts
    if n == 2:
        return [parts[0] + parts[1], parts[0] - parts[1]]
    even, odd = fast_hartley(parts[0::2]), fast_hartley(parts[1::2])
    m = n // 2
    out = [None] * n
    for k in range(m):
        if k == 0 or 4 * k == n:
            turned = odd[k]
        else:
            angle = 2.0 * math.pi * k / n
            turned = odd[k] * math.cos(angle) + odd[m - k] * math.sin(angle)
        out[k] = even[k] + turned
        out[k + m] = even[k] - turned
    return out


def twist(parts, first):
    out = []
    for k in range(TILES):
        mirror = parts[(TILES - k) % TILES]
        angle = 2.0 * math.pi * k / BOX
        if k == 0 or 2 * k == TILES:
            out.append(parts[k])
        else:
            out.append(jnp.where(first, parts[k], parts[k] * math.cos(angle) + mirror * math.sin(angle)))
    return out


def untwist(parts, first):
    out = []
    for k in range(TILES):
        mirror = parts[(TILES - k) % TILES]
        angle = 2.0 * math.pi * k / BOX
        back = 2.0 * math.pi * ((TILES - k) % TILES) / BOX
        if k == 0 or 2 * k == TILES:
            out.append(parts[k])
        else:
            out.append(jnp.where(first, parts[k], parts[k] * math.cos(angle) + mirror * math.sin(back)))
    return out


def spread_kernel(first, shift, orbitals, pieces, taken, tall, small, about, packed, arrived, sent):
    few = [
        pltpu.make_async_copy(first, small.at[0:1], arrived.at[GROUPS]),
        pltpu.make_async_copy(shift, small.at[8:10], arrived.at[GROUPS + 1]),
    ]
    width = BOX * BOX // GROUPS
    many = [
        pltpu.make_async_copy(orbitals.at[:, :, pl.ds(k * width, width)], taken.at[k], arrived.at[k])
        for k in range(GROUPS)
    ]
    for copy in few + many:
        copy.start()
    about[...] = jnp.zeros_like(about)
    for copy in few:
        copy.wait()
    about[0:1, :PAIR_DEV] = small[0:1, :].astype(jnp.float32)
    about[1:3, :PAIR_DEV] = small[8:10, :].astype(jnp.float32)
    placed = pltpu.roll(about[...], lax.axis_index("orb") % 8 * PAIR_DEV, 1).astype(jnp.bfloat16)
    inside = TILES // GROUPS
    out = []
    for k in range(GROUPS):
        many[k].wait()
        for orbital in range(ORB_DEV):
            box = taken[k, orbital].astype(jnp.float32)
            for tile in range(inside):
                row = (k * inside + tile) * ORB_DEV * 8 + 8 * orbital
                tall[row : row + 8, :] = box[:, tile * LANES : (tile + 1) * LANES]
        for tile in range(k * inside, (k + 1) * inside):
            for z in range(8):
                row = tile * ORB_DEV * 8 + z
                packed[tile, z] = tall[pl.ds(row, ORB_DEV, stride=8), :].astype(jnp.bfloat16)
            packed[tile, 8] = placed
        at = pl.ds(k * inside, inside)
        out.append(pltpu.make_async_copy(packed.at[at], pieces.at[at], sent.at[k]))
        out[k].start()
    for copy in out:
        copy.wait()


def dot_rows(one, two):
    return lax.dot_general(one, two, (((1,), (1,)), ((), ())), preferred_element_type=jnp.float32)


def chosen(column):
    lane = lax.broadcasted_iota(jnp.int32, (N_DEV, LANES), 1).astype(jnp.float32)
    hits = [jnp.where(column == lane + half * LANES, 1.0, 0.0) for half in range(2)]
    return jnp.concatenate(hits, axis=1).astype(jnp.bfloat16)


def place_kernel(count, owner, local, place, second, choose):
    shape = (4, LANES)
    slot = lax.broadcasted_iota(jnp.int32, shape, 0) * LANES + lax.broadcasted_iota(jnp.int32, shape, 1)
    orb, rank = slot // PAIR_DEV, slot % PAIR_DEV
    before, live = jnp.zeros(shape, jnp.int32), jnp.zeros(shape, jnp.int32)
    for e in range(N_ORB):
        before = before + jnp.where(orb > e, count[e], 0)
        live = jnp.where(orb == e, count[e], live)
    rank = jnp.where(rank < live, before + rank, -1).astype(jnp.float32)
    pair = lax.broadcasted_iota(jnp.int32, (N_DEV, LANES), 0).astype(jnp.float32)
    second[...] = (owner[...] * ORB_DEV + local[...]).astype(jnp.float32)
    for k in range(4):
        at = slice(k * LANES, (k + 1) * LANES)
        place[:, at] = jnp.where(pair == rank[k : k + 1], 1.0, 0.0).astype(jnp.bfloat16)
    rows = jnp.concatenate([second[k : k + 1, :] for k in range(4)], axis=1)
    rows = jnp.broadcast_to(rows, (LANES, 4 * LANES)).astype(jnp.bfloat16)
    choose[...] = chosen(dot_rows(place[...], rows))


def pick_kernel(place, second, choose, pieces, picked, index, mine, tall):
    blocks = []
    for k in range(4):
        block = jnp.sum(pieces[8 * k : 8 * k + 8, 8].astype(jnp.float32), axis=0)
        row = lax.broadcasted_iota(jnp.int32, (8, LANES), 0)
        lane = lax.broadcasted_iota(jnp.int32, (8, LANES), 1)
        orbital = (8 * (8 * k + lane // PAIR_DEV)).astype(jnp.float32)
        block = jnp.where(row == 0, block + orbital, block)
        blocks.append(jnp.where(row == 3, jnp.broadcast_to(second[k : k + 1, :], (8, LANES)), block))
    facts = jnp.concatenate(blocks, axis=1)
    first = jnp.broadcast_to(facts[0:1], (LANES, 4 * LANES)).astype(jnp.bfloat16)
    choose_first = chosen(dot_rows(place[...], first))
    known = dot_rows(facts.astype(jnp.bfloat16), place[...])
    index[0:1, :] = known[0:1].astype(jnp.int32)
    index[1:2, :] = known[3:4].astype(jnp.int32)
    lane = lax.broadcasted_iota(jnp.int32, (8, N_DEV), 1)
    me = lax.axis_index("orb") * 8 + lax.axis_index("slab")
    here = jnp.sum(jnp.where(lane == me, known, 0.0), axis=1, keepdims=True)
    lane = lax.broadcasted_iota(jnp.int32, (1, LANES), 1)
    mine[...] = jnp.where(lane == 0, here[1:2], here[2:3])
    for z in range(0, 8, 2):
        field = [
            pieces[:, z + k].astype(jnp.float32).reshape(N_DEV, LANES).astype(jnp.bfloat16) for k in range(2)
        ]
        field = jnp.concatenate(field, axis=1)
        for side, picker in enumerate((choose_first, choose[...])):
            out = jnp.dot(picker, field, preferred_element_type=jnp.float32)
            tall[pl.ds(8 * side + z, N_DEV, stride=16), :] = out[:, :LANES]
            tall[pl.ds(8 * side + z + 1, N_DEV, stride=16), :] = out[:, LANES:]
    for k in range(0, N_DEV, 8):
        picked[k : k + 8] = tall[16 * k : 16 * k + 128, :].reshape(8, 16, LANES).astype(jnp.bfloat16)


def shifted(tiles, start, count, flat, shift_x, shift_y):
    lane = lax.broadcasted_iota(jnp.int32, (8, LANES), 1)
    whole, rest = flat // LANES, flat % LANES
    later = (lane >= rest)[None]
    y = lane % BOX - shift_y
    keep_y = (y >= 0) & (y < BOX)
    turned = [
        pltpu.roll(tiles((start + k - whole - 1 + 2 * TILES) % TILES), rest, 2) for k in range(count + 1)
    ]
    out = []
    for k in range(count):
        x = 2 * (start + k) + lane // BOX - shift_x
        keep = jnp.where(keep_y & (x >= 0) & (x < BOX), 1.0, 0.0)
        out.append(jnp.where(later, turned[k + 1], turned[k]) * keep[None])
    return out


def solve_kernel(shift, right, left, screen, boxes, terms, moved, field, other):
    lane = lax.broadcasted_iota(jnp.int32, (1, LANES), 1)
    shift_x, shift_y = (jnp.sum(jnp.where(lane == k, shift[...], 0.0)).astype(jnp.int32) for k in range(2))
    full = BOX * BOX
    ahead = (shift_x * BOX + shift_y + full) % full
    back = (full - ahead) % full
    early = lax.broadcasted_iota(jnp.int32, (8, LANES), 1) < BOX
    sign = jnp.where(early, 1.0, -1.0)

    def first_tile(tile):
        return boxes[pl.ds(tile * 8, 8), :8, :].astype(jnp.float32)

    def second_tile(tile):
        return boxes[pl.ds(tile * 8, 8), 8:, :].astype(jnp.float32)

    def along_y(block):
        high, low = split(block)
        product = jnp.dot(
            jnp.concatenate([high, low], axis=1), right[...], preferred_element_type=jnp.float32
        )
        return product[:, :LANES] + product[:, LANES:]

    for start in range(0, TILES, 4):
        products = []
        for k, box in enumerate(shifted(second_tile, start, 4, ahead, shift_x, shift_y)):
            moved[start + k] = box
            products.append(first_tile(start + k) * box)
        block = along_y(jnp.stack(products).reshape(4 * BOX, LANES)).reshape(4, BOX, LANES)
        for k in range(4):
            field[start + k] = block[k]

    for row in range(0, BOX, 8):
        parts = twist(fast_hartley([field[k, row : row + 8, :] for k in range(TILES)]), early)
        for k in range(TILES):
            field[k, row : row + 8, :] = sign * parts[k] + pltpu.roll(parts[k], BOX, 1)

    def along_z(block):
        high, low = split(block)
        product = jnp.dot(
            left[...], jnp.concatenate([high, low], axis=0), preferred_element_type=jnp.float32
        )
        return product[:BOX] + product[BOX:]

    for tile in range(0, TILES, 2):
        block = along_z(jnp.concatenate([field[tile], field[tile + 1]], axis=1))
        block = block * jnp.concatenate([screen[tile], screen[tile + 1]], axis=1)
        block = along_z(block)
        field[tile] = block[:, :LANES]
        field[tile + 1] = block[:, LANES:]

    for row in range(0, BOX, 8):
        parts = [field[k, row : row + 8, :] for k in range(TILES)]
        parts = [sign * part + pltpu.roll(part, BOX, 1) for part in parts]
        parts = fast_hartley(untwist(parts, early))
        for k in range(TILES):
            field[k, row : row + 8, :] = parts[k]

    for start in range(0, TILES, 4):
        block = field[start : start + 4].reshape(4 * BOX, LANES)
        potential = along_y(block).reshape(4, 8, 8, LANES)
        for k in range(4):
            other[start + k] = potential[k] * first_tile(start + k)
            moved[start + k] = potential[k] * moved[start + k]

    for start in range(0, TILES, 4):
        carried = shifted(lambda tile: other[tile], start, 4, back, -shift_x, -shift_y)
        for k in range(4):
            both = jnp.concatenate([moved[start + k], carried[k]], axis=1)
            terms[(start + k) * 8 : (start + k + 1) * 8] = both.astype(jnp.bfloat16)


def sum_kernel(index, terms, pieces, tall, summed):
    for k in range(0, N_DEV, 8):
        tall[16 * k : 16 * k + 128, :] = terms[k : k + 8].astype(jnp.float32).reshape(128, LANES)
    orbital = lax.broadcasted_iota(jnp.int32, (N_DEV, N_DEV), 0)
    hits = [jnp.where(orbital == index[side : side + 1, :], 1.0, 0.0) for side in range(2)]
    hits = jnp.concatenate(hits, axis=1).astype(jnp.bfloat16)
    for z in range(0, 8, 2):
        field = [
            jnp.concatenate(
                [tall[pl.ds(8 * side + z + k, N_DEV, stride=16), :] for side in range(2)], axis=0
            ).astype(jnp.bfloat16)
            for k in range(2)
        ]
        out = jnp.dot(hits, jnp.concatenate(field, axis=1), preferred_element_type=jnp.float32)
        summed[pl.ds(z, N_DEV, stride=8), :] = out[:, :LANES]
        summed[pl.ds(z + 1, N_DEV, stride=8), :] = out[:, LANES:]
    for e in range(N_ORB):
        pieces[e] = summed[e * ORB_DEV * 8 : (e + 1) * ORB_DEV * 8, :].astype(jnp.bfloat16)


def join_kernel(pieces, result):
    for pair in range(ORB_DEV // 2):
        tiles = [pieces[tile, 16 * pair : 16 * pair + 16, :].astype(jnp.float32) for tile in range(TILES)]
        for side in range(2):
            rows = [tile[8 * side : 8 * side + 8] for tile in tiles]
            result[2 * pair + side] = jnp.concatenate(rows, axis=1).astype(jnp.bfloat16)


def body(orbitals, pair_first, second_owner, second_local, pair_shift, pair_count):
    f32, bf16, i32 = jnp.float32, jnp.bfloat16, jnp.int32
    shape = jax.ShapeDtypeStruct
    rows = ORB_DEV * 8
    pair_shape = shape((N_DEV, 16, LANES), bf16)
    pieces = pl.pallas_call(
        spread_kernel, out_shape=shape((N_ORB, 9, ORB_DEV, LANES), bf16),
        in_specs=[WHOLE_H] * 3, out_specs=WHOLE_H,
        scratch_shapes=[
            pltpu.VMEM((GROUPS, ORB_DEV, 8, BOX * BOX // GROUPS), bf16),
            pltpu.VMEM((TILES * rows + 64, LANES), f32),
            pltpu.VMEM((16, PAIR_DEV), i32),
            pltpu.VMEM((8, LANES), f32),
            pltpu.VMEM((N_ORB, 9, ORB_DEV, LANES), bf16),
            pltpu.SemaphoreType.DMA((GROUPS + 2,)),
            pltpu.SemaphoreType.DMA((GROUPS,)),
        ],
        compiler_params=pltpu.CompilerParams(vmem_limit_bytes=60 * 1024 * 1024), name="spread",
    )(pair_first.reshape(1, PAIR_DEV), pair_shift.T, orbitals)
    pieces = lax.all_to_all(pieces, "orb", split_axis=0, concat_axis=0, tiled=True)
    place, second, choose = pl.pallas_call(
        place_kernel,
        out_shape=(shape((N_DEV, 4 * LANES), bf16), shape((4, LANES), f32), shape((N_DEV, N_DEV), bf16)),
        in_specs=[WHOLE_S, WHOLE_V, WHOLE_V], out_specs=(WHOLE_V,) * 3,
        compiler_params=PARAMS, name="place",
    )(pair_count, second_owner.reshape(4, LANES), second_local.reshape(4, LANES))
    picked, index, mine = pl.pallas_call(
        pick_kernel,
        out_shape=(pair_shape, shape((2, N_DEV), i32), shape((1, LANES), f32)),
        in_specs=[WHOLE_V] * 4,
        out_specs=(WHOLE_V,) * 3,
        scratch_shapes=[pltpu.VMEM((N_DEV * 16 + 16, LANES), f32)],
        compiler_params=PARAMS, name="pick",
    )(place, second, choose, pieces)
    boxes = lax.all_to_all(picked, ("orb", "slab"), split_axis=0, concat_axis=0, tiled=True)
    right, left, screen = (jnp.asarray(table) for table in tables())
    terms = pl.pallas_call(
        solve_kernel, out_shape=pair_shape,
        in_specs=[WHOLE_V] * 5,
        out_specs=WHOLE_V,
        scratch_shapes=[
            pltpu.VMEM((TILES, 8, 8, LANES), f32),
            pltpu.VMEM((TILES, BOX, LANES), f32),
            pltpu.VMEM((TILES, 8, 8, LANES), f32),
        ],
        compiler_params=PARAMS, name="solve",
    )(mine, right, left, screen, boxes)
    terms = lax.all_to_all(terms, ("orb", "slab"), split_axis=0, concat_axis=0, tiled=True)
    pieces = pl.pallas_call(
        sum_kernel, out_shape=shape((N_ORB, rows, LANES), bf16),
        in_specs=[WHOLE_V, WHOLE_V], out_specs=WHOLE_V,
        scratch_shapes=[pltpu.VMEM((N_DEV * 16 + 16, LANES), f32), pltpu.VMEM((N_DEV * 8 + 8, LANES), f32)],
        compiler_params=PARAMS, name="sum",
    )(index, terms)
    pieces = lax.all_to_all(pieces, "orb", split_axis=0, concat_axis=0, tiled=True)
    return pl.pallas_call(
        join_kernel, out_shape=shape((ORB_DEV, 8, BOX * BOX), bf16),
        in_specs=[WHOLE_V], out_specs=WHOLE_V,
        compiler_params=PARAMS, name="join",
    )(pieces)


def solution(mesh):
    in_specs = (P("orb", "slab", None), P("orb"), P(), P(), P("orb", None), P())
    out_specs = P("orb", "slab", None)
    return jax.shard_map(body, mesh=mesh, in_specs=in_specs, out_specs=out_specs, check_vma=False)
```

```python
import math

import jax
import jax.numpy as jnp
import numpy as np
from jax import lax
from jax.experimental import pallas as pl
from jax.experimental.pallas import tpu as pltpu
from jax.sharding import PartitionSpec as P

BOX = 64
ORB_DEV = 8
PAIR_DEV = 16
N_ORB = 32
N_DEV = 256
TILES = 32
LANES = 128
SCREENING = 0.02
GROUPS = 4
PARAMS = pltpu.CompilerParams(vmem_limit_bytes=48 * 1024 * 1024)
WHOLE_V = pl.BlockSpec(memory_space=pltpu.VMEM)
WHOLE_H = pl.BlockSpec(memory_space=pltpu.HBM)
WHOLE_S = pl.BlockSpec(memory_space=pltpu.SMEM)


def hartley_table():
    line = np.arange(BOX)
    angle = (line[:, None] * line[None, :] % BOX) * (2.0 * math.pi / BOX)
    return np.cos(angle) + np.sin(angle)


def halves(table):
    high = table.astype(np.float32).astype(jnp.bfloat16)
    low = (table - high.astype(np.float64)).astype(np.float32).astype(jnp.bfloat16)
    return high, low


def tables():
    high, low = halves(hartley_table())
    zero = np.zeros((BOX, BOX), high.dtype)

    def twice(table):
        return np.block([[table, zero], [zero, table]])

    right = np.block([[twice(high), twice(low)], [twice(high), np.zeros((128, 128), high.dtype)]])
    left = np.block([[high, high], [low, np.zeros((BOX, BOX), high.dtype)]])
    lam = 2.0 - 2.0 * np.cos(np.arange(BOX) * (2.0 * math.pi / BOX))
    lam_a = np.repeat(lam.reshape(2, TILES).T, BOX, axis=1)
    under = lam_a[:, None, :] + lam[None, :, None] + np.tile(lam, 2)[None, None, :] + SCREENING
    return right, left, (1.0 / BOX**3 / under).astype(np.float32)


def split(field):
    high = field.astype(jnp.bfloat16)
    low = (field - high.astype(jnp.float32)).astype(jnp.bfloat16)
    return high, low


def fast_hartley(parts):
    n = len(parts)
    if n == 1:
        return parts
    if n == 2:
        return [parts[0] + parts[1], parts[0] - parts[1]]
    even, odd = fast_hartley(parts[0::2]), fast_hartley(parts[1::2])
    m = n // 2
    out = [None] * n
    for k in range(m):
        if k == 0 or 4 * k == n:
            turned = odd[k]
        else:
            angle = 2.0 * math.pi * k / n
            turned = odd[k] * math.cos(angle) + odd[m - k] * math.sin(angle)
        out[k] = even[k] + turned
        out[k + m] = even[k] - turned
    return out


def twist(parts, first):
    out = []
    for k in range(TILES):
        mirror = parts[(TILES - k) % TILES]
        angle = 2.0 * math.pi * k / BOX
        if k == 0 or 2 * k == TILES:
            out.append(parts[k])
        else:
            out.append(jnp.where(first, parts[k], parts[k] * math.cos(angle) + mirror * math.sin(angle)))
    return out


def untwist(parts, first):
    out = []
    for k in range(TILES):
        mirror = parts[(TILES - k) % TILES]
        angle = 2.0 * math.pi * k / BOX
        back = 2.0 * math.pi * ((TILES - k) % TILES) / BOX
        if k == 0 or 2 * k == TILES:
            out.append(parts[k])
        else:
            out.append(jnp.where(first, parts[k], parts[k] * math.cos(angle) + mirror * math.sin(back)))
    return out


def spread_kernel(first, shift, orbitals, pieces, taken, tall, small, about, packed, arrived, sent):
    few = [
        pltpu.make_async_copy(first, small.at[0:1], arrived.at[GROUPS]),
        pltpu.make_async_copy(shift, small.at[8:10], arrived.at[GROUPS + 1]),
    ]
    width = BOX * BOX // GROUPS
    many = [
        pltpu.make_async_copy(orbitals.at[:, :, pl.ds(k * width, width)], taken.at[k], arrived.at[k])
        for k in range(GROUPS)
    ]
    for copy in few + many:
        copy.start()
    about[...] = jnp.zeros_like(about)
    for copy in few:
        copy.wait()
    about[0:1, :PAIR_DEV] = small[0:1, :].astype(jnp.float32)
    about[1:3, :PAIR_DEV] = small[8:10, :].astype(jnp.float32)
    placed = pltpu.roll(about[...], lax.axis_index("orb") % 8 * PAIR_DEV, 1).astype(jnp.bfloat16)
    inside = TILES // GROUPS
    out = []
    for k in range(GROUPS):
        many[k].wait()
        for orbital in range(ORB_DEV):
            box = taken[k, orbital].astype(jnp.float32)
            for tile in range(inside):
                row = (k * inside + tile) * ORB_DEV * 8 + 8 * orbital
                tall[row : row + 8, :] = box[:, tile * LANES : (tile + 1) * LANES]
        for tile in range(k * inside, (k + 1) * inside):
            for z in range(8):
                row = tile * ORB_DEV * 8 + z
                packed[tile, z] = tall[pl.ds(row, ORB_DEV, stride=8), :].astype(jnp.bfloat16)
            packed[tile, 8] = placed
        at = pl.ds(k * inside, inside)
        out.append(pltpu.make_async_copy(packed.at[at], pieces.at[at], sent.at[k]))
        out[k].start()
    for copy in out:
        copy.wait()


def dot_rows(one, two):
    return lax.dot_general(one, two, (((1,), (1,)), ((), ())), preferred_element_type=jnp.float32)


def chosen(column):
    lane = lax.broadcasted_iota(jnp.int32, (N_DEV, LANES), 1).astype(jnp.float32)
    hits = [jnp.where(column == lane + half * LANES, 1.0, 0.0) for half in range(2)]
    return jnp.concatenate(hits, axis=1).astype(jnp.bfloat16)


def place_kernel(count, owner, local, place, second, choose):
    shape = (4, LANES)
    slot = lax.broadcasted_iota(jnp.int32, shape, 0) * LANES + lax.broadcasted_iota(jnp.int32, shape, 1)
    orb, rank = slot // PAIR_DEV, slot % PAIR_DEV
    before, live = jnp.zeros(shape, jnp.int32), jnp.zeros(shape, jnp.int32)
    for e in range(N_ORB):
        before = before + jnp.where(orb > e, count[e], 0)
        live = jnp.where(orb == e, count[e], live)
    rank = jnp.where(rank < live, before + rank, -1).astype(jnp.float32)
    pair = lax.broadcasted_iota(jnp.int32, (N_DEV, LANES), 0).astype(jnp.float32)
    second[...] = (owner[...] * ORB_DEV + local[...]).astype(jnp.float32)
    for k in range(4):
        at = slice(k * LANES, (k + 1) * LANES)
        place[:, at] = jnp.where(pair == rank[k : k + 1], 1.0, 0.0).astype(jnp.bfloat16)
    rows = jnp.concatenate([second[k : k + 1, :] for k in range(4)], axis=1)
    rows = jnp.broadcast_to(rows, (LANES, 4 * LANES)).astype(jnp.bfloat16)
    choose[...] = chosen(dot_rows(place[...], rows))


def pick_kernel(place, second, choose, pieces, picked, index, mine, tall):
    blocks = []
    for k in range(4):
        block = jnp.sum(pieces[8 * k : 8 * k + 8, 8].astype(jnp.float32), axis=0)
        row = lax.broadcasted_iota(jnp.int32, (8, LANES), 0)
        lane = lax.broadcasted_iota(jnp.int32, (8, LANES), 1)
        orbital = (8 * (8 * k + lane // PAIR_DEV)).astype(jnp.float32)
        block = jnp.where(row == 0, block + orbital, block)
        blocks.append(jnp.where(row == 3, jnp.broadcast_to(second[k : k + 1, :], (8, LANES)), block))
    facts = jnp.concatenate(blocks, axis=1)
    first = jnp.broadcast_to(facts[0:1], (LANES, 4 * LANES)).astype(jnp.bfloat16)
    choose_first = chosen(dot_rows(place[...], first))
    known = dot_rows(facts.astype(jnp.bfloat16), place[...])
    index[0:1, :] = known[0:1].astype(jnp.int32)
    index[1:2, :] = known[3:4].astype(jnp.int32)
    lane = lax.broadcasted_iota(jnp.int32, (8, N_DEV), 1)
    me = lax.axis_index("orb") * 8 + lax.axis_index("slab")
    here = jnp.sum(jnp.where(lane == me, known, 0.0), axis=1, keepdims=True)
    lane = lax.broadcasted_iota(jnp.int32, (1, LANES), 1)
    mine[...] = jnp.where(lane == 0, here[1:2], here[2:3])
    for z in range(0, 8, 2):
        field = [
            pieces[:, z + k].astype(jnp.float32).reshape(N_DEV, LANES).astype(jnp.bfloat16) for k in range(2)
        ]
        field = jnp.concatenate(field, axis=1)
        for side, picker in enumerate((choose_first, choose[...])):
            out = jnp.dot(picker, field, preferred_element_type=jnp.float32)
            tall[pl.ds(8 * side + z, N_DEV, stride=16), :] = out[:, :LANES]
            tall[pl.ds(8 * side + z + 1, N_DEV, stride=16), :] = out[:, LANES:]
    for k in range(0, N_DEV, 8):
        picked[k : k + 8] = tall[16 * k : 16 * k + 128, :].reshape(8, 16, LANES).astype(jnp.bfloat16)


def shifted(tiles, start, count, flat, shift_x, shift_y):
    lane = lax.broadcasted_iota(jnp.int32, (8, LANES), 1)
    whole, rest = flat // LANES, flat % LANES
    later = (lane >= rest)[None]
    y = lane % BOX - shift_y
    keep_y = (y >= 0) & (y < BOX)
    turned = [
        pltpu.roll(tiles((start + k - whole - 1 + 2 * TILES) % TILES), rest, 2) for k in range(count + 1)
    ]
    out = []
    for k in range(count):
        x = 2 * (start + k) + lane // BOX - shift_x
        keep = jnp.where(keep_y & (x >= 0) & (x < BOX), 1.0, 0.0)
        out.append(jnp.where(later, turned[k + 1], turned[k]) * keep[None])
    return out


def solve_kernel(shift, right, left, screen, boxes, terms, moved, field, other):
    lane = lax.broadcasted_iota(jnp.int32, (1, LANES), 1)
    shift_x, shift_y = (jnp.sum(jnp.where(lane == k, shift[...], 0.0)).astype(jnp.int32) for k in range(2))
    full = BOX * BOX
    ahead = (shift_x * BOX + shift_y + full) % full
    back = (full - ahead) % full
    early = lax.broadcasted_iota(jnp.int32, (8, LANES), 1) < BOX
    sign = jnp.where(early, 1.0, -1.0)

    def first_tile(tile):
        return boxes[pl.ds(tile * 8, 8), :8, :].astype(jnp.float32)

    def second_tile(tile):
        return boxes[pl.ds(tile * 8, 8), 8:, :].astype(jnp.float32)

    def along_y(block):
        high, low = split(block)
        product = jnp.dot(
            jnp.concatenate([high, low], axis=1), right[...], preferred_element_type=jnp.float32
        )
        return product[:, :LANES] + product[:, LANES:]

    for start in range(0, TILES, 4):
        products = []
        for k, box in enumerate(shifted(second_tile, start, 4, ahead, shift_x, shift_y)):
            moved[start + k] = box
            products.append(first_tile(start + k) * box)
        block = along_y(jnp.stack(products).reshape(4 * BOX, LANES)).reshape(4, BOX, LANES)
        for k in range(4):
            field[start + k] = block[k]

    for row in range(0, BOX, 8):
        parts = twist(fast_hartley([field[k, row : row + 8, :] for k in range(TILES)]), early)
        for k in range(TILES):
            field[k, row : row + 8, :] = sign * parts[k] + pltpu.roll(parts[k], BOX, 1)

    def along_z(block):
        high, low = split(block)
        product = jnp.dot(
            left[...], jnp.concatenate([high, low], axis=0), preferred_element_type=jnp.float32
        )
        return product[:BOX] + product[BOX:]

    for tile in range(0, TILES, 2):
        block = along_z(jnp.concatenate([field[tile], field[tile + 1]], axis=1))
        block = block * jnp.concatenate([screen[tile], screen[tile + 1]], axis=1)
        block = along_z(block)
        field[tile] = block[:, :LANES]
        field[tile + 1] = block[:, LANES:]

    for row in range(0, BOX, 8):
        parts = [field[k, row : row + 8, :] for k in range(TILES)]
        parts = [sign * part + pltpu.roll(part, BOX, 1) for part in parts]
        parts = fast_hartley(untwist(parts, early))
        for k in range(TILES):
            field[k, row : row + 8, :] = parts[k]

    for start in range(0, TILES, 4):
        block = field[start : start + 4].reshape(4 * BOX, LANES)
        potential = along_y(block).reshape(4, 8, 8, LANES)
        for k in range(4):
            other[start + k] = potential[k] * first_tile(start + k)
            moved[start + k] = potential[k] * moved[start + k]

    for start in range(0, TILES, 4):
        carried = shifted(lambda tile: other[tile], start, 4, back, -shift_x, -shift_y)
        for k in range(4):
            both = jnp.concatenate([moved[start + k], carried[k]], axis=1)
            terms[(start + k) * 8 : (start + k + 1) * 8] = both.astype(jnp.bfloat16)


def sum_kernel(index, terms, pieces, tall, summed):
    for k in range(0, N_DEV, 8):
        tall[16 * k : 16 * k + 128, :] = terms[k : k + 8].astype(jnp.float32).reshape(128, LANES)
    orbital = lax.broadcasted_iota(jnp.int32, (N_DEV, N_DEV), 0)
    hits = [jnp.where(orbital == index[side : side + 1, :], 1.0, 0.0) for side in range(2)]
    hits = jnp.concatenate(hits, axis=1).astype(jnp.bfloat16)
    for z in range(0, 8, 2):
        field = [
            jnp.concatenate(
                [tall[pl.ds(8 * side + z + k, N_DEV, stride=16), :] for side in range(2)], axis=0
            ).astype(jnp.bfloat16)
            for k in range(2)
        ]
        out = jnp.dot(hits, jnp.concatenate(field, axis=1), preferred_element_type=jnp.float32)
        summed[pl.ds(z, N_DEV, stride=8), :] = out[:, :LANES]
        summed[pl.ds(z + 1, N_DEV, stride=8), :] = out[:, LANES:]
    for e in range(N_ORB):
        pieces[e] = summed[e * ORB_DEV * 8 : (e + 1) * ORB_DEV * 8, :].astype(jnp.bfloat16)


def join_kernel(pieces, result):
    for orbital in range(ORB_DEV):
        rows = slice(8 * orbital, 8 * orbital + 8)
        for tile in range(TILES):
            result[orbital, :, tile * LANES : (tile + 1) * LANES] = pieces[tile, rows, :]


def body(orbitals, pair_first, second_owner, second_local, pair_shift, pair_count):
    f32, bf16, i32 = jnp.float32, jnp.bfloat16, jnp.int32
    shape = jax.ShapeDtypeStruct
    rows = ORB_DEV * 8
    pair_shape = shape((N_DEV, 16, LANES), bf16)
    pieces = pl.pallas_call(
        spread_kernel, out_shape=shape((N_ORB, 9, ORB_DEV, LANES), bf16),
        in_specs=[WHOLE_H] * 3, out_specs=WHOLE_H,
        scratch_shapes=[
            pltpu.VMEM((GROUPS, ORB_DEV, 8, BOX * BOX // GROUPS), bf16),
            pltpu.VMEM((TILES * rows + 64, LANES), f32),
            pltpu.VMEM((16, PAIR_DEV), i32),
            pltpu.VMEM((8, LANES), f32),
            pltpu.VMEM((N_ORB, 9, ORB_DEV, LANES), bf16),
            pltpu.SemaphoreType.DMA((GROUPS + 2,)),
            pltpu.SemaphoreType.DMA((GROUPS,)),
        ],
        compiler_params=pltpu.CompilerParams(vmem_limit_bytes=60 * 1024 * 1024), name="spread",
    )(pair_first.reshape(1, PAIR_DEV), pair_shift.T, orbitals)
    pieces = lax.all_to_all(pieces, "orb", split_axis=0, concat_axis=0, tiled=True)
    place, second, choose = pl.pallas_call(
        place_kernel,
        out_shape=(shape((N_DEV, 4 * LANES), bf16), shape((4, LANES), f32), shape((N_DEV, N_DEV), bf16)),
        in_specs=[WHOLE_S, WHOLE_V, WHOLE_V], out_specs=(WHOLE_V,) * 3,
        compiler_params=PARAMS, name="place",
    )(pair_count, second_owner.reshape(4, LANES), second_local.reshape(4, LANES))
    picked, index, mine = pl.pallas_call(
        pick_kernel,
        out_shape=(pair_shape, shape((2, N_DEV), i32), shape((1, LANES), f32)),
        in_specs=[WHOLE_V] * 4,
        out_specs=(WHOLE_V,) * 3,
        scratch_shapes=[pltpu.VMEM((N_DEV * 16 + 16, LANES), f32)],
        compiler_params=PARAMS, name="pick",
    )(place, second, choose, pieces)
    boxes = lax.all_to_all(picked, ("orb", "slab"), split_axis=0, concat_axis=0, tiled=True)
    right, left, screen = (jnp.asarray(table) for table in tables())
    terms = pl.pallas_call(
        solve_kernel, out_shape=pair_shape,
        in_specs=[WHOLE_V] * 5,
        out_specs=WHOLE_V,
        scratch_shapes=[
            pltpu.VMEM((TILES, 8, 8, LANES), f32),
            pltpu.VMEM((TILES, BOX, LANES), f32),
            pltpu.VMEM((TILES, 8, 8, LANES), f32),
        ],
        compiler_params=PARAMS, name="solve",
    )(mine, right, left, screen, boxes)
    terms = lax.all_to_all(terms, ("orb", "slab"), split_axis=0, concat_axis=0, tiled=True)
    pieces = pl.pallas_call(
        sum_kernel, out_shape=shape((N_ORB, rows, LANES), bf16),
        in_specs=[WHOLE_V, WHOLE_V], out_specs=WHOLE_V,
        scratch_shapes=[pltpu.VMEM((N_DEV * 16 + 16, LANES), f32), pltpu.VMEM((N_DEV * 8 + 8, LANES), f32)],
        compiler_params=PARAMS, name="sum",
    )(index, terms)
    pieces = lax.all_to_all(pieces, "orb", split_axis=0, concat_axis=0, tiled=True)
    return pl.pallas_call(
        join_kernel, out_shape=shape((ORB_DEV, 8, BOX * BOX), bf16),
        in_specs=[WHOLE_V], out_specs=WHOLE_V,
        compiler_params=PARAMS, name="join",
    )(pieces)


def solution(mesh):
    in_specs = (P("orb", "slab", None), P("orb"), P(), P(), P("orb", None), P())
    out_specs = P("orb", "slab", None)
    return jax.shard_map(body, mesh=mesh, in_specs=in_specs, out_specs=out_specs, check_vma=False)
```

```python
import math

import jax
import jax.numpy as jnp
import numpy as np
from jax import lax
from jax.experimental import pallas as pl
from jax.experimental.pallas import tpu as pltpu
from jax.sharding import PartitionSpec as P

BOX = 64
ORB_DEV = 8
PAIR_DEV = 16
N_ORB = 32
N_DEV = 256
TILES = 32
LANES = 128
SCREENING = 0.02
GROUPS = 4
PARAMS = pltpu.CompilerParams(vmem_limit_bytes=48 * 1024 * 1024)
WHOLE_V = pl.BlockSpec(memory_space=pltpu.VMEM)
WHOLE_H = pl.BlockSpec(memory_space=pltpu.HBM)
WHOLE_S = pl.BlockSpec(memory_space=pltpu.SMEM)


def hartley_table():
    line = np.arange(BOX)
    angle = (line[:, None] * line[None, :] % BOX) * (2.0 * math.pi / BOX)
    return np.cos(angle) + np.sin(angle)


def halves(table):
    high = table.astype(np.float32).astype(jnp.bfloat16)
    low = (table - high.astype(np.float64)).astype(np.float32).astype(jnp.bfloat16)
    return high, low


def tables():
    high, low = halves(hartley_table())
    zero = np.zeros((BOX, BOX), high.dtype)

    def twice(table):
        return np.block([[table, zero], [zero, table]])

    right = np.block([[twice(high), twice(low)], [twice(high), np.zeros((128, 128), high.dtype)]])
    left = np.block([[high, high], [low, np.zeros((BOX, BOX), high.dtype)]])
    lam = 2.0 - 2.0 * np.cos(np.arange(BOX) * (2.0 * math.pi / BOX))
    lam_a = np.repeat(lam.reshape(2, TILES).T, BOX, axis=1)
    under = lam_a[:, None, :] + lam[None, :, None] + np.tile(lam, 2)[None, None, :] + SCREENING
    return right, left, (1.0 / BOX**3 / under).astype(np.float32)


def split(field):
    high = field.astype(jnp.bfloat16)
    low = (field - high.astype(jnp.float32)).astype(jnp.bfloat16)
    return high, low


def fast_hartley(parts):
    n = len(parts)
    if n == 1:
        return parts
    if n == 2:
        return [parts[0] + parts[1], parts[0] - parts[1]]
    even, odd = fast_hartley(parts[0::2]), fast_hartley(parts[1::2])
    m = n // 2
    out = [None] * n
    for k in range(m):
        if k == 0 or 4 * k == n:
            turned = odd[k]
        elif 8 * k == n:
            turned = (odd[k] + odd[m - k]) * math.sqrt(0.5)
        elif 8 * k == 3 * n:
            turned = (odd[m - k] - odd[k]) * math.sqrt(0.5)
        else:
            angle = 2.0 * math.pi * k / n
            turned = odd[k] * math.cos(angle) + odd[m - k] * math.sin(angle)
        out[k] = even[k] + turned
        out[k + m] = even[k] - turned
    return out


def turns(first):
    angles = [2.0 * math.pi * k / BOX for k in range(TILES // 2 + 1)]
    return [(jnp.where(first, 1.0, math.cos(b)), jnp.where(first, 0.0, math.sin(b))) for b in angles], first


def twist(parts, known):
    turn, first = known
    out = list(parts)
    for k in range(1, TILES // 2):
        one, two = parts[k], parts[TILES - k]
        out[k] = one * turn[k][0] + two * turn[k][1]
        out[TILES - k] = jnp.where(first, two, one * turn[k][1] - two * turn[k][0])
    return out


def spread_kernel(first, shift, orbitals, pieces, taken, tall, small, about, packed, arrived, sent):
    few = [
        pltpu.make_async_copy(first, small.at[0:1], arrived.at[GROUPS]),
        pltpu.make_async_copy(shift, small.at[8:10], arrived.at[GROUPS + 1]),
    ]
    width = BOX * BOX // GROUPS
    many = [
        pltpu.make_async_copy(orbitals.at[:, :, pl.ds(k * width, width)], taken.at[k], arrived.at[k])
        for k in range(GROUPS)
    ]
    for copy in few + many:
        copy.start()
    about[...] = jnp.zeros_like(about)
    for copy in few:
        copy.wait()
    about[0:1, :PAIR_DEV] = small[0:1, :].astype(jnp.float32)
    about[1:3, :PAIR_DEV] = small[8:10, :].astype(jnp.float32)
    placed = pltpu.roll(about[...], lax.axis_index("orb") % 8 * PAIR_DEV, 1).astype(jnp.bfloat16)
    inside = TILES // GROUPS
    out = []
    for k in range(GROUPS):
        many[k].wait()
        for orbital in range(ORB_DEV):
            box = taken[k, orbital].astype(jnp.float32)
            for tile in range(inside):
                row = (k * inside + tile) * ORB_DEV * 8 + 8 * orbital
                tall[row : row + 8, :] = box[:, tile * LANES : (tile + 1) * LANES]
        for tile in range(k * inside, (k + 1) * inside):
            for z in range(8):
                row = tile * ORB_DEV * 8 + z
                packed[tile, z] = tall[pl.ds(row, ORB_DEV, stride=8), :].astype(jnp.bfloat16)
            packed[tile, 8] = placed
        at = pl.ds(k * inside, inside)
        out.append(pltpu.make_async_copy(packed.at[at], pieces.at[at], sent.at[k]))
        out[k].start()
    for copy in out:
        copy.wait()


def dot_rows(one, two):
    return lax.dot_general(one, two, (((1,), (1,)), ((), ())), preferred_element_type=jnp.float32)


def chosen(column):
    lane = lax.broadcasted_iota(jnp.int32, (N_DEV, LANES), 1).astype(jnp.float32)
    hits = [jnp.where(column == lane + half * LANES, 1.0, 0.0) for half in range(2)]
    return jnp.concatenate(hits, axis=1).astype(jnp.bfloat16)


def place_kernel(count, owner, local, place, second, choose):
    shape = (4, LANES)
    slot = lax.broadcasted_iota(jnp.int32, shape, 0) * LANES + lax.broadcasted_iota(jnp.int32, shape, 1)
    orb, rank = slot // PAIR_DEV, slot % PAIR_DEV
    before, live = jnp.zeros(shape, jnp.int32), jnp.zeros(shape, jnp.int32)
    for e in range(N_ORB):
        before = before + jnp.where(orb > e, count[e], 0)
        live = jnp.where(orb == e, count[e], live)
    rank = jnp.where(rank < live, before + rank, -1).astype(jnp.float32)
    pair = lax.broadcasted_iota(jnp.int32, (N_DEV, LANES), 0).astype(jnp.float32)
    second[...] = (owner[...] * ORB_DEV + local[...]).astype(jnp.float32)
    for k in range(4):
        at = slice(k * LANES, (k + 1) * LANES)
        place[:, at] = jnp.where(pair == rank[k : k + 1], 1.0, 0.0).astype(jnp.bfloat16)
    rows = jnp.concatenate([second[k : k + 1, :] for k in range(4)], axis=1)
    rows = jnp.broadcast_to(rows, (LANES, 4 * LANES)).astype(jnp.bfloat16)
    choose[...] = chosen(dot_rows(place[...], rows))


def pick_kernel(place, second, choose, pieces, picked, index, mine, tall):
    blocks = []
    for k in range(4):
        block = jnp.sum(pieces[8 * k : 8 * k + 8, 8].astype(jnp.float32), axis=0)
        row = lax.broadcasted_iota(jnp.int32, (8, LANES), 0)
        lane = lax.broadcasted_iota(jnp.int32, (8, LANES), 1)
        orbital = (8 * (8 * k + lane // PAIR_DEV)).astype(jnp.float32)
        block = jnp.where(row == 0, block + orbital, block)
        blocks.append(jnp.where(row == 3, jnp.broadcast_to(second[k : k + 1, :], (8, LANES)), block))
    facts = jnp.concatenate(blocks, axis=1)
    first = jnp.broadcast_to(facts[0:1], (LANES, 4 * LANES)).astype(jnp.bfloat16)
    choose_first = chosen(dot_rows(place[...], first))
    known = dot_rows(facts.astype(jnp.bfloat16), place[...])
    index[0:1, :] = known[0:1].astype(jnp.int32)
    index[1:2, :] = known[3:4].astype(jnp.int32)
    lane = lax.broadcasted_iota(jnp.int32, (8, N_DEV), 1)
    me = lax.axis_index("orb") * 8 + lax.axis_index("slab")
    here = jnp.sum(jnp.where(lane == me, known, 0.0), axis=1, keepdims=True)
    lane = lax.broadcasted_iota(jnp.int32, (1, LANES), 1)
    mine[...] = jnp.where(lane == 0, here[1:2], here[2:3])
    for z in range(0, 8, 2):
        field = [
            pieces[:, z + k].astype(jnp.float32).reshape(N_DEV, LANES).astype(jnp.bfloat16) for k in range(2)
        ]
        field = jnp.concatenate(field, axis=1)
        for side, picker in enumerate((choose_first, choose[...])):
            out = jnp.dot(picker, field, preferred_element_type=jnp.float32)
            tall[pl.ds(8 * side + z, N_DEV, stride=16), :] = out[:, :LANES]
            tall[pl.ds(8 * side + z + 1, N_DEV, stride=16), :] = out[:, LANES:]
    for k in range(0, N_DEV, 8):
        picked[k : k + 8] = tall[16 * k : 16 * k + 128, :].reshape(8, 16, LANES).astype(jnp.bfloat16)


def shifted(tiles, start, count, flat, shift_x, shift_y):
    lane = lax.broadcasted_iota(jnp.int32, (8, LANES), 1)
    whole, rest = flat // LANES, flat % LANES
    later = (lane >= rest)[None]
    y = lane % BOX - shift_y
    keep_y = (y >= 0) & (y < BOX)
    turned = [
        pltpu.roll(tiles((start + k - whole - 1 + 2 * TILES) % TILES), rest, 2) for k in range(count + 1)
    ]
    out = []
    for k in range(count):
        x = 2 * (start + k) + lane // BOX - shift_x
        keep = jnp.where(keep_y & (x >= 0) & (x < BOX), 1.0, 0.0)
        out.append(jnp.where(later, turned[k + 1], turned[k]) * keep[None])
    return out


def solve_kernel(shift, right, left, screen, boxes, terms, moved, field, other):
    lane = lax.broadcasted_iota(jnp.int32, (1, LANES), 1)
    shift_x, shift_y = (jnp.sum(jnp.where(lane == k, shift[...], 0.0)).astype(jnp.int32) for k in range(2))
    full = BOX * BOX
    ahead = (shift_x * BOX + shift_y + full) % full
    back = (full - ahead) % full
    early = lax.broadcasted_iota(jnp.int32, (8, LANES), 1) < BOX
    sign = jnp.where(early, 1.0, -1.0)
    known = turns(early)

    def first_tile(tile):
        return boxes[pl.ds(tile * 8, 8), :8, :].astype(jnp.float32)

    def second_tile(tile):
        return boxes[pl.ds(tile * 8, 8), 8:, :].astype(jnp.float32)

    def along_y(block):
        high, low = split(block)
        product = jnp.dot(
            jnp.concatenate([high, low], axis=1), right[...], preferred_element_type=jnp.float32
        )
        return product[:, :LANES] + product[:, LANES:]

    for start in range(0, TILES, 4):
        products = []
        for k, box in enumerate(shifted(second_tile, start, 4, ahead, shift_x, shift_y)):
            moved[start + k] = box
            products.append(first_tile(start + k) * box)
        block = along_y(jnp.stack(products).reshape(4 * BOX, LANES)).reshape(4, BOX, LANES)
        for k in range(4):
            field[start + k] = block[k]

    for row in range(0, BOX, 8):
        parts = twist(fast_hartley([field[k, row : row + 8, :] for k in range(TILES)]), known)
        for k in range(TILES):
            field[k, row : row + 8, :] = sign * parts[k] + pltpu.roll(parts[k], BOX, 1)

    def along_z(block):
        high, low = split(block)
        product = jnp.dot(
            left[...], jnp.concatenate([high, low], axis=0), preferred_element_type=jnp.float32
        )
        return product[:BOX] + product[BOX:]

    for tile in range(0, TILES, 2):
        block = along_z(jnp.concatenate([field[tile], field[tile + 1]], axis=1))
        block = block * jnp.concatenate([screen[tile], screen[tile + 1]], axis=1)
        block = along_z(block)
        field[tile] = block[:, :LANES]
        field[tile + 1] = block[:, LANES:]

    for row in range(0, BOX, 8):
        parts = [field[k, row : row + 8, :] for k in range(TILES)]
        parts = [sign * part + pltpu.roll(part, BOX, 1) for part in parts]
        parts = fast_hartley(twist(parts, known))
        for k in range(TILES):
            field[k, row : row + 8, :] = parts[k]

    for start in range(0, TILES, 4):
        block = field[start : start + 4].reshape(4 * BOX, LANES)
        potential = along_y(block).reshape(4, 8, 8, LANES)
        for k in range(4):
            other[start + k] = potential[k] * first_tile(start + k)
            moved[start + k] = potential[k] * moved[start + k]

    for start in range(0, TILES, 4):
        carried = shifted(lambda tile: other[tile], start, 4, back, -shift_x, -shift_y)
        for k in range(4):
            both = jnp.concatenate([moved[start + k], carried[k]], axis=1)
            terms[(start + k) * 8 : (start + k + 1) * 8] = both.astype(jnp.bfloat16)


def sum_kernel(index, terms, pieces, tall, summed):
    for k in range(0, N_DEV, 8):
        tall[16 * k : 16 * k + 128, :] = terms[k : k + 8].astype(jnp.float32).reshape(128, LANES)
    orbital = lax.broadcasted_iota(jnp.int32, (N_DEV, N_DEV), 0)
    hits = [jnp.where(orbital == index[side : side + 1, :], 1.0, 0.0) for side in range(2)]
    hits = jnp.concatenate(hits, axis=1).astype(jnp.bfloat16)
    for z in range(0, 8, 2):
        field = [
            jnp.concatenate(
                [tall[pl.ds(8 * side + z + k, N_DEV, stride=16), :] for side in range(2)], axis=0
            ).astype(jnp.bfloat16)
            for k in range(2)
        ]
        out = jnp.dot(hits, jnp.concatenate(field, axis=1), preferred_element_type=jnp.float32)
        summed[pl.ds(z, N_DEV, stride=8), :] = out[:, :LANES]
        summed[pl.ds(z + 1, N_DEV, stride=8), :] = out[:, LANES:]
    for e in range(N_ORB):
        pieces[e] = summed[e * ORB_DEV * 8 : (e + 1) * ORB_DEV * 8, :].astype(jnp.bfloat16)


def join_kernel(pieces, result):
    for pair in range(ORB_DEV // 2):
        tiles = [pieces[tile, 16 * pair : 16 * pair + 16, :].astype(jnp.float32) for tile in range(TILES)]
        for side in range(2):
            rows = [tile[8 * side : 8 * side + 8] for tile in tiles]
            result[2 * pair + side] = jnp.concatenate(rows, axis=1).astype(jnp.bfloat16)


def body(orbitals, pair_first, second_owner, second_local, pair_shift, pair_count):
    f32, bf16, i32 = jnp.float32, jnp.bfloat16, jnp.int32
    shape = jax.ShapeDtypeStruct
    rows = ORB_DEV * 8
    pair_shape = shape((N_DEV, 16, LANES), bf16)
    pieces = pl.pallas_call(
        spread_kernel, out_shape=shape((N_ORB, 9, ORB_DEV, LANES), bf16),
        in_specs=[WHOLE_H] * 3, out_specs=WHOLE_H,
        scratch_shapes=[
            pltpu.VMEM((GROUPS, ORB_DEV, 8, BOX * BOX // GROUPS), bf16),
            pltpu.VMEM((TILES * rows + 64, LANES), f32),
            pltpu.VMEM((16, PAIR_DEV), i32),
            pltpu.VMEM((8, LANES), f32),
            pltpu.VMEM((N_ORB, 9, ORB_DEV, LANES), bf16),
            pltpu.SemaphoreType.DMA((GROUPS + 2,)),
            pltpu.SemaphoreType.DMA((GROUPS,)),
        ],
        compiler_params=pltpu.CompilerParams(vmem_limit_bytes=60 * 1024 * 1024), name="spread",
    )(pair_first.reshape(1, PAIR_DEV), pair_shift.T, orbitals)
    pieces = lax.all_to_all(pieces, "orb", split_axis=0, concat_axis=0, tiled=True)
    place, second, choose = pl.pallas_call(
        place_kernel,
        out_shape=(shape((N_DEV, 4 * LANES), bf16), shape((4, LANES), f32), shape((N_DEV, N_DEV), bf16)),
        in_specs=[WHOLE_S, WHOLE_V, WHOLE_V], out_specs=(WHOLE_V,) * 3,
        compiler_params=PARAMS, name="place",
    )(pair_count, second_owner.reshape(4, LANES), second_local.reshape(4, LANES))
    picked, index, mine = pl.pallas_call(
        pick_kernel,
        out_shape=(pair_shape, shape((2, N_DEV), i32), shape((1, LANES), f32)),
        in_specs=[WHOLE_V] * 4,
        out_specs=(WHOLE_V,) * 3,
        scratch_shapes=[pltpu.VMEM((N_DEV * 16 + 16, LANES), f32)],
        compiler_params=PARAMS, name="pick",
    )(place, second, choose, pieces)
    boxes = lax.all_to_all(picked, ("orb", "slab"), split_axis=0, concat_axis=0, tiled=True)
    right, left, screen = (jnp.asarray(table) for table in tables())
    terms = pl.pallas_call(
        solve_kernel, out_shape=pair_shape,
        in_specs=[WHOLE_V] * 5,
        out_specs=WHOLE_V,
        scratch_shapes=[
            pltpu.VMEM((TILES, 8, 8, LANES), f32),
            pltpu.VMEM((TILES, BOX, LANES), f32),
            pltpu.VMEM((TILES, 8, 8, LANES), f32),
        ],
        compiler_params=PARAMS, name="solve",
    )(mine, right, left, screen, boxes)
    terms = lax.all_to_all(terms, ("orb", "slab"), split_axis=0, concat_axis=0, tiled=True)
    pieces = pl.pallas_call(
        sum_kernel, out_shape=shape((N_ORB, rows, LANES), bf16),
        in_specs=[WHOLE_V, WHOLE_V], out_specs=WHOLE_V,
        scratch_shapes=[pltpu.VMEM((N_DEV * 16 + 16, LANES), f32), pltpu.VMEM((N_DEV * 8 + 8, LANES), f32)],
        compiler_params=PARAMS, name="sum",
    )(index, terms)
    pieces = lax.all_to_all(pieces, "orb", split_axis=0, concat_axis=0, tiled=True)
    return pl.pallas_call(
        join_kernel, out_shape=shape((ORB_DEV, 8, BOX * BOX), bf16),
        in_specs=[WHOLE_V], out_specs=WHOLE_V,
        compiler_params=PARAMS, name="join",
    )(pieces)


def solution(mesh):
    in_specs = (P("orb", "slab", None), P("orb"), P(), P(), P("orb", None), P())
    out_specs = P("orb", "slab", None)
    return jax.shard_map(body, mesh=mesh, in_specs=in_specs, out_specs=out_specs, check_vma=False)
```

```python
import math

import jax
import jax.numpy as jnp
import numpy as np
from jax import lax
from jax.experimental import pallas as pl
from jax.experimental.pallas import tpu as pltpu
from jax.sharding import PartitionSpec as P

BOX = 64
ORB_DEV = 8
PAIR_DEV = 16
N_ORB = 32
N_DEV = 256
TILES = 32
LANES = 128
SCREENING = 0.02
GROUPS = 4
PARAMS = pltpu.CompilerParams(vmem_limit_bytes=48 * 1024 * 1024)
WHOLE_V = pl.BlockSpec(memory_space=pltpu.VMEM)
WHOLE_H = pl.BlockSpec(memory_space=pltpu.HBM)
WHOLE_S = pl.BlockSpec(memory_space=pltpu.SMEM)


def hartley_table():
    line = np.arange(BOX)
    angle = (line[:, None] * line[None, :] % BOX) * (2.0 * math.pi / BOX)
    return np.cos(angle) + np.sin(angle)


def halves(table):
    high = table.astype(np.float32).astype(jnp.bfloat16)
    low = (table - high.astype(np.float64)).astype(np.float32).astype(jnp.bfloat16)
    return high, low


def tables():
    high, low = halves(hartley_table())
    zero = np.zeros((BOX, BOX), high.dtype)

    def twice(table):
        return np.block([[table, zero], [zero, table]])

    right = np.block([[twice(high), twice(low)], [twice(high), np.zeros((128, 128), high.dtype)]])
    left = np.block([[high, high], [low, np.zeros((BOX, BOX), high.dtype)]])
    lam = 2.0 - 2.0 * np.cos(np.arange(BOX) * (2.0 * math.pi / BOX))
    lam_a = np.repeat(lam.reshape(2, TILES).T, BOX, axis=1)
    under = lam_a[:, None, :] + lam[None, :, None] + np.tile(lam, 2)[None, None, :] + SCREENING
    return right, left, (1.0 / BOX**3 / under).astype(np.float32)


def split(field):
    high = field.astype(jnp.bfloat16)
    low = (field - high.astype(jnp.float32)).astype(jnp.bfloat16)
    return high, low


def fast_hartley(parts):
    n = len(parts)
    if n == 1:
        return parts
    if n == 2:
        return [parts[0] + parts[1], parts[0] - parts[1]]
    even, odd = fast_hartley(parts[0::2]), fast_hartley(parts[1::2])
    m = n // 2
    out = [None] * n
    for k in range(m):
        if k == 0 or 4 * k == n:
            turned = odd[k]
        elif 8 * k == n:
            turned = (odd[k] + odd[m - k]) * math.sqrt(0.5)
        elif 8 * k == 3 * n:
            turned = (odd[m - k] - odd[k]) * math.sqrt(0.5)
        else:
            angle = 2.0 * math.pi * k / n
            turned = odd[k] * math.cos(angle) + odd[m - k] * math.sin(angle)
        out[k] = even[k] + turned
        out[k + m] = even[k] - turned
    return out


def turns(first):
    angles = [2.0 * math.pi * k / BOX for k in range(TILES // 2 + 1)]
    return [(jnp.where(first, 1.0, math.cos(b)), jnp.where(first, 0.0, math.sin(b))) for b in angles], first


def twist(parts, known):
    turn, first = known
    out = list(parts)
    for k in range(1, TILES // 2):
        one, two = parts[k], parts[TILES - k]
        out[k] = one * turn[k][0] + two * turn[k][1]
        out[TILES - k] = jnp.where(first, two, one * turn[k][1] - two * turn[k][0])
    return out


def spread_kernel(first, shift, orbitals, pieces, taken, tall, small, about, packed, arrived, sent):
    few = [
        pltpu.make_async_copy(first, small.at[0:1], arrived.at[GROUPS]),
        pltpu.make_async_copy(shift, small.at[8:10], arrived.at[GROUPS + 1]),
    ]
    width = BOX * BOX // GROUPS
    many = [
        pltpu.make_async_copy(orbitals.at[:, :, pl.ds(k * width, width)], taken.at[k], arrived.at[k])
        for k in range(GROUPS)
    ]
    for copy in few + many:
        copy.start()
    about[...] = jnp.zeros_like(about)
    for copy in few:
        copy.wait()
    about[0:1, :PAIR_DEV] = small[0:1, :].astype(jnp.float32)
    about[1:3, :PAIR_DEV] = small[8:10, :].astype(jnp.float32)
    placed = pltpu.roll(about[...], lax.axis_index("orb") % 8 * PAIR_DEV, 1).astype(jnp.bfloat16)
    inside = TILES // GROUPS
    out = []
    for k in range(GROUPS):
        many[k].wait()
        for orbital in range(ORB_DEV):
            box = taken[k, orbital].astype(jnp.float32)
            for tile in range(inside):
                row = (k * inside + tile) * ORB_DEV * 8 + 8 * orbital
                tall[row : row + 8, :] = box[:, tile * LANES : (tile + 1) * LANES]
        for tile in range(k * inside, (k + 1) * inside):
            for z in range(8):
                row = tile * ORB_DEV * 8 + z
                packed[tile, z] = tall[pl.ds(row, ORB_DEV, stride=8), :].astype(jnp.bfloat16)
            packed[tile, 8] = placed
        at = pl.ds(k * inside, inside)
        out.append(pltpu.make_async_copy(packed.at[at], pieces.at[at], sent.at[k]))
        out[k].start()
    for copy in out:
        copy.wait()


def dot_rows(one, two):
    return lax.dot_general(one, two, (((1,), (1,)), ((), ())), preferred_element_type=jnp.float32)


def chosen(column):
    lane = lax.broadcasted_iota(jnp.int32, (N_DEV, LANES), 1).astype(jnp.float32)
    hits = [jnp.where(column == lane + half * LANES, 1.0, 0.0) for half in range(2)]
    return jnp.concatenate(hits, axis=1).astype(jnp.bfloat16)


def place_kernel(count, owner, local, place, second, choose):
    shape = (4, LANES)
    slot = lax.broadcasted_iota(jnp.int32, shape, 0) * LANES + lax.broadcasted_iota(jnp.int32, shape, 1)
    orb, rank = slot // PAIR_DEV, slot % PAIR_DEV
    before, live = jnp.zeros(shape, jnp.int32), jnp.zeros(shape, jnp.int32)
    for e in range(N_ORB):
        before = before + jnp.where(orb > e, count[e], 0)
        live = jnp.where(orb == e, count[e], live)
    rank = jnp.where(rank < live, before + rank, -1).astype(jnp.float32)
    pair = lax.broadcasted_iota(jnp.int32, (N_DEV, LANES), 0).astype(jnp.float32)
    second[...] = (owner[...] * ORB_DEV + local[...]).astype(jnp.float32)
    for k in range(4):
        at = slice(k * LANES, (k + 1) * LANES)
        place[:, at] = jnp.where(pair == rank[k : k + 1], 1.0, 0.0).astype(jnp.bfloat16)
    rows = jnp.concatenate([second[k : k + 1, :] for k in range(4)], axis=1)
    rows = jnp.broadcast_to(rows, (LANES, 4 * LANES)).astype(jnp.bfloat16)
    choose[...] = chosen(dot_rows(place[...], rows))


def pick_kernel(place, second, choose, pieces, picked, index, mine, tall):
    blocks = []
    for k in range(4):
        block = jnp.sum(pieces[8 * k : 8 * k + 8, 8].astype(jnp.float32), axis=0)
        row = lax.broadcasted_iota(jnp.int32, (8, LANES), 0)
        lane = lax.broadcasted_iota(jnp.int32, (8, LANES), 1)
        orbital = (8 * (8 * k + lane // PAIR_DEV)).astype(jnp.float32)
        block = jnp.where(row == 0, block + orbital, block)
        blocks.append(jnp.where(row == 3, jnp.broadcast_to(second[k : k + 1, :], (8, LANES)), block))
    facts = jnp.concatenate(blocks, axis=1)
    first = jnp.broadcast_to(facts[0:1], (LANES, 4 * LANES)).astype(jnp.bfloat16)
    choose_first = chosen(dot_rows(place[...], first))
    known = dot_rows(facts.astype(jnp.bfloat16), place[...])
    index[0:1, :] = known[0:1].astype(jnp.int32)
    index[1:2, :] = known[3:4].astype(jnp.int32)
    lane = lax.broadcasted_iota(jnp.int32, (8, N_DEV), 1)
    me = lax.axis_index("orb") * 8 + lax.axis_index("slab")
    here = jnp.sum(jnp.where(lane == me, known, 0.0), axis=1, keepdims=True)
    lane = lax.broadcasted_iota(jnp.int32, (1, LANES), 1)
    mine[...] = jnp.where(lane == 0, here[1:2], here[2:3])
    for z in range(0, 8, 2):
        field = [
            pieces[:, z + k].astype(jnp.float32).reshape(N_DEV, LANES).astype(jnp.bfloat16) for k in range(2)
        ]
        field = jnp.concatenate(field, axis=1)
        for side, picker in enumerate((choose_first, choose[...])):
            out = jnp.dot(picker, field, preferred_element_type=jnp.float32)
            tall[pl.ds(8 * side + z, N_DEV, stride=16), :] = out[:, :LANES]
            tall[pl.ds(8 * side + z + 1, N_DEV, stride=16), :] = out[:, LANES:]
    for k in range(0, N_DEV, 8):
        picked[k : k + 8] = tall[16 * k : 16 * k + 128, :].reshape(8, 16, LANES).astype(jnp.bfloat16)


def shifted(tiles, start, count, flat, shift_x, shift_y):
    lane = lax.broadcasted_iota(jnp.int32, (8, LANES), 1)
    whole, rest = flat // LANES, flat % LANES
    later = (lane >= rest)[None]
    y = lane % BOX - shift_y
    keep_y = (y >= 0) & (y < BOX)
    turned = [
        pltpu.roll(tiles((start + k - whole - 1 + 2 * TILES) % TILES), rest, 2) for k in range(count + 1)
    ]
    out = []
    for k in range(count):
        x = 2 * (start + k) + lane // BOX - shift_x
        keep = jnp.where(keep_y & (x >= 0) & (x < BOX), 1.0, 0.0)
        out.append(jnp.where(later, turned[k + 1], turned[k]) * keep[None])
    return out


def solve_kernel(shift, right, left, screen, boxes, terms, moved, field, other):
    lane = lax.broadcasted_iota(jnp.int32, (1, LANES), 1)
    shift_x, shift_y = (jnp.sum(jnp.where(lane == k, shift[...], 0.0)).astype(jnp.int32) for k in range(2))
    full = BOX * BOX
    ahead = (shift_x * BOX + shift_y + full) % full
    back = (full - ahead) % full
    early = lax.broadcasted_iota(jnp.int32, (8, LANES), 1) < BOX
    sign = jnp.where(early, 1.0, -1.0)
    known = turns(early)

    def first_tile(tile):
        return boxes[pl.ds(tile * 8, 8), :8, :].astype(jnp.float32)

    def second_tile(tile):
        return boxes[pl.ds(tile * 8, 8), 8:, :].astype(jnp.float32)

    def along_y(block):
        high, low = split(block)
        product = jnp.dot(
            jnp.concatenate([high, low], axis=1), right[...], preferred_element_type=jnp.float32
        )
        return product[:, :LANES] + product[:, LANES:]

    for start in range(0, TILES, 4):
        products = []
        for k, box in enumerate(shifted(second_tile, start, 4, ahead, shift_x, shift_y)):
            moved[start + k] = box
            products.append(first_tile(start + k) * box)
        block = along_y(jnp.stack(products).reshape(4 * BOX, LANES)).reshape(4, BOX, LANES)
        for k in range(4):
            field[start + k] = block[k]

    for row in range(0, BOX, 8):
        parts = twist(fast_hartley([field[k, row : row + 8, :] for k in range(TILES)]), known)
        for k in range(TILES):
            field[k, row : row + 8, :] = sign * parts[k] + pltpu.roll(parts[k], BOX, 1)

    def along_z(block):
        high, low = split(block)
        product = jnp.dot(
            left[...], jnp.concatenate([high, low], axis=0), preferred_element_type=jnp.float32
        )
        return product[:BOX] + product[BOX:]

    for tile in range(0, TILES, 2):
        block = along_z(jnp.concatenate([field[tile], field[tile + 1]], axis=1))
        block = block * jnp.concatenate([screen[tile], screen[tile + 1]], axis=1)
        block = along_z(block)
        field[tile] = block[:, :LANES]
        field[tile + 1] = block[:, LANES:]

    for row in range(0, BOX, 8):
        parts = [field[k, row : row + 8, :] for k in range(TILES)]
        parts = [sign * part + pltpu.roll(part, BOX, 1) for part in parts]
        parts = fast_hartley(twist(parts, known))
        for k in range(TILES):
            field[k, row : row + 8, :] = parts[k]

    for start in range(0, TILES, 4):
        block = field[start : start + 4].reshape(4 * BOX, LANES)
        potential = along_y(block).reshape(4, 8, 8, LANES)
        for k in range(4):
            other[start + k] = potential[k] * first_tile(start + k)
            own = potential[k] * moved[start + k]
            terms[(start + k) * 8 : (start + k + 1) * 8, :8, :] = own.astype(jnp.bfloat16)

    for start in range(0, TILES, 4):
        carried = shifted(lambda tile: other[tile], start, 4, back, -shift_x, -shift_y)
        for k in range(4):
            terms[(start + k) * 8 : (start + k + 1) * 8, 8:, :] = carried[k].astype(jnp.bfloat16)


def sum_kernel(index, terms, pieces, tall, summed):
    for k in range(0, N_DEV, 8):
        tall[16 * k : 16 * k + 128, :] = terms[k : k + 8].astype(jnp.float32).reshape(128, LANES)
    orbital = lax.broadcasted_iota(jnp.int32, (N_DEV, N_DEV), 0)
    hits = [jnp.where(orbital == index[side : side + 1, :], 1.0, 0.0) for side in range(2)]
    hits = jnp.concatenate(hits, axis=1).astype(jnp.bfloat16)
    for z in range(0, 8, 2):
        field = [
            jnp.concatenate(
                [tall[pl.ds(8 * side + z + k, N_DEV, stride=16), :] for side in range(2)], axis=0
            ).astype(jnp.bfloat16)
            for k in range(2)
        ]
        out = jnp.dot(hits, jnp.concatenate(field, axis=1), preferred_element_type=jnp.float32)
        summed[pl.ds(z, N_DEV, stride=8), :] = out[:, :LANES]
        summed[pl.ds(z + 1, N_DEV, stride=8), :] = out[:, LANES:]
    for e in range(N_ORB):
        pieces[e] = summed[e * ORB_DEV * 8 : (e + 1) * ORB_DEV * 8, :].astype(jnp.bfloat16)


def join_kernel(pieces, result):
    for pair in range(ORB_DEV // 2):
        tiles = [pieces[tile, 16 * pair : 16 * pair + 16, :].astype(jnp.float32) for tile in range(TILES)]
        for side in range(2):
            rows = [tile[8 * side : 8 * side + 8] for tile in tiles]
            result[2 * pair + side] = jnp.concatenate(rows, axis=1).astype(jnp.bfloat16)


def body(orbitals, pair_first, second_owner, second_local, pair_shift, pair_count):
    f32, bf16, i32 = jnp.float32, jnp.bfloat16, jnp.int32
    shape = jax.ShapeDtypeStruct
    rows = ORB_DEV * 8
    pair_shape = shape((N_DEV, 16, LANES), bf16)
    pieces = pl.pallas_call(
        spread_kernel, out_shape=shape((N_ORB, 9, ORB_DEV, LANES), bf16),
        in_specs=[WHOLE_H] * 3, out_specs=WHOLE_H,
        scratch_shapes=[
            pltpu.VMEM((GROUPS, ORB_DEV, 8, BOX * BOX // GROUPS), bf16),
            pltpu.VMEM((TILES * rows + 64, LANES), f32),
            pltpu.VMEM((16, PAIR_DEV), i32),
            pltpu.VMEM((8, LANES), f32),
            pltpu.VMEM((N_ORB, 9, ORB_DEV, LANES), bf16),
            pltpu.SemaphoreType.DMA((GROUPS + 2,)),
            pltpu.SemaphoreType.DMA((GROUPS,)),
        ],
        compiler_params=pltpu.CompilerParams(vmem_limit_bytes=60 * 1024 * 1024), name="spread",
    )(pair_first.reshape(1, PAIR_DEV), pair_shift.T, orbitals)
    pieces = lax.all_to_all(pieces, "orb", split_axis=0, concat_axis=0, tiled=True)
    place, second, choose = pl.pallas_call(
        place_kernel,
        out_shape=(shape((N_DEV, 4 * LANES), bf16), shape((4, LANES), f32), shape((N_DEV, N_DEV), bf16)),
        in_specs=[WHOLE_S, WHOLE_V, WHOLE_V], out_specs=(WHOLE_V,) * 3,
        compiler_params=PARAMS, name="place",
    )(pair_count, second_owner.reshape(4, LANES), second_local.reshape(4, LANES))
    picked, index, mine = pl.pallas_call(
        pick_kernel,
        out_shape=(pair_shape, shape((2, N_DEV), i32), shape((1, LANES), f32)),
        in_specs=[WHOLE_V] * 4,
        out_specs=(WHOLE_V,) * 3,
        scratch_shapes=[pltpu.VMEM((N_DEV * 16 + 16, LANES), f32)],
        compiler_params=PARAMS, name="pick",
    )(place, second, choose, pieces)
    boxes = lax.all_to_all(picked, ("orb", "slab"), split_axis=0, concat_axis=0, tiled=True)
    right, left, screen = (jnp.asarray(table) for table in tables())
    terms = pl.pallas_call(
        solve_kernel, out_shape=pair_shape,
        in_specs=[WHOLE_V] * 5,
        out_specs=WHOLE_V,
        scratch_shapes=[
            pltpu.VMEM((TILES, 8, 8, LANES), f32),
            pltpu.VMEM((TILES, BOX, LANES), f32),
            pltpu.VMEM((TILES, 8, 8, LANES), f32),
        ],
        compiler_params=PARAMS, name="solve",
    )(mine, right, left, screen, boxes)
    terms = lax.all_to_all(terms, ("orb", "slab"), split_axis=0, concat_axis=0, tiled=True)
    pieces = pl.pallas_call(
        sum_kernel, out_shape=shape((N_ORB, rows, LANES), bf16),
        in_specs=[WHOLE_V, WHOLE_V], out_specs=WHOLE_V,
        scratch_shapes=[pltpu.VMEM((N_DEV * 16 + 16, LANES), f32), pltpu.VMEM((N_DEV * 8 + 8, LANES), f32)],
        compiler_params=PARAMS, name="sum",
    )(index, terms)
    pieces = lax.all_to_all(pieces, "orb", split_axis=0, concat_axis=0, tiled=True)
    return pl.pallas_call(
        join_kernel, out_shape=shape((ORB_DEV, 8, BOX * BOX), bf16),
        in_specs=[WHOLE_V], out_specs=WHOLE_V,
        compiler_params=PARAMS, name="join",
    )(pieces)


def solution(mesh):
    in_specs = (P("orb", "slab", None), P("orb"), P(), P(), P("orb", None), P())
    out_specs = P("orb", "slab", None)
    return jax.shard_map(body, mesh=mesh, in_specs=in_specs, out_specs=out_specs, check_vma=False)
```
